32 devices in a mesh: dp: 4 (over x, core), row: 4 (over z), col: 2 (over y).
Axes of the slice: x: 2, y: 2, z: 4, core: 2. Of those that a mesh axis runs over, the one named last changes fastest.
Arguments:
- tokens: float32 [6304, 1024], P('dp', ('row', 'col')), may hold values from -6 to 6
- cotangent: float32 [6304, 1024], P('dp', ('row', 'col')), may hold values from -6 to 6
- w_qkv: bfloat16 [1024, 3, 16, 64], P('row', None, 'col', 'dp'), may hold values from -0.4375 to 0.4375
- b_qkv: bfloat16 [2, 16, 64], P(None, 'col', 'dp'), may hold values from -3 to 3
- w_out: bfloat16 [16, 64, 1024], P('col', 'dp', 'row'), may hold values from -1 to 1
- w_up: bfloat16 [1024, 64, 64], P('row', 'col', 'dp'), may hold values from -0.34375 to 0.34375
- b_up: bfloat16 [64, 64], P('col', 'dp'), may hold values from -3 to 3
- w_down: bfloat16 [64, 64, 1024], P('col', 'dp', 'row'), may hold values from -0.09375 to 0.09375
- vectors: bfloat16 [6, 16, 64], P(None, ('row', 'col'), 'dp'), may hold values from -1.2 to 1.4, as said below
- state_qkv: float32 [2, 1024, 3, 16, 64], P(None, 'row', None, 'col', 'dp'), may hold values from -4.5 to 4.5, as said below
- state_qkv_bias: float32 [2, 2, 16, 64], P(None, None, 'col', 'dp'), may hold values from -4.5 to 4.5, as said below
- state_out: float32 [2, 16, 64, 1024], P(None, 'col', 'dp', 'row'), may hold values from -14.5 to 14.5, as said below
- state_up: float32 [2, 1024, 64, 64], P(None, 'row', 'col', 'dp'), may hold values from -3.9 to 3.9, as said below
- state_up_bias: float32 [2, 64, 64], P(None, 'col', 'dp'), may hold values from -3.9 to 3.9, as said below
- state_down: float32 [2, 64, 64, 1024], P(None, 'col', 'dp', 'row'), may hold values from -7.4 to 7.4, as said below
- state_vectors: float32 [2, 6, 16, 64], P(None, None, ('row', 'col'), 'dp'), may hold values from -14.5 to 14.5, as said below
Outputs:
- layer_out: float32 [6304, 1024], P('dp', ('row', 'col'))
- grad_tokens: float32 [6304, 1024], P('dp', ('row', 'col'))
- grad_w_qkv: float32 [1024, 3, 16, 64], P('row', None, 'col', 'dp')
- grad_b_qkv: float32 [2, 16, 64], P(None, 'col', 'dp')
- grad_w_out: float32 [16, 64, 1024], P('col', 'dp', 'row')
- grad_w_up: float32 [1024, 64, 64], P('row', 'col', 'dp')
- grad_b_up: float32 [64, 64], P('col', 'dp')
- grad_w_down: float32 [64, 64, 1024], P('col', 'dp', 'row')
- grad_vectors: float32 [6, 16, 64], P(None, ('row', 'col'), 'dp')
- change_w_qkv: float32 [1024, 3, 16, 64], P('row', None, 'col', 'dp')
- change_b_qkv: float32 [2, 16, 64], P(None, 'col', 'dp')
- change_w_out: float32 [16, 64, 1024], P('col', 'dp', 'row')
- change_w_up: float32 [1024, 64, 64], P('row', 'col', 'dp')
- change_b_up: float32 [64, 64], P('col', 'dp')
- change_w_down: float32 [64, 64, 1024], P('col', 'dp', 'row')
- change_vectors: float32 [6, 16, 64], P(None, ('row', 'col'), 'dp')
- new_state_qkv: float32 [2, 1024, 3, 16, 64], P(None, 'row', None, 'col', 'dp')
- new_state_qkv_bias: float32 [2, 2, 16, 64], P(None, None, 'col', 'dp')
- new_state_out: float32 [2, 16, 64, 1024], P(None, 'col', 'dp', 'row')
- new_state_up: float32 [2, 1024, 64, 64], P(None, 'row', 'col', 'dp')
- new_state_up_bias: float32 [2, 64, 64], P(None, 'col', 'dp')
- new_state_down: float32 [2, 64, 64, 1024], P(None, 'col', 'dp', 'row')
- new_state_vectors: float32 [2, 6, 16, 64], P(None, None, ('row', 'col'), 'dp')
The draws below stay inside these ranges and needn't reach their ends.
Inputs may be any that keep to these rules, and one draw needn't show every extreme that they name: `vectors`: rows 0 and 3 are gains between 0.6 and 1.4. `state_qkv`: slice 0 is the first moment; slice 1, the second moment, is positive. `state_qkv_bias`: slice 0 is the first moment; slice 1, the second moment, is positive. `state_out`: slice 0 is the first moment; slice 1, the second moment, is positive. `state_up`: slice 0 is the first moment; slice 1, the second moment, is positive. `state_up_bias`: slice 0 is the first moment; slice 1, the second moment, is positive. `state_down`: slice 0 is the first moment; slice 1, the second moment, is positive. `state_vectors`: slice 0 is the first moment; slice 1, the second moment, is positive.
All inputs are finite; a program needn't handle non-finite values.
Results may differ from the reference program's by a relative error of at most 0.023.
Values may be sent and summed in bfloat16 or wider, within the bound.
No kernel may reach another device: no remote copies, remote signals or barrier semaphores. Data moves between devices by JAX's collectives and lax.ppermute only.
A program may use at most 128 MiB of HBM per device.

```python
import math
import jax
import jax.numpy as jnp
from jax import lax

D = 1024
H = 16
HD = 64
FF = 4096
SEQ = 197
STEP = 10
TOKENS = 6304


grad_gain = 32.0


def draw_moments(key, shape, grad_base):
    grad_size = grad_base * grad_gain
    key_first, key_second = jax.random.split(jax.random.fold_in(key, 7))
    first_moment = jnp.clip(jax.random.normal(key_first, shape, jnp.float32) * 0.11, -0.44, 0.44) * grad_size
    second_moment = jnp.exp(jax.random.uniform(key_second, shape, jnp.float32, math.log(0.001), math.log(0.004))) * (grad_size * grad_size)
    return jnp.stack([first_moment, second_moment])


def draw_w_qkv(key, part):
    key_noise, key_offset = jax.random.split(jax.random.fold_in(key, 11))
    noise = jnp.clip(jax.random.normal(key_noise, (D, 3, H, HD), jnp.float32), -4.5, 4.5)
    offset = jnp.clip(jax.random.normal(key_offset, (1, 1, H, HD), jnp.float32), -3.0, 3.0) * 3.0
    value_part = (jnp.arange(3) == 2).astype(jnp.float32).reshape(1, 3, 1, 1)
    return ((noise + offset * value_part) / math.sqrt(D)).astype(jnp.bfloat16)


def draw_w_up(key, part):
    key_noise, key_offset = jax.random.split(jax.random.fold_in(key, 13))
    noise = jnp.clip(jax.random.normal(key_noise, (D, FF // HD, HD), jnp.float32), -4.5, 4.5)
    offset = jnp.clip(jax.random.normal(key_offset, (1, FF // HD, HD), jnp.float32), -3.0, 3.0) * 2.0
    return ((noise + offset) / math.sqrt(D)).astype(jnp.bfloat16)


def draw_vectors(key, part):
    key_gain, key_shift = jax.random.split(jax.random.fold_in(key, 3))
    gain_rows = jax.random.uniform(key_gain, (2, H, HD), jnp.float32, 0.6, 1.4)
    shift_rows = jnp.clip(jax.random.normal(key_shift, (4, H, HD), jnp.float32) * 0.3, -1.2, 1.2)
    stacked = jnp.stack([gain_rows[0], shift_rows[0], shift_rows[1], gain_rows[1], shift_rows[2], shift_rows[3]])
    return stacked.astype(jnp.bfloat16)


def draw_state_qkv(key, part):
    return draw_moments(key, (D, 3, H, HD), 0.3)


def draw_state_qkv_bias(key, part):
    return draw_moments(key, (2, H, HD), 0.3)


def draw_state_out(key, part):
    return draw_moments(key, (H, HD, D), 1.0)


def draw_state_up(key, part):
    return draw_moments(key, (D, FF // HD, HD), 0.25)


def draw_state_up_bias(key, part):
    return draw_moments(key, (FF // HD, HD), 0.25)


def draw_state_down(key, part):
    return draw_moments(key, (FF // HD, HD, D), 0.5)


def draw_state_vectors(key, part):
    return draw_moments(key, (6, H, HD), 1.0)


def levels(key, shape, pieces, least, high):
    factor_of, own = 1.0, jax.random.fold_in(key, 6)
    for position, parts in pieces:
        steps = jnp.exp(jax.random.uniform(jax.random.fold_in(own, position), (parts,), jnp.float32, least / len(pieces), high / len(pieces)))
        factor_of = factor_of * jnp.repeat(steps, shape[position] // parts).reshape([-1 if axis == position else 1 for axis in range(len(shape))])
    return factor_of


def normal_values(own_key, dims, deviation, most, pieces=(), dtype=jnp.bfloat16):
    drawn = jax.random.normal(own_key, dims, jnp.float32) * deviation
    if len(pieces) > 0:
        drawn = levels(own_key, dims, pieces, -0.22, 0.18) * drawn
    return jnp.clip(drawn, min=-most, max=most).astype(dtype)


def setup_inputs(seed: int = 0) -> dict:
    splits = jax.random.split(jax.random.key(seed), 17)
    tokens = normal_values(splits[0], (TOKENS, D), 1.0, 6.0, ((0, 4), (1, 8)), jnp.float32)
    cotangent = normal_values(splits[1], (TOKENS, D), 1.0, 6.0, ((0, 4), (1, 8)), jnp.float32)
    w_qkv = draw_w_qkv(jax.random.fold_in(splits[16], 71), 0)
    b_qkv = normal_values(splits[3], (2, H, HD), 0.5, 3.0, ((1, 2), (2, 4)))
    w_out = normal_values(splits[4], (H, HD, D), (HD // 2) ** -0.5, 1.0, ((0, 2), (1, 4), (2, 4)))
    w_up = draw_w_up(jax.random.fold_in(splits[16], 71), 0)
    b_up = normal_values(splits[6], (FF // HD, HD), 0.5, 3.0, ((0, 2), (1, 4)))
    w_down = normal_values(splits[7], (FF // HD, HD, D), FF ** -0.5, 0.09375, ((0, 2), (1, 4), (2, 4)))
    vectors = draw_vectors(jax.random.fold_in(splits[16], 71), 0)
    state_qkv = draw_state_qkv(jax.random.fold_in(splits[16], 71), 0)
    state_qkv_bias = draw_state_qkv_bias(jax.random.fold_in(splits[16], 71), 0)
    state_out = draw_state_out(jax.random.fold_in(splits[16], 71), 0)
    state_up = draw_state_up(jax.random.fold_in(splits[16], 71), 0)
    state_up_bias = draw_state_up_bias(jax.random.fold_in(splits[16], 71), 0)
    state_down = draw_state_down(jax.random.fold_in(splits[16], 71), 0)
    state_vectors = draw_state_vectors(jax.random.fold_in(splits[16], 71), 0)
    return {"tokens": tokens, "cotangent": cotangent, "w_qkv": w_qkv, "b_qkv": b_qkv, "w_out": w_out, "w_up": w_up, "b_up": b_up, "w_down": w_down, "vectors": vectors, "state_qkv": state_qkv, "state_qkv_bias": state_qkv_bias, "state_out": state_out, "state_up": state_up, "state_up_bias": state_up_bias, "state_down": state_down, "state_vectors": state_vectors}


norm_eps = 1e-06
beta_first = 0.9
beta_second = 0.999
learn_rate = 0.01
weight_decay = 0.05
adam_eps = 1e-08
grad_gain = 32.0

@jax.custom_vjp
def low(v):
    return lax.optimization_barrier(v.astype(jnp.bfloat16)).astype(jnp.float32)

@jax.custom_vjp
def low_back(v):
    return v

def low_keep(v):
    return (low(v), None)

def low_pass(kept, grad):
    return (grad,)

def back_keep(v):
    return (v, None)

def back_low(kept, grad):
    return (low(grad),)
low.defvjp(low_keep, low_pass)
low_back.defvjp(back_keep, back_low)

def product(left, right):
    return jnp.dot(left, right, precision=lax.Precision.HIGHEST)

def layer_norm(stream, norm_gain, norm_shift):
    center = lax.optimization_barrier(jnp.mean(stream, axis=-1, keepdims=True))
    offset = stream - center
    spread = lax.optimization_barrier(jnp.mean(offset * offset, axis=-1, keepdims=True))
    return offset * lax.rsqrt(spread + norm_eps) * norm_gain + norm_shift

def forward(tokens, w_qkv, b_qkv, w_out, w_up, b_up, w_down, vectors):
    feature_width = w_qkv.shape[0]
    vector_rows = vectors.reshape(6, feature_width)
    normed_one = low(layer_norm(tokens, vector_rows[0], vector_rows[1]))
    bias_full = jnp.stack([b_qkv[0], jnp.zeros_like(b_qkv[0]), b_qkv[1]]).reshape(-1)
    packed = product(normed_one, w_qkv.reshape(feature_width, -1)) + bias_full
    packed = low(low_back(packed))
    split_heads = packed.reshape(-1, SEQ, 3, H, HD)
    queries = split_heads[:, :, 0]
    key_rows = split_heads[:, :, 1]
    values = split_heads[:, :, 2]
    scores = jnp.einsum('nqhe,nkhe->nhqk', queries, key_rows, precision=lax.Precision.HIGHEST) * (1.0 / math.sqrt(HD))
    scores = low_back(scores)
    shifted = jnp.exp(scores - lax.optimization_barrier(jnp.max(scores, axis=-1, keepdims=True)))
    weights = shifted / lax.optimization_barrier(jnp.sum(shifted, axis=-1, keepdims=True))
    attended = jnp.einsum('nhqk,nkhe->nqhe', low(weights), values, precision=lax.Precision.HIGHEST)
    attended = low(low_back(attended.reshape(-1, feature_width)))
    branch = low_back(product(attended, w_out.reshape(feature_width, feature_width)) + vector_rows[2])
    middle = tokens + branch
    normed_two = low(layer_norm(middle, vector_rows[3], vector_rows[4]))
    hidden = low_back(product(normed_two, w_up.reshape(feature_width, -1)) + b_up.reshape(-1))
    activated = low(jax.nn.gelu(hidden, approximate=False))
    mixed = low_back(product(activated, w_down.reshape(-1, feature_width)) + vector_rows[5])
    return middle + mixed

def adam_step(weight_old, gradient, moments, decay_on):
    first_moment = beta_first * moments[0] + (1.0 - beta_first) * gradient
    second_moment = beta_second * moments[1] + (1.0 - beta_second) * gradient * gradient
    first_hat = first_moment / (1.0 - beta_first ** STEP)
    second_hat = second_moment / (1.0 - beta_second ** STEP)
    change = -learn_rate * (first_hat / (jnp.sqrt(second_hat) + adam_eps) + decay_on * weight_old)
    return (change, jnp.stack([first_moment, second_moment]))

def reference(tokens, cotangent, w_qkv, b_qkv, w_out, w_up, b_up, w_down, vectors, state_qkv, state_qkv_bias, state_out, state_up, state_up_bias, state_down, state_vectors):
    params = (w_qkv.astype(jnp.float32), b_qkv.astype(jnp.float32), w_out.astype(jnp.float32), w_up.astype(jnp.float32), b_up.astype(jnp.float32), w_down.astype(jnp.float32), vectors.astype(jnp.float32))
    result, pull_back = jax.vjp(forward, tokens, params[0], params[1], params[2], params[3], params[4], params[5], params[6])
    gradients = pull_back(cotangent)
    grad_scale = grad_gain / math.sqrt(tokens.shape[0])
    states = (state_qkv, state_qkv_bias, state_out, state_up, state_up_bias, state_down, state_vectors)
    decays = (weight_decay, 0.0, weight_decay, weight_decay, 0.0, weight_decay, 0.0)
    scaled = []
    updated = []
    fresh = []
    for number in range(7):
        gradient = gradients[number + 1] * grad_scale
        change, moments = adam_step(params[number], gradient, states[number], decays[number])
        scaled.append(gradient)
        updated.append(change)
        fresh.append(moments)
    return (result, gradients[0], scaled[0], scaled[1], scaled[2], scaled[3], scaled[4], scaled[5], scaled[6], updated[0], updated[1], updated[2], updated[3], updated[4], updated[5], updated[6], fresh[0], fresh[1], fresh[2], fresh[3], fresh[4], fresh[5], fresh[6])
```

```python
import math

import jax
import jax.numpy as jnp
from jax import lax
from jax.sharding import PartitionSpec as P

HD = 64
SEQ = 197
STEP = 10

norm_eps = 1e-06
beta_first = 0.9
beta_second = 0.999
learn_rate = 0.01
weight_decay = 0.05
adam_eps = 1e-08
grad_gain = 32.0

LOW = jnp.bfloat16
WIDE = jnp.float32


def turn(values, shift):
    count = lax.axis_size("row")
    return lax.ppermute(values, "row", [(i, (i + shift) % count) for i in range(count)])


def swap_col(values):
    return lax.ppermute(values, "col", [(0, 1), (1, 0)])


def swap_dp(values, bit):
    count = lax.axis_size("dp")
    return lax.ppermute(values, "dp", [(i, i ^ bit) for i in range(count)])


def dp_bits():
    bits = []
    bit = 1
    while bit < lax.axis_size("dp"):
        bits.append(bit)
        bit *= 2
    return bits


def gather_row(values):
    return [values] + [turn(values, k) for k in range(1, lax.axis_size("row"))]


def gather_dp(values):
    blocks = {0: values}
    for bit in reversed(dp_bits()):
        for place in list(blocks):
            blocks[place ^ bit] = swap_dp(blocks[place], bit)
    return [blocks[d] for d in range(len(blocks))]


def scatter_dp(blocks, kind):
    held = dict(enumerate(blocks))
    for bit in dp_bits():
        for place in [d for d in held if not d & bit]:
            came = swap_dp(held.pop(place ^ bit), bit)
            held[place] = (held[place].astype(WIDE) + came.astype(WIDE)).astype(kind)
    return held[0]


def scatter_row(blocks):
    total = blocks[0].astype(WIDE)
    for k in range(1, len(blocks)):
        total = total + turn(blocks[k], -k).astype(WIDE)
    return total


def xor_order(values, axis):
    mine = lax.axis_index("dp")
    shape = values.shape
    for bit in dp_bits():
        split = values.reshape(shape[:axis] + (shape[axis] // (2 * bit), 2, bit) + shape[axis + 1 :])
        flipped = jnp.flip(split, axis + 1)
        values = jnp.where((mine & bit) > 0, flipped, split).reshape(shape)
    return values


def exact_gelu(values):
    return jax.nn.gelu(values, approximate=False)


def adam_step(weight_old, gradient, moments, decay_on):
    first_moment = beta_first * moments[0] + (1.0 - beta_first) * gradient
    second_moment = beta_second * moments[1] + (1.0 - beta_second) * gradient * gradient
    first_hat = first_moment / (1.0 - beta_first**STEP)
    second_hat = second_moment / (1.0 - beta_second**STEP)
    change = -learn_rate * (first_hat / (jnp.sqrt(second_hat) + adam_eps) + decay_on * weight_old)
    return (change, jnp.stack([first_moment, second_moment]))


def dot_nt(left, right):
    return jnp.einsum("nta,fa->ntf", left, right, preferred_element_type=WIDE)


def dot_nn(left, right):
    return jnp.einsum("ntf,fa->nta", left, right, preferred_element_type=WIDE)


def dot_tn(left, right):
    return jnp.einsum("ntf,nta->fa", left, right, preferred_element_type=WIDE)


def norm_forward(stream, gain, shift):
    center = jnp.mean(stream, axis=-1, keepdims=True)
    offset = stream - center
    inv_std = lax.rsqrt(jnp.mean(offset * offset, axis=-1, keepdims=True) + norm_eps)
    scaled = offset * inv_std
    return (scaled * gain + shift).astype(LOW), scaled, inv_std


def norm_backward(grad_norm, scaled, inv_std, gain):
    weighted = grad_norm * gain
    return inv_std * (
        weighted
        - jnp.mean(weighted, axis=-1, keepdims=True)
        - scaled * jnp.mean(weighted * scaled, axis=-1, keepdims=True)
    )


def attend(packed_low, heads):
    split = packed_low.reshape(packed_low.shape[0], SEQ, 3, heads, HD)
    scores = jnp.einsum("nqhe,nkhe->nhqk", split[:, :, 0], split[:, :, 1], preferred_element_type=WIDE) * (1.0 / math.sqrt(HD))
    row_max = jnp.max(scores, axis=-1, keepdims=True)
    log_total = row_max + jnp.log(jnp.sum(jnp.exp(scores - row_max), axis=-1, keepdims=True))
    weights = jnp.exp(scores - log_total).astype(LOW)
    attended = jnp.einsum("nhqk,nkhe->nqhe", weights, split[:, :, 2], preferred_element_type=WIDE)
    return attended.reshape(packed_low.shape[0], SEQ, -1).astype(LOW), log_total


def attend_back(packed_low, log_total, grad_low, heads):
    split = packed_low.reshape(packed_low.shape[0], SEQ, 3, heads, HD)
    queries, key_rows, values = split[:, :, 0], split[:, :, 1], split[:, :, 2]
    score_scale = 1.0 / math.sqrt(HD)
    scores = jnp.einsum("nqhe,nkhe->nhqk", queries, key_rows, preferred_element_type=WIDE) * score_scale
    weights = jnp.exp(scores - log_total)
    grad_heads = grad_low.reshape(queries.shape)
    grad_values = jnp.einsum("nhqk,nqhe->nkhe", weights.astype(LOW), grad_heads, preferred_element_type=WIDE)
    grad_weights = jnp.einsum("nqhe,nkhe->nhqk", grad_heads, values, preferred_element_type=WIDE)
    grad_scores = weights * (grad_weights - jnp.sum(grad_weights * weights, axis=-1, keepdims=True))
    grad_scores = grad_scores.astype(LOW)
    grad_queries = jnp.einsum("nhqk,nkhe->nqhe", grad_scores, key_rows, preferred_element_type=WIDE) * score_scale
    grad_keys = jnp.einsum("nhqk,nqhe->nkhe", grad_scores, queries, preferred_element_type=WIDE) * score_scale
    stacked = jnp.stack([grad_queries, grad_keys, grad_values], axis=2)
    return stacked.reshape(packed_low.shape[0], SEQ, -1).astype(LOW)


def on_device(
    tokens, cotangent, w_qkv, b_qkv, w_out, w_up, b_up, w_down, vectors,
    state_qkv, state_qkv_bias, state_out, state_up, state_up_bias, state_down, state_vectors,
):
    parts, rows = lax.axis_size("dp"), lax.axis_size("row")
    low_col = lax.axis_index("col") == 0
    row_index = lax.axis_index("row")
    width = w_qkv.shape[0]
    heads, chunk = w_qkv.shape[2], w_qkv.shape[3]
    groups = w_up.shape[1]
    strip = tokens.shape[1]
    images = tokens.shape[0] // (SEQ * rows)

    qkv_own = w_qkv.transpose(1, 2, 3, 0).reshape(-1, width)
    out_own = w_out.reshape(-1, width)
    up_own = w_up.transpose(1, 2, 0).reshape(-1, width)
    down_own = w_down.reshape(-1, width)

    vec_own = vectors.reshape(-1)
    vec_far = swap_col(vec_own)
    vec_pair = jnp.stack([jnp.where(low_col, vec_own, vec_far), jnp.where(low_col, vec_far, vec_own)])

    def to_images(stream):
        blocks = stream.astype(LOW).reshape(rows, images, SEQ, strip)
        came = [lax.dynamic_index_in_dim(blocks, row_index, 0, False)]
        for k in range(1, rows):
            came.append(turn(lax.dynamic_index_in_dim(blocks, (row_index + k) % rows, 0, False), k))
        near = jnp.stack(came)
        far = swap_col(near)
        both = jnp.stack([jnp.where(low_col, near, far), jnp.where(low_col, far, near)])
        return both.transpose(2, 3, 1, 0, 4).reshape(images, SEQ, -1)

    def own_strips(stream):
        split = stream.reshape(images, SEQ, rows, 2, strip)
        return (
            jnp.where(low_col, split[:, :, :, 0], split[:, :, :, 1]),
            jnp.where(low_col, split[:, :, :, 1], split[:, :, :, 0]),
        )

    def from_images(strips):
        came = [strips[:, :, 0]] + [turn(strips[:, :, k], -k) for k in range(1, rows)]
        stacked = jnp.stack(came)
        order = (jnp.arange(rows) - row_index) % rows
        return stacked[order].reshape(-1, strip).astype(WIDE)

    stream = to_images(tokens).astype(WIDE)

    small_own = jnp.concatenate([b_qkv.reshape(-1), b_up.reshape(-1)])
    vec_blocks = gather_row(vec_pair.reshape(-1))
    small_rows = jnp.stack([jnp.concatenate([small_own, block]) for block in vec_blocks])
    small_size = small_rows.shape[1]
    pad = -small_size % (16 * width)
    small_rows = jnp.pad(small_rows, ((0, 0), (0, pad))).reshape(rows, -1, width)
    first = jnp.concatenate([jnp.stack(gather_row(qkv_own)), small_rows], axis=1)
    first_all = jnp.stack(gather_dp(first))
    second_all = jnp.stack(gather_dp(jnp.stack(gather_row(jnp.concatenate([out_own, up_own])))))
    third_all = jnp.stack(gather_dp(jnp.stack(gather_row(down_own))))

    qkv_count = qkv_own.shape[0]
    small = first_all[:, :, qkv_count:].reshape(parts, rows, -1)[:, :, :small_size]
    bias_qkv = small[:, 0, : 2 * heads * chunk].reshape(parts, 2, heads, chunk).transpose(1, 2, 0, 3).reshape(2, -1).astype(WIDE)
    at = 2 * heads * chunk
    bias_up = small[:, 0, at : at + groups * chunk].reshape(-1).astype(WIDE)
    at = at + groups * chunk
    vec = xor_order(small[:, :, at:].reshape(parts, rows, 2, 6, 2, chunk), 0)
    vec = vec.transpose(3, 1, 2, 4, 0, 5).reshape(6, -1).astype(WIDE)

    def flat(blocks):
        return blocks.transpose(0, 2, 1, 3).reshape(-1, rows * width)

    qkv_flat = flat(
        first_all[:, :, :qkv_count].reshape(parts, rows, 3 * heads, chunk, width).transpose(2, 1, 0, 3, 4).reshape(3 * heads, rows, -1, width)
    )
    out_count = out_own.shape[0]
    out_flat = flat(second_all[:, :, :out_count].reshape(parts, rows, heads, chunk, width).transpose(2, 1, 0, 3, 4).reshape(heads, rows, -1, width))
    up_flat = flat(second_all[:, :, out_count:])
    down_flat = flat(third_all)

    grad_stream = to_images(cotangent)
    grad_wide = grad_stream.astype(WIDE)

    normed_one, scaled_one, inv_one = norm_forward(stream, vec[0], vec[1])
    packed = dot_nt(normed_one, qkv_flat)
    packed = packed + jnp.concatenate([bias_qkv[0], jnp.zeros_like(bias_qkv[0]), bias_qkv[1]])
    packed_low = packed.astype(LOW)
    heads_low, log_total = attend(packed_low, heads)
    branch = dot_nn(heads_low, out_flat).astype(LOW)
    middle = stream + (branch.astype(WIDE) + swap_col(branch).astype(WIDE) + vec[2])
    normed_two, scaled_two, inv_two = norm_forward(middle, vec[3], vec[4])
    hidden = dot_nt(normed_two, up_flat) + bias_up
    activated, gelu_pull = jax.vjp(exact_gelu, hidden)
    units_low = activated.astype(LOW)
    mixed = dot_nn(units_low, down_flat)
    mixed_near, mixed_far = own_strips(mixed)
    top = own_strips(middle + vec[5])[0] + mixed_near + swap_col(mixed_far.astype(LOW)).astype(WIDE)
    result = from_images(top.astype(LOW))

    grad_hidden = gelu_pull(dot_nt(grad_stream, down_flat))[0].astype(LOW)
    up_back = dot_nn(grad_hidden, up_flat).astype(LOW)
    grad_normed_two = up_back.astype(WIDE) + swap_col(up_back).astype(WIDE)
    down_grad = dot_tn(units_low, grad_stream)
    up_grad = dot_tn(grad_hidden, normed_two)
    grad_middle = grad_wide + norm_backward(grad_normed_two, scaled_two, inv_two, vec[3])
    grad_branch = grad_middle.astype(LOW)
    grad_heads = dot_nt(grad_branch, out_flat).astype(LOW)
    out_grad = dot_tn(heads_low, grad_branch)
    grad_packed = attend_back(packed_low, log_total, grad_heads, heads)
    qkv_grad = dot_tn(grad_packed, normed_one)
    back_one = dot_nn(grad_packed, qkv_flat).astype(LOW)
    grad_normed_one = back_one.astype(WIDE) + swap_col(back_one).astype(WIDE)
    grad_tokens = grad_middle + norm_backward(grad_normed_one, scaled_one, inv_one, vec[0])
    grad_tokens = from_images(own_strips(grad_tokens)[0].astype(LOW))

    def to_blocks(grad, lead):
        split = grad.astype(LOW).reshape(lead, parts, chunk, rows, width)
        return split.transpose(1, 3, 0, 2, 4).reshape(parts, rows, -1, width)

    def to_unit_blocks(grad):
        return grad.astype(LOW).reshape(parts, -1, rows, width).transpose(0, 2, 1, 3)

    feed = jnp.concatenate([to_unit_blocks(up_grad), to_unit_blocks(down_grad)], axis=2)
    feed = scatter_dp([feed[d] for d in range(parts)], LOW)
    feed = scatter_row([feed[k] for k in range(rows)])
    attn = jnp.concatenate([to_blocks(qkv_grad, 3 * heads), to_blocks(out_grad, heads)], axis=2)
    attn = scatter_dp([attn[d] for d in range(parts)], LOW)
    attn = scatter_row([attn[k] for k in range(rows)])

    token_sum = lambda v: jnp.sum(v.astype(WIDE), axis=(0, 1))
    vector_sum = jnp.stack([
        token_sum(grad_normed_one * scaled_one),
        token_sum(grad_normed_one),
        token_sum(grad_branch),
        token_sum(grad_normed_two * scaled_two),
        token_sum(grad_normed_two),
        token_sum(grad_stream),
    ])
    packed_sum = token_sum(grad_packed).reshape(3, heads, parts, chunk)
    packed_sum = packed_sum[jnp.array([0, 2])].transpose(2, 0, 1, 3).reshape(parts, -1)
    unit_sum = token_sum(grad_hidden).reshape(parts, -1)
    vector_split = vector_sum.reshape(6, rows, 2, 2, parts, chunk)
    vector_split = jnp.where(low_col, vector_split[:, :, 0], vector_split[:, :, 1])
    vector_split = xor_order(vector_split.transpose(3, 1, 0, 2, 4), 0)
    vector_split = vector_split[:, (row_index - jnp.arange(rows)) % rows]
    tiny = jnp.concatenate([packed_sum, unit_sum, vector_split.reshape(parts, -1)], axis=1)
    tiny = scatter_dp([tiny[d] for d in range(parts)], WIDE)
    tiny = lax.psum(tiny, "row")
    size_packed, size_unit = packed_sum.shape[1], unit_sum.shape[1]
    tiny_vec = tiny[size_packed + size_unit :].reshape(rows, 6, 2, chunk)
    tiny_vec = lax.dynamic_index_in_dim(tiny_vec, row_index, 0, False)

    feed_up, feed_down = feed[: up_own.shape[0]], feed[up_own.shape[0] :]
    attn_qkv, attn_out = attn[:qkv_count], attn[qkv_count:]
    summed = (
        attn_qkv.reshape(3, heads, chunk, width).transpose(3, 0, 1, 2),
        tiny[:size_packed].reshape(b_qkv.shape),
        attn_out.reshape(w_out.shape),
        feed_up.reshape(groups, chunk, width).transpose(2, 0, 1),
        tiny[size_packed : size_packed + size_unit].reshape(b_up.shape),
        feed_down.reshape(w_down.shape),
        tiny_vec,
    )
    grad_scale = grad_gain / math.sqrt(tokens.shape[0] * parts)
    old_params = (w_qkv, b_qkv, w_out, w_up, b_up, w_down, vectors)
    states = (state_qkv, state_qkv_bias, state_out, state_up, state_up_bias, state_down, state_vectors)
    decays = (weight_decay, 0.0, weight_decay, weight_decay, 0.0, weight_decay, 0.0)
    scaled, updated, fresh = [], [], []
    for number in range(7):
        gradient = summed[number] * grad_scale
        change, moments = adam_step(old_params[number].astype(WIDE), gradient, states[number], decays[number])
        scaled.append(gradient)
        updated.append(change)
        fresh.append(moments)
    return (result, grad_tokens, *scaled, *updated, *fresh)


def solution(mesh):
    placed = (
        P("dp", ("row", "col")),
        P("dp", ("row", "col")),
        P("row", None, "col", "dp"),
        P(None, "col", "dp"),
        P("col", "dp", "row"),
        P("row", "col", "dp"),
        P("col", "dp"),
        P("col", "dp", "row"),
        P(None, ("row", "col"), "dp"),
        P(None, "row", None, "col", "dp"),
        P(None, None, "col", "dp"),
        P(None, "col", "dp", "row"),
        P(None, "row", "col", "dp"),
        P(None, "col", "dp"),
        P(None, "col", "dp", "row"),
        P(None, None, ("row", "col"), "dp"),
    )
    params = placed[2:9]
    return jax.shard_map(
        on_device,
        mesh=mesh,
        in_specs=placed,
        out_specs=(placed[0], placed[0], *params, *params, *placed[9:]),
        check_vma=False,
    )
```

```python
import functools
import math

import jax
import jax.numpy as jnp
from jax import lax
from jax.experimental import pallas as pl
from jax.experimental.pallas import tpu as pltpu
from jax.sharding import PartitionSpec as P

HD = 64
SEQ = 197
PAD = 208
STEP = 10

norm_eps = 1e-06
beta_first = 0.9
beta_second = 0.999
learn_rate = 0.01
weight_decay = 0.05
adam_eps = 1e-08
grad_gain = 32.0

LOW = jnp.bfloat16
WIDE = jnp.float32


def turn(values, shift):
    count = lax.axis_size("row")
    return lax.ppermute(values, "row", [(i, (i + shift) % count) for i in range(count)])


def swap_col(values):
    return lax.ppermute(values, "col", [(0, 1), (1, 0)])


def swap_dp(values, bit):
    count = lax.axis_size("dp")
    return lax.ppermute(values, "dp", [(i, i ^ bit) for i in range(count)])


def dp_bits():
    bits = []
    bit = 1
    while bit < lax.axis_size("dp"):
        bits.append(bit)
        bit *= 2
    return bits


def gather_row(values):
    return [values] + [turn(values, k) for k in range(1, lax.axis_size("row"))]


def gather_dp(values):
    blocks = {0: values}
    for bit in reversed(dp_bits()):
        for place in list(blocks):
            blocks[place ^ bit] = swap_dp(blocks[place], bit)
    return [blocks[d] for d in range(len(blocks))]


def scatter_dp(blocks, kind):
    held = dict(enumerate(blocks))
    for bit in dp_bits():
        for place in [d for d in held if not d & bit]:
            came = swap_dp(held.pop(place ^ bit), bit)
            held[place] = (held[place].astype(WIDE) + came.astype(WIDE)).astype(kind)
    return held[0]


def scatter_row(blocks):
    total = blocks[0].astype(WIDE)
    for k in range(1, len(blocks)):
        total = total + turn(blocks[k], -k).astype(WIDE)
    return total


def xor_order(values, axis):
    mine = lax.axis_index("dp")
    shape = values.shape
    for bit in dp_bits():
        split = values.reshape(shape[:axis] + (shape[axis] // (2 * bit), 2, bit) + shape[axis + 1 :])
        flipped = jnp.flip(split, axis + 1)
        values = jnp.where((mine & bit) > 0, flipped, split).reshape(shape)
    return values


def adam_step(weight_old, gradient, moments, decay_on):
    first_moment = beta_first * moments[0] + (1.0 - beta_first) * gradient
    second_moment = beta_second * moments[1] + (1.0 - beta_second) * gradient * gradient
    first_hat = first_moment / (1.0 - beta_first**STEP)
    second_hat = second_moment / (1.0 - beta_second**STEP)
    change = -learn_rate * (first_hat / (jnp.sqrt(second_hat) + adam_eps) + decay_on * weight_old)
    return (change, jnp.stack([first_moment, second_moment]))


def dot_nt(left, right):
    return lax.dot_general(left, right, (((1,), (1,)), ((), ())), preferred_element_type=WIDE)


def dot_nn(left, right):
    return lax.dot_general(left, right, (((1,), (0,)), ((), ())), preferred_element_type=WIDE)


def dot_tn(left, right):
    return lax.dot_general(left, right, (((0,), (0,)), ((), ())), preferred_element_type=WIDE)


def moments_of(stream):
    center = jnp.mean(stream, axis=-1, keepdims=True)
    offset = stream - center
    inv_std = lax.rsqrt(jnp.mean(offset * offset, axis=-1, keepdims=True) + norm_eps)
    return offset * inv_std, inv_std


def norm_backward(grad_norm, scaled, inv_std, gain):
    weighted = grad_norm * gain
    return inv_std * (
        weighted
        - jnp.mean(weighted, axis=-1, keepdims=True)
        - scaled * jnp.mean(weighted * scaled, axis=-1, keepdims=True)
    )


def lay_strips(low_col, near, far, rows):
    pieces = []
    for k in range(rows):
        mine, other = near(k), far(k)
        pieces.append(jnp.where(low_col, mine, other))
        pieces.append(jnp.where(low_col, other, mine))
    return jnp.concatenate(pieces, axis=1)


def lay_rows(blocks, rows, first, count):
    parts = []
    for k in range(rows):
        total = blocks[0][k, first:, :].astype(WIDE)
        for block in blocks[1:]:
            total = total + block[k, first:, :].astype(WIDE)
        parts.append(total[:count])
    return jnp.concatenate(parts, axis=1)


def lay_heads(target, blocks, me, groups, rows):
    own = HD // len(blocks)
    for k in range(rows):
        for d, block in enumerate(blocks):
            place = me ^ d if len(blocks) > 1 else 0
            for g in range(groups):
                at = g * HD + place * own
                if len(blocks) > 1:
                    at = pl.multiple_of(at, own)
                target[k, pl.ds(at, own), :] = block[k, g * own : (g + 1) * own, :]


def soft(scores):
    lane = lax.broadcasted_iota(jnp.int32, scores.shape, 1)
    scores = jnp.where(lane < SEQ, scores * (1.0 / math.sqrt(HD)), -1e30)
    raised = jnp.exp(scores - jnp.max(scores, axis=-1, keepdims=True))
    return raised * (1.0 / jnp.sum(raised, axis=-1, keepdims=True))


def first_kernel(spec, pos, near, far, *refs):
    n, rows, heads, width = spec
    qkv, out = refs[:n], refs[n : 2 * n]
    vec_o, x_o, normed_o, packed_o, att_o, part_o, qkv_s, out_s = refs[2 * n :]
    low_col, me = pos[0] == 0, pos[1]
    count = 3 * heads * HD // n
    vec = lay_rows(qkv, rows, count, 6)
    vec_o[0:6, :] = vec
    small = qkv[0][0, count:, :].astype(WIDE)
    for d in range(1, n):
        small = small + qkv[d][0, count:, :].astype(WIDE)
    lay_heads(qkv_s, qkv, me, 3 * heads, rows)
    lay_heads(out_s, out, me, heads, rows)
    stream = lay_strips(low_col, lambda k: near[k, 0], lambda k: far[k, 0], rows)
    x_o[...] = stream
    scaled, _ = moments_of(stream.astype(WIDE))
    normed = (scaled * vec[0:1] + vec[1:2]).astype(LOW)
    normed_o[...] = normed
    span = heads * HD
    lines = span // width
    for part in range(3):
        total = dot_nt(normed[:, :width], qkv_s[0, part * span : (part + 1) * span, :])
        for k in range(1, rows):
            total = total + dot_nt(normed[:, k * width : (k + 1) * width], qkv_s[k, part * span : (part + 1) * span, :])
        if part != 1:
            line = 6 + (lines if part == 2 else 0)
            total = total + jnp.concatenate([small[line + i : line + i + 1] for i in range(lines)], axis=1)
        packed_o[:, part * span : (part + 1) * span] = total.astype(LOW)
    two = 2 * HD
    lane = lax.broadcasted_iota(jnp.int32, (1, two), 1)
    for pair in range(heads // 2):
        at = pair * two
        queries = packed_o[:, at : at + two]
        key_rows = packed_o[:, span + at : span + at + two]
        values = packed_o[:, 2 * span + at : 2 * span + at + two]
        halves = []
        for side in range(2):
            mask = (lane < HD) if side == 0 else (lane >= HD)
            probs = soft(dot_nt(jnp.where(mask, queries, jnp.zeros_like(queries)), key_rows))
            halves.append(dot_nn(probs.astype(LOW), values))
        att_o[:, at : at + two] = jnp.where(lane < HD, halves[0], halves[1]).astype(LOW)
    for k in range(rows):
        part_o[:, k * width : (k + 1) * width] = dot_nn(att_o[...], out_s[k]).astype(LOW)


def gelu_both(values):
    tail = 0.5 * (1.0 + lax.erf(values * (1.0 / math.sqrt(2.0))))
    bell = jnp.exp(values * values * -0.5) * (1.0 / math.sqrt(2.0 * math.pi))
    return values * tail, tail + values * bell


def feed_kernel(spec, pos, vec, small, x, part, came, near, far, *refs):
    n, rows, groups, width, block = spec
    up, down = refs[:n], refs[n : 2 * n]
    (mid_o, normed_o, dy_o, units_o, hid_o, unit_sum_o, dy_sum_o, top_o, far_o, back_o, mixed_s, back_s) = refs[2 * n :]
    low_col, me = pos[0] == 0, pos[1]
    step = pl.program_id(0)

    @pl.when(step == 0)
    def _():
        dy = lay_strips(low_col, lambda k: near[k, 0], lambda k: far[k, 0], rows)
        dy_o[...] = dy
        dy_sum_o[...] = jnp.sum(dy.astype(WIDE), axis=0, keepdims=True)
        middle = x[...].astype(WIDE) + (part[...].astype(WIDE) + came[...].astype(WIDE) + vec[2:3, :])
        mid_o[...] = middle
        scaled, _ = moments_of(middle)
        normed_o[...] = (scaled * vec[3:4, :] + vec[4:5, :]).astype(LOW)
        mixed_s[...] = jnp.zeros_like(mixed_s)
        back_s[...] = jnp.zeros_like(back_s)

    def cols(ref, k):
        return ref[:, k * width : (k + 1) * width]

    up_rows = [jnp.concatenate([w[k] for w in up], axis=0) for k in range(rows)]
    down_rows = [jnp.concatenate([w[k] for w in down], axis=0) for k in range(rows)]
    hidden = dot_nt(cols(normed_o, 0), up_rows[0])
    for k in range(1, rows):
        hidden = hidden + dot_nt(cols(normed_o, k), up_rows[k])
    hidden = hidden + small[0]
    active, slope = gelu_both(hidden)
    active = active.astype(LOW)
    units_o[...] = active
    grad = dot_nt(cols(dy_o, 0), down_rows[0])
    for k in range(1, rows):
        grad = grad + dot_nt(cols(dy_o, k), down_rows[k])
    grad = (grad * slope).astype(LOW)
    hid_o[...] = grad
    unit_sum_o[...] = jnp.sum(grad.astype(WIDE), axis=0, keepdims=True)
    for k in range(rows):
        at = slice(k * width, (k + 1) * width)
        mixed_s[:, at] += dot_nn(active, down_rows[k])
        back_s[:, at] += dot_nn(grad, up_rows[k])

    @pl.when(step == pl.num_programs(0) - 1)
    def _():
        back_o[...] = back_s[...].astype(LOW)
        half = width // 2
        for k in range(rows):
            left, right = slice(k * width, k * width + half), slice(k * width + half, (k + 1) * width)
            base = mid_o[...] + vec[5:6, :]
            top_l, top_r = mixed_s[:, left] + base[:, left], mixed_s[:, right] + base[:, right]
            top_o[k] = jnp.where(low_col, top_l, top_r)
            far_o[k] = jnp.where(low_col, mixed_s[:, right], mixed_s[:, left]).astype(LOW)


def feed_grad_kernel(spec, *refs):
    n, rows, width = spec
    left, right, outs = refs[0:2], refs[2:4], refs[4:]
    total = dot_tn(left[0][...], right[0][...]) + dot_tn(left[1][...], right[1][...])
    block = total.shape[0] // n
    for d in range(n):
        for k in range(rows):
            outs[d][k] = total[d * block : (d + 1) * block, k * width : (k + 1) * width].astype(LOW)


def second_kernel(spec, pos, vec, mid, back, came, dy, packed, *refs):
    n, rows, heads, width = spec
    qkv, out = refs[:n], refs[n : 2 * n]
    dmid_o, dz_o, dpacked_o, back_o, sums_o, psum_o, qkv_s, out_s, datt_s = refs[2 * n :]
    me = pos[1]
    lay_heads(qkv_s, qkv, me, 3 * heads, rows)
    lay_heads(out_s, out, me, heads, rows)
    grad_norm = back[...].astype(WIDE) + came[...].astype(WIDE)
    scaled, inv_std = moments_of(mid[...])
    dmid = dy[...].astype(WIDE) + norm_backward(grad_norm, scaled, inv_std, vec[3:4, :])
    dmid_o[...] = dmid
    dz = dmid.astype(LOW)
    dz_o[...] = dz
    sums_o[0:1, :] = jnp.sum(dz.astype(WIDE), axis=0, keepdims=True)
    sums_o[1:2, :] = jnp.sum(grad_norm * scaled, axis=0, keepdims=True)
    sums_o[2:3, :] = jnp.sum(grad_norm, axis=0, keepdims=True)
    total = dot_nt(dz[:, :width], out_s[0])
    for k in range(1, rows):
        total = total + dot_nt(dz[:, k * width : (k + 1) * width], out_s[k])
    datt_s[...] = total.astype(LOW)
    span = heads * HD
    two = 2 * HD
    scale = 1.0 / math.sqrt(HD)
    lane = lax.broadcasted_iota(jnp.int32, (1, two), 1)
    for pair in range(heads // 2):
        at = pair * two
        queries = packed[:, at : at + two]
        key_rows = packed[:, span + at : span + at + two]
        values = packed[:, 2 * span + at : 2 * span + at + two]
        grads = datt_s[:, at : at + two]
        dqs, dks, dvs = [], [], []
        for side in range(2):
            mask = (lane < HD) if side == 0 else (lane >= HD)
            probs = soft(dot_nt(jnp.where(mask, queries, jnp.zeros_like(queries)), key_rows))
            dprobs = dot_nt(jnp.where(mask, grads, jnp.zeros_like(grads)), values)
            dscores = probs * (dprobs - jnp.sum(dprobs * probs, axis=-1, keepdims=True))
            dscores = dscores.astype(LOW)
            dqs.append(dot_nn(dscores, key_rows))
            dks.append(dot_tn(dscores, queries))
            dvs.append(dot_tn(probs.astype(LOW), grads))
        first = lane < HD
        dpacked_o[:, at : at + two] = (jnp.where(first, dqs[0], dqs[1]) * scale).astype(LOW)
        dpacked_o[:, span + at : span + at + two] = (jnp.where(first, dks[0], dks[1]) * scale).astype(LOW)
        dpacked_o[:, 2 * span + at : 2 * span + at + two] = jnp.where(first, dvs[0], dvs[1]).astype(LOW)
    psum_o[...] = jnp.sum(dpacked_o[...].astype(WIDE), axis=0, keepdims=True)
    for k in range(rows):
        back_o[:, k * width : (k + 1) * width] = dot_nn(dpacked_o[...], qkv_s[k]).astype(LOW)


def attn_grad_kernel(spec, pos, *refs):
    n, rows, heads, width = spec
    dpacked, normed, att, dz = refs[0:2], refs[2:4], refs[4:6], refs[6:8]
    outs, total_s = refs[8 : 8 + n], refs[8 + n]
    me = pos[1]
    span = heads * HD
    own = HD // n
    for part in range(4):
        if part < 3:
            at = slice(part * span, (part + 1) * span)
            total = dot_tn(dpacked[0][:, at], normed[0][...]) + dot_tn(dpacked[1][:, at], normed[1][...])
        else:
            total = dot_tn(att[0][...], dz[0][...]) + dot_tn(att[1][...], dz[1][...])
        total_s[...] = total.astype(LOW)
        for d in range(n):
            place = me ^ d if n > 1 else 0
            for g in range(heads):
                line = g * HD + place * own
                if n > 1:
                    line = pl.multiple_of(line, own)
                value = total_s[pl.ds(line, own), :]
                to = (part * heads + g) * own
                for k in range(rows):
                    outs[d][k, to : to + own, :] = value[:, k * width : (k + 1) * width]


def last_kernel(spec, pos, vec, *refs):
    rows, width, images = spec
    x, back, came, dmid = (refs[i * images : (i + 1) * images] for i in range(4))
    out_o, sums_o = refs[4 * images :]
    low_col = pos[0] == 0
    half = width // 2
    for i in range(images):
        scaled, inv_std = moments_of(x[i][...].astype(WIDE))
        grad_norm = back[i][...].astype(WIDE) + came[i][...].astype(WIDE)
        value = dmid[i][...] + norm_backward(grad_norm, scaled, inv_std, vec[0:1, :])
        gain_sum = jnp.sum(grad_norm * scaled, axis=0, keepdims=True)
        shift_sum = jnp.sum(grad_norm, axis=0, keepdims=True)
        if i == 0:
            sums_o[0:1, :] = gain_sum
            sums_o[1:2, :] = shift_sum
        else:
            sums_o[0:1, :] += gain_sum
            sums_o[1:2, :] += shift_sum
        for k in range(rows):
            left, right = value[:, k * width : k * width + half], value[:, k * width + half : (k + 1) * width]
            out_o[k, i] = jnp.where(low_col, left, right).astype(LOW)


ROOM = 56 * 1024 * 1024


def whole(array):
    zeros = (0,) * len(array.shape)
    return pl.BlockSpec(tuple(array.shape), lambda *_: zeros)


def run_kernel(body, args, outs, scratch=(), grid=None, in_specs=None, out_specs=None, flops=0):
    if in_specs is None:
        in_specs = [pl.BlockSpec(memory_space=pltpu.SMEM)] + [whole(a) for a in args[1:]]
    if out_specs is None:
        out_specs = [whole(o) for o in outs]
    size = sum(math.prod(a.shape) * a.dtype.itemsize for a in (*args, *outs))
    return pl.pallas_call(
        body,
        grid=grid or (1,),
        in_specs=in_specs,
        out_specs=out_specs,
        out_shape=outs,
        scratch_shapes=list(scratch),
        compiler_params=pltpu.CompilerParams(vmem_limit_bytes=ROOM),
        cost_estimate=pl.CostEstimate(flops=flops, bytes_accessed=size, transcendentals=0),
    )(*args)


def shaped(shape, kind):
    return jax.ShapeDtypeStruct(shape, kind)


def on_device(
    tokens, cotangent, w_qkv, b_qkv, w_out, w_up, b_up, w_down, vectors,
    state_qkv, state_qkv_bias, state_out, state_up, state_up_bias, state_down, state_vectors,
):
    parts, rows = lax.axis_size("dp"), lax.axis_size("row")
    col, row_index, me = lax.axis_index("col"), lax.axis_index("row"), lax.axis_index("dp")
    low_col = col == 0
    width = w_qkv.shape[0]
    heads, chunk = w_qkv.shape[2], w_qkv.shape[3]
    groups = w_up.shape[1]
    strip = tokens.shape[1]
    images = tokens.shape[0] // (SEQ * rows)
    model = rows * width
    span = heads * HD
    units = groups * HD
    pos = jnp.stack([col, me]).astype(jnp.int32)

    qkv_own = w_qkv.transpose(1, 2, 3, 0).reshape(-1, width)
    out_own = w_out.reshape(-1, width)
    up_own = w_up.transpose(1, 2, 0).reshape(-1, width)
    down_own = w_down.reshape(-1, width)
    qkv_count, out_count, up_count = qkv_own.shape[0], out_own.shape[0], up_own.shape[0]

    at_me = (jnp.arange(parts) == me)[:, None]
    vec_own = jnp.where(at_me, vectors[:, :, None, :], 0).reshape(6, -1)
    vec_far = swap_col(vec_own)
    vec_pair = jnp.stack([jnp.where(low_col, vec_own, vec_far), jnp.where(low_col, vec_far, vec_own)])
    bias_own = jnp.where(at_me, b_qkv[:, :, None, :], 0).reshape(-1, width)
    blocks_up = up_count // out_count
    unit_own = jnp.where(at_me, b_up.reshape(blocks_up, 1, -1), 0).reshape(-1, width)
    small_count = 6 + bias_own.shape[0] + unit_own.shape[0]
    small_pad = -small_count % 16

    def to_images(stream, extra):
        blocks = stream.astype(LOW).reshape(rows, images, SEQ, strip)
        blocks = jnp.pad(blocks, ((0, 0), (0, 0), (0, PAD - SEQ), (0, 0)))
        if extra is not None:
            extra = jnp.pad(extra, ((0, 0), (0, 2), (0, 0)))
            blocks = jnp.concatenate([blocks, jnp.broadcast_to(extra, (rows, *extra.shape))], axis=2)
        came = [lax.dynamic_index_in_dim(blocks, row_index, 0, False)]
        for k in range(1, rows):
            came.append(turn(lax.dynamic_index_in_dim(blocks, (row_index + k) % rows, 0, False), k))
        near = jnp.stack([block[:, :PAD] for block in came])
        return near, swap_col(near), came

    first = gather_row(qkv_own)
    near, far, came = to_images(tokens, vec_pair)
    vec_rows = [jnp.concatenate([block[0, PAD : PAD + 6], block[1, PAD : PAD + 6]], axis=1) for block in came]
    tail_rows = [
        jnp.concatenate([block, bias_own, unit_own, jnp.zeros((small_pad, width), LOW)]) for block in vec_rows
    ]
    first = jnp.stack([jnp.concatenate([a, b]) for a, b in zip(first, tail_rows)])
    first_all = gather_dp(first)
    second_all = gather_dp(jnp.stack(gather_row(jnp.concatenate([out_own, up_own]))))
    third_all = gather_dp(jnp.stack(gather_row(down_own)))
    near_dy, far_dy, _ = to_images(cotangent, None)

    own = chunk
    if chunk % 16:
        own = HD

        def merge(blocks, lead):
            both = xor_order(jnp.stack(blocks), 0).reshape(parts, rows, lead, -1, width)
            return both.transpose(1, 2, 0, 3, 4).reshape(rows, -1, width)

        heads_rows = merge([b[:, :qkv_count] for b in first_all], 3 * heads)
        small_rows = sum(b[:, qkv_count:].astype(WIDE) for b in first_all).astype(LOW)
        first_all = [jnp.concatenate([heads_rows, small_rows], axis=1)]
        out_rows = merge([b[:, :out_count] for b in second_all], heads)
        up_rows = merge([b[:, out_count:] for b in second_all], blocks_up)
        second_all = [jnp.concatenate([out_rows, up_rows], axis=1)]
        third_all = [merge(third_all, blocks_up)]
    n = len(first_all)
    out_rows_each = out_count * parts // n

    def source_specs(blocks, count, moving=None):
        if moving is None:
            return [pl.BlockSpec((rows, count, width), lambda *_: (0, 0, 0)) for _ in blocks]
        return [pl.BlockSpec((rows, count, width), lambda u: (0, u + moving, 0)) for _ in blocks]

    scalars = pl.BlockSpec(memory_space=pltpu.SMEM)
    first_rows = first_all[0].shape[1]

    def forward_one(i):
        strips = pl.BlockSpec((rows, 1, PAD, strip), lambda *_: (0, i, 0, 0))
        outs = [
            shaped((8, model), WIDE),
            shaped((PAD, model), LOW),
            shaped((PAD, model), LOW),
            shaped((PAD, 3 * span), LOW),
            shaped((PAD, span), LOW),
            shaped((PAD, model), LOW),
        ]
        return run_kernel(
            functools.partial(first_kernel, (n, rows, heads, width)),
            (pos, near, far, *first_all, *second_all),
            outs,
            scratch=[pltpu.VMEM((rows, 3 * span, width), LOW), pltpu.VMEM((rows, span, width), LOW)],
            in_specs=[scalars, strips, strips, *source_specs(first_all, first_rows), *source_specs(second_all, out_rows_each)],
            flops=10**10,
        )

    done = [forward_one(i) for i in range(images)]
    vec = done[0][0]
    came_one = [swap_col(d[5]) for d in done]

    unit_rows = sum(b[0, qkv_count * parts // n + 6 + bias_own.shape[0] :][: unit_own.shape[0]].astype(WIDE) for b in first_all)
    unit_rows = unit_rows.reshape(blocks_up, parts, -1)
    if n > 1:
        unit_rows = xor_order(unit_rows, 1)
    unit_rows = unit_rows.reshape(blocks_up, 1, -1)
    block_units = units // blocks_up

    def feed_one(i):
        strips = pl.BlockSpec((rows, 1, PAD, strip), lambda *_: (0, i, 0, 0))
        x, part = done[i][1], done[i][5]
        outs = [
            shaped((PAD, model), WIDE),
            shaped((PAD, model), LOW),
            shaped((PAD, model), LOW),
            shaped((PAD, units), LOW),
            shaped((PAD, units), LOW),
            shaped((1, units), WIDE),
            shaped((1, model), WIDE),
            shaped((rows, PAD, strip), WIDE),
            shaped((rows, PAD, strip), LOW),
            shaped((PAD, model), LOW),
        ]
        by_block = lambda lead: pl.BlockSpec((lead, block_units), lambda u: (0, u))
        out_specs = [whole(o) for o in outs]
        out_specs[3], out_specs[4], out_specs[5] = by_block(PAD), by_block(PAD), by_block(1)
        return run_kernel(
            functools.partial(feed_kernel, (n, rows, groups, width, block_units)),
            (pos, vec, unit_rows, x, part, came_one[i], near_dy, far_dy, *second_all, *third_all),
            outs,
            scratch=[pltpu.VMEM((PAD, model), WIDE), pltpu.VMEM((PAD, model), WIDE)],
            grid=(blocks_up,),
            in_specs=[
                scalars, whole(vec), pl.BlockSpec((1, 1, block_units), lambda u: (u, 0, 0)), whole(x), whole(part), whole(part),
                strips, strips,
                *source_specs(second_all, out_rows_each, 1), *source_specs(third_all, out_rows_each, 0),
            ],
            out_specs=out_specs,
            flops=10**10,
        )

    fed = [feed_one(i) for i in range(images)]
    came_two = [swap_col(f[9]) for f in fed]

    def feed_grad(lefts, rights):
        each = out_rows_each
        outs = [shaped((rows, each * blocks_up, width), LOW) for _ in range(n)]
        return run_kernel(
            functools.partial(feed_grad_kernel, (n, rows, width)),
            (*lefts, *rights),
            outs,
            grid=(blocks_up,),
            in_specs=[pl.BlockSpec((PAD, block_units), lambda u: (0, u)) for _ in lefts] + [whole(r) for r in rights],
            out_specs=[pl.BlockSpec((rows, each, width), lambda u: (0, u, 0)) for _ in range(n)],
            flops=10**10,
        )

    def split_sources(blocks, lead):
        if n == parts:
            return blocks
        split = blocks[0].reshape(rows, lead, parts, -1, width).transpose(2, 0, 1, 3, 4)
        split = xor_order(split.reshape(parts, rows, -1, width), 0)
        return [split[d] for d in range(parts)]

    down_grad = feed_grad([f[3] for f in fed], [f[2] for f in fed])
    up_grad = feed_grad([f[4] for f in fed], [f[1] for f in fed])

    def reduce_all(blocks):
        held = scatter_dp(blocks, LOW)
        return scatter_row([held[k] for k in range(rows)])

    feed_down = reduce_all(split_sources(down_grad, blocks_up))
    feed_up = reduce_all(split_sources(up_grad, blocks_up))

    def from_images(strips):
        came = [strips[0]] + [turn(strips[k], -k) for k in range(1, rows)]
        stacked = jnp.stack(came)[:, :, :SEQ]
        order = (jnp.arange(rows) - row_index) % rows
        return stacked[order].reshape(-1, strip).astype(WIDE)

    top = jnp.stack([f[7] + swap_col(f[8]).astype(WIDE) for f in fed], axis=1).astype(LOW)
    result = from_images(top)

    def backward_one(i):
        outs = [
            shaped((PAD, model), WIDE),
            shaped((PAD, model), LOW),
            shaped((PAD, 3 * span), LOW),
            shaped((PAD, model), LOW),
            shaped((8, model), WIDE),
            shaped((1, 3 * span), WIDE),
        ]
        acts = (vec, fed[i][0], fed[i][9], came_two[i], fed[i][2], done[i][3])
        return run_kernel(
            functools.partial(second_kernel, (n, rows, heads, width)),
            (pos, *acts, *first_all, *second_all),
            outs,
            scratch=[
                pltpu.VMEM((rows, 3 * span, width), LOW), pltpu.VMEM((rows, span, width), LOW), pltpu.VMEM((PAD, span), LOW),
            ],
            in_specs=[
                scalars, *[whole(a) for a in acts], *source_specs(first_all, first_rows), *source_specs(second_all, out_rows_each),
            ],
            flops=10**10,
        )

    returned = [backward_one(i) for i in range(images)]
    came_three = [swap_col(r[3]) for r in returned]
    attn_grad = run_kernel(
        functools.partial(attn_grad_kernel, (n, rows, heads, width)),
        (
            pos, *[r[2] for r in returned], *[d[2] for d in done], *[d[4] for d in done], *[r[1] for r in returned],
        ),
        [shaped((rows, (qkv_count + out_count) * parts // n, width), LOW) for _ in range(n)],
        scratch=[pltpu.VMEM((span, model), LOW)],
        flops=10**10,
    )
    attn = reduce_all(split_sources(attn_grad, 4 * heads))
    grad_strips, sums_one = run_kernel(
        functools.partial(last_kernel, (rows, width, images)),
        (
            pos, vec, *[d[1] for d in done], *[r[3] for r in returned], *came_three, *[r[0] for r in returned],
        ),
        [shaped((rows, images, PAD, strip), LOW), shaped((8, model), WIDE)],
        flops=10**9,
    )
    grad_tokens = from_images(grad_strips)

    sums_two = sum(r[4] for r in returned)
    dy_sum = sum(f[6] for f in fed)
    vector_sum = jnp.concatenate([sums_one[0:2], sums_two[0:3], dy_sum])
    packed_sum = sum(r[5] for r in returned).reshape(3, heads, parts, chunk)
    packed_sum = xor_order(jnp.stack([packed_sum[0], packed_sum[2]]).transpose(2, 0, 1, 3), 0).reshape(parts, -1)
    unit_sum = sum(f[5] for f in fed).reshape(blocks_up, parts, -1).transpose(1, 0, 2)
    if n == 1:
        unit_sum = xor_order(unit_sum, 0)
    unit_sum = unit_sum.reshape(parts, -1)
    vector_split = vector_sum.reshape(6, rows, 2, 2, parts, chunk)
    vector_split = jnp.where(low_col, vector_split[:, :, 0], vector_split[:, :, 1])
    vector_split = xor_order(vector_split.transpose(3, 1, 0, 2, 4), 0)
    vector_split = vector_split[:, (row_index - jnp.arange(rows)) % rows]
    tiny = jnp.concatenate([packed_sum, unit_sum, vector_split.reshape(parts, -1)], axis=1)
    tiny = scatter_dp([tiny[d] for d in range(parts)], WIDE)
    tiny = lax.psum(tiny, "row")
    size_packed, size_unit = packed_sum.shape[1], unit_sum.shape[1]
    tiny_vec = tiny[size_packed + size_unit :].reshape(rows, 6, 2, chunk)
    tiny_vec = lax.dynamic_index_in_dim(tiny_vec, row_index, 0, False)

    attn_qkv, attn_out = attn[:qkv_count], attn[qkv_count:]
    summed = (
        attn_qkv.reshape(3, heads, chunk, width).transpose(3, 0, 1, 2),
        tiny[:size_packed].reshape(b_qkv.shape),
        attn_out.reshape(w_out.shape),
        feed_up.reshape(groups, chunk, width).transpose(2, 0, 1),
        tiny[size_packed : size_packed + size_unit].reshape(b_up.shape),
        feed_down.reshape(w_down.shape),
        tiny_vec,
    )
    grad_scale = grad_gain / math.sqrt(tokens.shape[0] * parts)
    old_params = (w_qkv, b_qkv, w_out, w_up, b_up, w_down, vectors)
    states = (state_qkv, state_qkv_bias, state_out, state_up, state_up_bias, state_down, state_vectors)
    decays = (weight_decay, 0.0, weight_decay, weight_decay, 0.0, weight_decay, 0.0)
    scaled, updated, fresh = [], [], []
    for number in range(7):
        gradient = summed[number] * grad_scale
        change, moments = adam_step(old_params[number].astype(WIDE), gradient, states[number], decays[number])
        scaled.append(gradient)
        updated.append(change)
        fresh.append(moments)
    return (result, grad_tokens, *scaled, *updated, *fresh)


def solution(mesh):
    placed = (
        P("dp", ("row", "col")),
        P("dp", ("row", "col")),
        P("row", None, "col", "dp"),
        P(None, "col", "dp"),
        P("col", "dp", "row"),
        P("row", "col", "dp"),
        P("col", "dp"),
        P("col", "dp", "row"),
        P(None, ("row", "col"), "dp"),
        P(None, "row", None, "col", "dp"),
        P(None, None, "col", "dp"),
        P(None, "col", "dp", "row"),
        P(None, "row", "col", "dp"),
        P(None, "col", "dp"),
        P(None, "col", "dp", "row"),
        P(None, None, ("row", "col"), "dp"),
    )
    params = placed[2:9]
    return jax.shard_map(
        on_device,
        mesh=mesh,
        in_specs=placed,
        out_specs=(placed[0], placed[0], *params, *params, *placed[9:]),
        check_vma=False,
    )
```

```python
import functools
import math

import jax
import jax.numpy as jnp
from jax import lax
from jax.experimental import pallas as pl
from jax.experimental.pallas import tpu as pltpu
from jax.sharding import PartitionSpec as P

HD = 64
SEQ = 197
PAD = 208
STEP = 10

norm_eps = 1e-06
beta_first = 0.9
beta_second = 0.999
learn_rate = 0.01
weight_decay = 0.05
adam_eps = 1e-08
grad_gain = 32.0

LOW = jnp.bfloat16
WIDE = jnp.float32


def swap(values, name, bit):
    count = lax.axis_size(name)
    return lax.ppermute(values, name, [(i, i ^ bit) for i in range(count)])


def bits_of(name):
    bits, bit = [], 1
    while bit < lax.axis_size(name):
        bits.append(bit)
        bit *= 2
    return bits


def after(value, *others):
    return lax.optimization_barrier((value, *others))[0]


def fence(*values):
    return lax.optimization_barrier(values)


def planes(values):
    blocks = {0: values}
    for bit in reversed(bits_of("dp")[:-1]):
        for place in list(blocks):
            blocks[place ^ bit] = swap(blocks[place], "dp", bit)
    return [blocks[d] for d in range(len(blocks))]


def across(values):
    return swap(values, "dp", lax.axis_size("dp") // 2)


def along_row(values):
    blocks = {0: values}
    for bit in reversed(bits_of("row")):
        for place in list(blocks):
            blocks[place ^ bit] = swap(blocks[place], "row", bit)
    return [blocks[k] for k in range(1, len(blocks))]


def add_low(left, right):
    return (left.astype(WIDE) + right.astype(WIDE)).astype(left.dtype)


def join(held, name, bit):
    return {d: add_low(held[d], swap(held[d ^ bit], name, bit)) for d in held if not d & bit}


def scatter(blocks, name):
    held = dict(enumerate(blocks))
    for bit in bits_of(name):
        held = join(held, name, bit)
    return held[0]


def xor_order(values, axis, name):
    mine = lax.axis_index(name)
    shape = values.shape
    for bit in bits_of(name):
        split = values.reshape(shape[:axis] + (shape[axis] // (2 * bit), 2, bit) + shape[axis + 1 :])
        flipped = jnp.flip(split, axis + 1)
        values = jnp.where((mine & bit) > 0, flipped, split).reshape(shape)
    return values


def adam_step(weight_old, gradient, first_old, second_old, decay_on):
    first_moment = beta_first * first_old + (1.0 - beta_first) * gradient
    second_moment = beta_second * second_old + (1.0 - beta_second) * gradient * gradient
    first_hat = first_moment / (1.0 - beta_first**STEP)
    second_hat = second_moment / (1.0 - beta_second**STEP)
    change = -learn_rate * (first_hat / (jnp.sqrt(second_hat) + adam_eps) + decay_on * weight_old)
    return change, first_moment, second_moment


def adam_kernel(spec, first, *refs):
    count, sizes, grad_scale = spec
    pieces, refs = refs[:count], refs[count:]
    weights, states, outs = refs[: len(sizes)], refs[len(sizes) : 2 * len(sizes)], refs[2 * len(sizes) :]
    at = 0
    for i, size in enumerate(sizes):
        lines = slice(at, at + size)
        at += size
        total = first[lines].astype(WIDE)
        for piece in pieces:
            total = total + piece[lines].astype(WIDE)
        gradient = total * grad_scale
        change, low_moment, high_moment = adam_step(
            weights[i][...].astype(WIDE), gradient, states[i][0], states[i][1], weight_decay
        )
        outs[3 * i][...] = gradient
        outs[3 * i + 1][...] = change
        outs[3 * i + 2][0] = low_moment
        outs[3 * i + 2][1] = high_moment


def collect_kernel(spec, pos, ones, *refs):
    rows, heads, chunk, parts, width, images, split, places = spec
    twos, dys, packs, refs = refs[:images], refs[images : 2 * images], refs[2 * images : 3 * images], refs[3 * images :]
    units, out, = refs[:-1], refs[-1]
    low_col, me, row = pos[0] == 0, pos[1], pos[2]
    out[...] = jnp.zeros_like(out)
    add = lambda items: functools.reduce(lambda a, b: a + b, items)
    two = add([t[0:3, :] for t in twos])
    lines = [ones[0:1, :], ones[1:2, :], two[0:1], two[1:2], two[2:3], add([d[...] for d in dys])]
    pack = add([p[...] for p in packs])
    span = heads * HD
    half = width // 2
    turns = [add([u[...] for u in units[i : i + images]]) for i in range(0, len(units), images)]
    def put(d, line, pieces):
        value = jnp.concatenate(pieces, axis=1)
        short = out.shape[2] - value.shape[1]
        if short:
            value = jnp.concatenate([value, jnp.zeros((1, short), WIDE)], axis=1)
        out[pl.ds(d, 1), pl.ds(line, 1), :] = value[None]

    for owner in range(parts):
        d = me ^ owner
        spots = [part * span + h * HD + owner * chunk for part in (0, 2) for h in range(heads)]
        put(d, 0, [pack[:, at : at + chunk] for at in spots])
        put(owner if split else d, 1, [turns[turn][:, at : at + size] for turn, at, size in places[owner]])
        for k in range(rows):
            pieces = []
            for v in range(6):
                for j in range(2):
                    at = k * width + j * HD + owner * chunk
                    near, far = lines[v][:, at : at + chunk], lines[v][:, at + half : at + half + chunk]
                    pieces.append(jnp.where(low_col, near, far))
            put(d, 4 + (row ^ k), pieces)


def small_adam_kernel(spec, pos, tiny, *refs):
    heads, groups, chunk, grad_scale = spec
    row = pos[0]
    weights, states, grads, changes, fresh = (refs[3 * i : 3 * i + 3] for i in range(5))
    for part in range(2):
        for h in range(heads):
            at = (part * heads + h) * chunk
            grads[0][part, h : h + 1, :] = tiny[0:1, at : at + chunk] * grad_scale
    side = lax.broadcasted_iota(jnp.int32, (groups, chunk), 0)
    table = jnp.zeros((groups, chunk), WIDE)
    for g in range(groups):
        table = jnp.where(side == g, tiny[1:2, g * chunk : (g + 1) * chunk], table)
    grads[1][...] = table.T * grad_scale
    mine = tiny[pl.ds(4 + row, 1), :] * grad_scale
    for v in range(6):
        for j in range(2):
            at = (v * 2 + j) * chunk
            grads[2][v, j : j + 1, :] = mine[:, at : at + chunk]
    for i in range(3):
        change, low_moment, high_moment = adam_step(weights[i][...].astype(WIDE), grads[i][...], states[i][0], states[i][1], 0.0)
        changes[i][...] = change
        fresh[i][0] = low_moment
        fresh[i][1] = high_moment


def dot_nt(left, right):
    return lax.dot_general(left, right, (((1,), (1,)), ((), ())), preferred_element_type=WIDE)


def dot_nn(left, right):
    return lax.dot_general(left, right, (((1,), (0,)), ((), ())), preferred_element_type=WIDE)


def dot_tn(left, right):
    return lax.dot_general(left, right, (((0,), (0,)), ((), ())), preferred_element_type=WIDE)


def moments_of(stream):
    center = jnp.mean(stream, axis=-1, keepdims=True)
    offset = stream - center
    inv_std = lax.rsqrt(jnp.mean(offset * offset, axis=-1, keepdims=True) + norm_eps)
    return offset * inv_std, inv_std


def norm_backward(grad_norm, scaled, inv_std, gain):
    weighted = grad_norm * gain
    return inv_std * (
        weighted
        - jnp.mean(weighted, axis=-1, keepdims=True)
        - scaled * jnp.mean(weighted * scaled, axis=-1, keepdims=True)
    )


def lay_strips(low_col, near, far, rows):
    pieces = []
    for k in range(rows):
        mine, other = near(k), far(k)
        pieces.append(jnp.where(low_col, mine, other))
        pieces.append(jnp.where(low_col, other, mine))
    return jnp.concatenate(pieces, axis=1)


def soft(scores):
    lane = lax.broadcasted_iota(jnp.int32, scores.shape, 1)
    scores = jnp.where(lane < SEQ, scores * (1.0 / math.sqrt(HD)), -1e30)
    raised = jnp.exp(scores - jnp.max(scores, axis=-1, keepdims=True))
    return raised * (1.0 / jnp.sum(raised, axis=-1, keepdims=True))


class Source:
    def __init__(self, own, rest, count):
        self.own, self.rest, self.count = own, rest, count

    def block(self, k, first, size):
        if k == 0:
            return self.own[first : first + size, :]
        at = (k - 1) * self.count + first
        return self.rest[at : at + size, :]


def lay_heads(target, sources, me, groups, rows):
    own = HD // len(sources)
    for k in range(rows):
        for d, source in enumerate(sources):
            place = me ^ d if len(sources) > 1 else 0
            for g in range(groups):
                at = g * HD + place * own
                if len(sources) > 1:
                    at = pl.multiple_of(at, own)
                target[k, pl.ds(at, own), :] = source.block(k, g * own, own)


def first_kernel(spec, pos, near, far, *refs):
    n, rows, heads, width = spec
    count = 4 * heads * HD // n
    sources = [Source(refs[d], refs[n + d], count) for d in range(n)]
    vec_o, x_o, normed_o, packed_o, att_o, part_o, qkv_s = refs[2 * n :]
    low_col, me = pos[0] == 0, pos[1]
    base = (rows - 1) * count
    small = refs[n][base:, :].astype(WIDE)
    for d in range(1, n):
        small = small + refs[n + d][base:, :].astype(WIDE)
    each = small.shape[0] // rows
    vec = jnp.concatenate([small[k * each : k * each + 6] for k in range(rows)], axis=1)
    vec_o[0:6, :] = vec
    lay_heads(qkv_s, sources, me, 4 * heads, rows)
    stream = lay_strips(low_col, lambda k: near[k, 0], lambda k: far[k, 0], rows)
    x_o[...] = stream
    scaled, _ = moments_of(stream.astype(WIDE))
    normed = (scaled * vec[0:1] + vec[1:2]).astype(LOW)
    normed_o[...] = normed
    span = heads * HD
    lines = span // width
    for part in range(3):
        total = dot_nt(normed[:, :width], qkv_s[0, part * span : (part + 1) * span, :])
        for k in range(1, rows):
            total = total + dot_nt(normed[:, k * width : (k + 1) * width], qkv_s[k, part * span : (part + 1) * span, :])
        if part != 1:
            line = 6 + (lines if part == 2 else 0)
            total = total + jnp.concatenate([small[line + i : line + i + 1] for i in range(lines)], axis=1)
        packed_o[:, part * span : (part + 1) * span] = total.astype(LOW)
    two = 2 * HD
    lane = lax.broadcasted_iota(jnp.int32, (1, two), 1)
    for pair in range(heads // 2):
        at = pair * two
        queries = packed_o[:, at : at + two]
        key_rows = packed_o[:, span + at : span + at + two]
        values = packed_o[:, 2 * span + at : 2 * span + at + two]
        halves = []
        for side in range(2):
            mask = (lane < HD) if side == 0 else (lane >= HD)
            probs = soft(dot_nt(jnp.where(mask, queries, jnp.zeros_like(queries)), key_rows))
            halves.append(dot_nn(probs.astype(LOW), values))
        att_o[:, at : at + two] = jnp.where(lane < HD, halves[0], halves[1]).astype(LOW)
    for k in range(rows):
        part_o[:, k * width : (k + 1) * width] = dot_nn(att_o[...], qkv_s[k, 3 * span :, :]).astype(LOW)


def feed_kernel(spec, pos, vec, small, *refs):
    m, rows, width, opens, closes = spec
    acts = 5 if opens else 5
    given, refs = refs[:acts], refs[acts:]
    up = [refs[d * rows : (d + 1) * rows] for d in range(m)]
    down = [refs[(m + d) * rows : (m + d + 1) * rows] for d in range(m)]
    refs = refs[2 * m * rows :]
    units_o, hid_o, unit_sum_o = refs[:3]
    refs = refs[3:]
    if opens:
        x, part, came, near, far = given
        mid, normed, dy, dy_sum_o = refs[:4]
        refs = refs[4:]
    else:
        mid, normed, dy, mixed_in, back_in = given
    low_col = pos[0] == 0
    step = pl.program_id(0)
    if closes:
        top_o, far_o, back_o, mixed_s, back_s = refs
    else:
        mixed_s, back_s = refs

    @pl.when(step == 0)
    def _():
        if opens:
            dy[...] = lay_strips(low_col, lambda k: near[k, 0], lambda k: far[k, 0], rows)
            dy_sum_o[...] = jnp.sum(dy[...].astype(WIDE), axis=0, keepdims=True)
            middle = x[...].astype(WIDE) + (part[...].astype(WIDE) + came[...].astype(WIDE) + vec[2:3, :])
            mid[...] = middle
            scaled, _ = moments_of(middle)
            normed[...] = (scaled * vec[3:4, :] + vec[4:5, :]).astype(LOW)
            mixed_s[...] = jnp.zeros_like(mixed_s)
            back_s[...] = jnp.zeros_like(back_s)
        else:
            mixed_s[...] = mixed_in[...]
            back_s[...] = back_in[...]

    def cols(ref, k):
        return ref[:, k * width : (k + 1) * width]

    up_rows = [jnp.concatenate([w[k][...] for w in up], axis=0) for k in range(rows)]
    down_rows = [jnp.concatenate([w[k][...] for w in down], axis=0) for k in range(rows)]
    hidden = dot_nt(cols(normed, 0), up_rows[0])
    for k in range(1, rows):
        hidden = hidden + dot_nt(cols(normed, k), up_rows[k])
    hidden = hidden + small[0]
    active, slope = gelu_both(hidden)
    active = active.astype(LOW)
    units_o[...] = active
    grad = dot_nt(cols(dy, 0), down_rows[0])
    for k in range(1, rows):
        grad = grad + dot_nt(cols(dy, k), down_rows[k])
    grad = (grad * slope).astype(LOW)
    hid_o[...] = grad
    unit_sum_o[...] = jnp.sum(grad.astype(WIDE), axis=0, keepdims=True)
    for k in range(rows):
        at = slice(k * width, (k + 1) * width)
        mixed_s[:, at] += dot_nn(active, down_rows[k])
        back_s[:, at] += dot_nn(grad, up_rows[k])

    if closes:

        @pl.when(step == pl.num_programs(0) - 1)
        def _():
            back_o[...] = back_s[...].astype(LOW)
            half = width // 2
            for k in range(rows):
                left, right = slice(k * width, k * width + half), slice(k * width + half, (k + 1) * width)
                base = mid[...] + vec[5:6, :]
                top_l, top_r = mixed_s[:, left] + base[:, left], mixed_s[:, right] + base[:, right]
                top_o[k] = jnp.where(low_col, top_l, top_r)
                far_o[k] = jnp.where(low_col, mixed_s[:, right], mixed_s[:, left]).astype(LOW)


def feed_grad_kernel(spec, *refs):
    m, rows, width = spec
    left, right, outs = refs[0:2], refs[2:4], refs[4:]
    total = dot_tn(left[0][...], right[0][...]) + dot_tn(left[1][...], right[1][...])
    block = total.shape[0] // m
    for d in range(m):
        for k in range(rows):
            outs[d][k] = total[d * block : (d + 1) * block, k * width : (k + 1) * width].astype(LOW)


def second_kernel(spec, pos, vec, mid, back, came, dy, packed, *refs):
    n, rows, heads, width = spec
    count = 4 * heads * HD // n
    sources = [Source(refs[d], refs[n + d], count) for d in range(n)]
    dmid_o, dz_o, dpacked_o, back_o, sums_o, psum_o, qkv_s, datt_s = refs[2 * n :]
    me = pos[1]
    lay_heads(qkv_s, sources, me, 4 * heads, rows)
    span = heads * HD
    grad_norm = back[...].astype(WIDE) + came[...].astype(WIDE)
    scaled, inv_std = moments_of(mid[...])
    dmid = dy[...].astype(WIDE) + norm_backward(grad_norm, scaled, inv_std, vec[3:4, :])
    dmid_o[...] = dmid
    dz = dmid.astype(LOW)
    dz_o[...] = dz
    sums_o[0:1, :] = jnp.sum(dz.astype(WIDE), axis=0, keepdims=True)
    sums_o[1:2, :] = jnp.sum(grad_norm * scaled, axis=0, keepdims=True)
    sums_o[2:3, :] = jnp.sum(grad_norm, axis=0, keepdims=True)
    total = dot_nt(dz[:, :width], qkv_s[0, 3 * span :, :])
    for k in range(1, rows):
        total = total + dot_nt(dz[:, k * width : (k + 1) * width], qkv_s[k, 3 * span :, :])
    datt_s[...] = total.astype(LOW)
    two = 2 * HD
    scale = 1.0 / math.sqrt(HD)
    lane = lax.broadcasted_iota(jnp.int32, (1, two), 1)
    for pair in range(heads // 2):
        at = pair * two
        queries = packed[:, at : at + two]
        key_rows = packed[:, span + at : span + at + two]
        values = packed[:, 2 * span + at : 2 * span + at + two]
        grads = datt_s[:, at : at + two]
        dqs, dks, dvs = [], [], []
        for side in range(2):
            mask = (lane < HD) if side == 0 else (lane >= HD)
            probs = soft(dot_nt(jnp.where(mask, queries, jnp.zeros_like(queries)), key_rows))
            dprobs = dot_nt(jnp.where(mask, grads, jnp.zeros_like(grads)), values)
            dscores = probs * (dprobs - jnp.sum(dprobs * probs, axis=-1, keepdims=True))
            dscores = dscores.astype(LOW)
            dqs.append(dot_nn(dscores, key_rows))
            dks.append(dot_tn(dscores, queries))
            dvs.append(dot_tn(probs.astype(LOW), grads))
        first = lane < HD
        dpacked_o[:, at : at + two] = (jnp.where(first, dqs[0], dqs[1]) * scale).astype(LOW)
        dpacked_o[:, span + at : span + at + two] = (jnp.where(first, dks[0], dks[1]) * scale).astype(LOW)
        dpacked_o[:, 2 * span + at : 2 * span + at + two] = jnp.where(first, dvs[0], dvs[1]).astype(LOW)
    psum_o[...] = jnp.sum(dpacked_o[...].astype(WIDE), axis=0, keepdims=True)
    for k in range(rows):
        back_o[:, k * width : (k + 1) * width] = dot_nn(dpacked_o[...], qkv_s[k, : 3 * span, :]).astype(LOW)


def attn_grad_kernel(spec, pos, *refs):
    n, rows, heads, width = spec
    dpacked, normed, att, dz = refs[0:2], refs[2:4], refs[4:6], refs[6:8]
    outs, total_s = refs[8 : 8 + n], refs[8 + n]
    me = pos[1]
    span = heads * HD
    own = HD // n
    for part in range(4):
        if part < 3:
            at = slice(part * span, (part + 1) * span)
            total = dot_tn(dpacked[0][:, at], normed[0][...]) + dot_tn(dpacked[1][:, at], normed[1][...])
        else:
            total = dot_tn(att[0][...], dz[0][...]) + dot_tn(att[1][...], dz[1][...])
        total_s[...] = total.astype(LOW)
        for d in range(n):
            place = me ^ d if n > 1 else 0
            for g in range(heads):
                line = g * HD + place * own
                if n > 1:
                    line = pl.multiple_of(line, own)
                value = total_s[pl.ds(line, own), :]
                to = (part * heads + g) * own
                for k in range(rows):
                    outs[d][k, to : to + own, :] = value[:, k * width : (k + 1) * width]


def gelu_both(values):
    tail = 0.5 * (1.0 + lax.erf(values * (1.0 / math.sqrt(2.0))))
    bell = jnp.exp(values * values * -0.5) * (1.0 / math.sqrt(2.0 * math.pi))
    return values * tail, tail + values * bell


def last_kernel(spec, pos, vec, *refs):
    rows, width, images = spec
    x, back, came, dmid = (refs[i * images : (i + 1) * images] for i in range(4))
    out_o, sums_o = refs[4 * images :]
    low_col = pos[0] == 0
    half = width // 2
    for i in range(images):
        scaled, inv_std = moments_of(x[i][...].astype(WIDE))
        grad_norm = back[i][...].astype(WIDE) + came[i][...].astype(WIDE)
        value = dmid[i][...] + norm_backward(grad_norm, scaled, inv_std, vec[0:1, :])
        gain_sum = jnp.sum(grad_norm * scaled, axis=0, keepdims=True)
        shift_sum = jnp.sum(grad_norm, axis=0, keepdims=True)
        if i == 0:
            sums_o[0:1, :] = gain_sum
            sums_o[1:2, :] = shift_sum
        else:
            sums_o[0:1, :] += gain_sum
            sums_o[1:2, :] += shift_sum
        for k in range(rows):
            left, right = value[:, k * width : k * width + half], value[:, k * width + half : (k + 1) * width]
            out_o[k, i] = jnp.where(low_col, left, right).astype(LOW)


ROOM = 56 * 1024 * 1024


def whole(array):
    zeros = (0,) * len(array.shape)
    return pl.BlockSpec(tuple(array.shape), lambda *_: zeros)


def run_kernel(body, args, outs, scratch=(), grid=None, in_specs=None, out_specs=None):
    if in_specs is None:
        in_specs = [pl.BlockSpec(memory_space=pltpu.SMEM)] + [whole(a) for a in args[1:]]
    if out_specs is None:
        out_specs = [whole(o) for o in outs]
    return pl.pallas_call(
        body,
        grid=grid or (1,),
        in_specs=in_specs,
        out_specs=out_specs,
        out_shape=outs,
        scratch_shapes=list(scratch),
        compiler_params=pltpu.CompilerParams(vmem_limit_bytes=ROOM),
        cost_estimate=pl.CostEstimate(flops=1024, bytes_accessed=1024, transcendentals=0),
    )(*args)


def shaped(shape, kind):
    return jax.ShapeDtypeStruct(shape, kind)


def on_device(
    tokens, cotangent, w_qkv, b_qkv, w_out, w_up, b_up, w_down, vectors,
    state_qkv, state_qkv_bias, state_out, state_up, state_up_bias, state_down, state_vectors,
):
    parts, rows = lax.axis_size("dp"), lax.axis_size("row")
    col, row_index, me = lax.axis_index("col"), lax.axis_index("row"), lax.axis_index("dp")
    low_col = col == 0
    width = w_qkv.shape[0]
    heads, chunk = w_qkv.shape[2], w_qkv.shape[3]
    groups = w_up.shape[1]
    strip = tokens.shape[1]
    images = tokens.shape[0] // (SEQ * rows)
    model = rows * width
    span = heads * HD
    pos = jnp.stack([col, me]).astype(jnp.int32)

    qkv_own = w_qkv.transpose(1, 2, 3, 0).reshape(-1, width)
    out_own = w_out.reshape(-1, width)
    up_own = w_up.transpose(1, 2, 0).reshape(-1, width)
    down_own = w_down.reshape(-1, width)
    qkv_count, unit_count = qkv_own.shape[0], up_own.shape[0]
    head_own = jnp.concatenate([qkv_own, out_own])
    head_count = head_own.shape[0]

    at_me = (jnp.arange(parts) == me)[:, None]
    vec_own = jnp.where(at_me, vectors[:, :, None, :], 0).reshape(6, -1)
    vec_far = swap(vec_own, "col", 1)
    vec_pair = jnp.stack([jnp.where(low_col, vec_own, vec_far), jnp.where(low_col, vec_far, vec_own)])
    bias_own = jnp.where(at_me, b_qkv[:, :, None, :], 0).reshape(-1, width)
    unit_own = jnp.where(at_me, b_up.reshape(1, -1), 0).reshape(-1, width)
    small_count = 6 + bias_own.shape[0] + unit_own.shape[0]
    small_each = small_count + -small_count % 16

    def to_send(stream, extra):
        blocks = stream.astype(LOW).reshape(rows, images, SEQ, strip)
        blocks = jnp.pad(blocks, ((0, 0), (0, 0), (0, PAD - SEQ), (0, 0)))
        if extra is not None:
            extra = jnp.pad(extra, ((0, 0), (0, 2), (0, 0)))
            blocks = jnp.concatenate([blocks, jnp.broadcast_to(extra, (rows, *extra.shape))], axis=2)
        return [lax.dynamic_index_in_dim(blocks, row_index ^ k, 0, False) for k in range(rows)]

    def send_images(blocks):
        return [blocks[0]] + [swap(block, "row", k) for k, block in enumerate(blocks) if k]

    head_row = along_row(head_own)[:2] if rows == 4 else along_row(head_own)
    head_x = across(head_own)
    token_blocks = to_send(tokens, vec_pair)
    head_row, head_x, token_blocks, up_own1, down_own1 = fence(head_row, head_x, token_blocks, up_own, down_own)
    if rows == 4:
        head_row = [*head_row, swap(head_row[1], "row", 1)]
    came = send_images(token_blocks)
    up_x, down_x = across(up_own1), across(down_own1)
    head_owns = [*planes(head_own), *planes(head_x)]
    head_row, came, up_x, down_x, head_owns, up_own2, down_own2 = fence(
        head_row, came, up_x, down_x, head_owns, up_own, down_own
    )
    small_rows = [
        jnp.concatenate([
            block[0, PAD : PAD + 6], block[1, PAD : PAD + 6]], axis=1)
        for block in came
    ]
    small_rows = [
        jnp.concatenate([block, bias_own, unit_own, jnp.zeros((small_each - small_count, width), LOW)])
        for block in small_rows
    ]
    head_rest = jnp.concatenate([*head_row, after(jnp.concatenate(small_rows))])
    near = jnp.stack([block[:, :PAD] for block in came])
    far = swap(near, "col", 1)
    head_rest_x = across(head_rest)
    head_rest_planes = planes(head_rest)
    up_row = along_row(up_own2)
    head_rest_x, head_rest_planes, far, up_row, down_own3, dy_in = fence(
        head_rest_x, head_rest_planes, far, up_row, down_own2, cotangent
    )
    head_rests = [*head_rest_planes, *planes(head_rest_x)]
    up_rest = jnp.concatenate(up_row)
    up_rest_x = across(up_rest)
    down_row = along_row(down_own3)
    dy_came = send_images(to_send(dy_in, None))

    split = chunk % 16 == 0
    n = parts if split else 1
    if not split:
        def merge(blocks, lead):
            both = xor_order(jnp.stack(blocks), 0, "dp").reshape(parts, -1, lead, blocks[0].shape[0] // lead, width)[:, 0]
            return both.transpose(1, 0, 2, 3).reshape(-1, width)

        def merge_rest(blocks, count, lead):
            return [merge([b[k * count : (k + 1) * count] for b in blocks], lead) for k in range(rows - 1)]

        small_sum = sum(b[(rows - 1) * head_count :].astype(WIDE) for b in head_rests).astype(LOW)
        head_rests = [jnp.concatenate([*merge_rest(head_rests, head_count, 4 * heads), small_sum])]
        head_owns = [merge(head_owns, 4 * heads)]
    scalars = pl.BlockSpec(memory_space=pltpu.SMEM)
    specs = functools.partial(functools.reduce, lambda a, b: a + [whole(b)])

    def forward_one(i):
        strips = pl.BlockSpec((rows, 1, PAD, strip), lambda *_: (0, i, 0, 0))
        outs = [
            shaped((8, model), WIDE),
            shaped((PAD, model), LOW),
            shaped((PAD, model), LOW),
            shaped((PAD, 3 * span), LOW),
            shaped((PAD, span), LOW),
            shaped((PAD, model), LOW),
        ]
        weights = (*head_owns, *head_rests)
        return run_kernel(
            functools.partial(first_kernel, (n, rows, heads, width)),
            (pos, near, far, *weights),
            outs,
            scratch=[pltpu.VMEM((rows, 4 * span, width), LOW)],
            in_specs=specs(weights, [scalars, strips, strips]),
            )

    done = [forward_one(i) for i in range(images)]
    vec = done[0][0]
    came_one = [swap(done[0][5], "col", 1)]
    (up_rest_x, down_row, dy_came, came_one, last_part, up_x, down_x, up_own4, down_own4) = fence(
        up_rest_x, down_row, dy_came, came_one, done[-1][5], up_x, down_x, up_own, down_own
    )
    near_dy = jnp.stack(dy_came)
    far_dy = swap(near_dy, "col", 1)
    came_one = [*came_one, swap(last_part, "col", 1)]
    down_rest = jnp.concatenate(down_row)
    down_rest_x = across(down_rest)
    up_owns, down_owns = planes(up_own4), planes(down_own4)
    up_rests, down_rests = planes(up_rest), planes(down_rest)
    up_owns_x, down_owns_x = planes(up_x), planes(down_x)
    up_rests_x = planes(up_rest_x)
    if not split:
        down_rests_x = planes(down_rest_x)
        both = lambda a, b: [merge([*a, *b], 1)]
        both_rest = lambda a, b: [jnp.concatenate(merge_rest([*a, *b], unit_count, 1))]
        up_owns, down_owns = both(up_owns, up_owns_x), both(down_owns, down_owns_x)
        up_rests, down_rests = both_rest(up_rests, up_rests_x), both_rest(down_rests, down_rests_x)

    first_small = (rows - 1) * head_count * parts // n
    unit_rows = sum(b[first_small + 6 + bias_own.shape[0] :][: unit_own.shape[0]].astype(WIDE) for b in head_rests)
    unit_rows = unit_rows.reshape(parts, -1)
    if split:
        unit_rows = xor_order(unit_rows, 0, "dp")
    unit_rows = unit_rows.reshape(n, -1)
    plane = unit_count * parts // n
    block = min(plane, 256)
    steps = plane // block

    turns = [(0, n)] if not split else [(0, n // 2), (n // 2, n)]

    def feed_one(i, turn, before):
        low, high = turns[turn]
        m = high - low
        opens, closes = turn == 0, turn == len(turns) - 1
        wide_block = m * block
        small = unit_rows[low:high].reshape(m, steps, block).transpose(1, 0, 2).reshape(steps, 1, wide_block)
        strips = pl.BlockSpec((rows, 1, PAD, strip), lambda *_: (0, i, 0, 0))
        full, low_full = shaped((PAD, model), WIDE), shaped((PAD, model), LOW)
        by_block = lambda lead: pl.BlockSpec((lead, wide_block), lambda u: (0, u))
        outs = [shaped((PAD, m * plane), LOW), shaped((PAD, m * plane), LOW), shaped((1, m * plane), WIDE)]
        out_specs = [by_block(PAD), by_block(PAD), by_block(1)]
        if opens:
            given = (done[i][1], done[i][5], came_one[i], near_dy, far_dy)
            given_specs = [whole(g) for g in given[:3]] + [strips, strips]
            outs += [full, low_full, low_full, shaped((1, model), WIDE)]
        else:
            given = (before[3], before[4], before[5], before[-2], before[-1])
            given_specs = [whole(g) for g in given]
        scratch = []
        if closes:
            outs += [shaped((rows, PAD, strip), WIDE), shaped((rows, PAD, strip), LOW), low_full]
            scratch = [pltpu.VMEM((PAD, model), WIDE), pltpu.VMEM((PAD, model), WIDE)]
        else:
            outs += [full, full]
        out_specs += [whole(o) for o in outs[3:]]
        weights, weight_specs = [], []
        for owns, rests in ((up_owns, up_rests), (down_owns, down_rests)):
            for d in range(low, high):
                for k in range(rows):
                    weights.append(owns[d] if k == 0 else rests[d])
                    first = max(k - 1, 0) * steps
                    weight_specs.append(pl.BlockSpec((block, width), lambda u, first=first: (u + first, 0)))
        return run_kernel(
            functools.partial(feed_kernel, (m, rows, width, opens, closes)),
            (pos, vec, small, *given, *weights),
            outs,
            scratch=scratch,
            grid=(steps,),
            in_specs=[
                scalars, whole(vec), pl.BlockSpec((1, 1, wide_block), lambda u: (u, 0, 0)), *given_specs, *weight_specs,
            ],
            out_specs=out_specs,
            )

    def feed_grad(lefts, rights, turn, *waits):
        low, high = turns[turn]
        m = high - low
        outs = [shaped((rows, plane, width), LOW) for _ in range(m)]
        lefts = [after(lefts[0], *waits), *lefts[1:]]
        return run_kernel(
            functools.partial(feed_grad_kernel, (m, rows, width)),
            (*lefts, *rights),
            outs,
            grid=(steps,),
            in_specs=[pl.BlockSpec((PAD, m * block), lambda u: (0, u)) for _ in lefts] + [whole(r) for r in rights],
            out_specs=[pl.BlockSpec((rows, block, width), lambda u: (0, u, 0)) for _ in range(m)],
            )

    fed = [[feed_one(i, 0, None) for i in range(images)]]
    dys, normed_two = [f[5] for f in fed[0]], [f[4] for f in fed[0]]
    if split:
        fed, down_rest_x, up_rests_x, up_owns_x, down_owns_x = fence(fed, down_rest_x, up_rests_x, up_owns_x, down_owns_x)
        dys, normed_two = [f[5] for f in fed[0]], [f[4] for f in fed[0]]
        up_owns, down_owns = [*up_owns, *up_owns_x], [*down_owns, *down_owns_x]
        up_rests, down_rests = [*up_rests, *up_rests_x], [*down_rests, *planes(down_rest_x)]
    down_grads = feed_grad([f[0] for f in fed[0]], dys, 0)
    up_grads = feed_grad([f[1] for f in fed[0]], normed_two, 0)
    if split:
        down_grads, up_grads, down_rests = fence(down_grads, up_grads, down_rests)
        fed.append([feed_one(0, 1, fed[0][0])])
        came_two = [swap(fed[1][0][-1], "col", 1)]
        fed[1].append(feed_one(1, 1, fed[0][1]))
        fed, came_two, down_grads, up_grads = fence(fed, came_two, down_grads, up_grads)
        dys, normed_two = [f[5] for f in fed[0]], [f[4] for f in fed[0]]
        came_two = [*came_two, swap(fed[1][1][-1], "col", 1)]
        down_grads = [*down_grads, *feed_grad([f[0] for f in fed[1]], dys, 1)]
        up_grads = [*up_grads, *feed_grad([f[1] for f in fed[1]], normed_two, 1)]
    else:
        came_two = [swap(f[-1], "col", 1) for f in fed[0]]
    closing = fed[-1]

    def split_sources(blocks, lead):
        if n == parts:
            return blocks
        both = blocks[0].reshape(rows, lead, parts, -1, width).transpose(2, 0, 1, 3, 4)
        both = xor_order(both.reshape(parts, rows, -1, width), 0, "dp")
        return [both[d] for d in range(parts)]

    def split_units(blocks):
        if n == parts:
            return blocks
        both = xor_order(blocks[0].reshape(rows, parts, -1, width).transpose(1, 0, 2, 3), 0, "dp")
        return [both[d] for d in range(parts)]

    def start_reduce(blocks):
        held = dict(enumerate(blocks))
        for bit in bits_of("dp")[:-1]:
            held = join(held, "dp", bit)
        return held

    half_rows = rows // 2

    def send_high(held):
        return across(held[parts // 2][half_rows:])

    def send_low(held):
        return across(held[parts // 2][:half_rows])

    def add_half(held, came, high):
        lines = held[0][half_rows:] if high else held[0][:half_rows]
        return [add_low(lines[k], came[k]) for k in range(half_rows)]

    down_held = start_reduce(split_units(down_grads))
    up_held = start_reduce(split_units(up_grads))

    def from_images(strips):
        came = [strips[0]] + [swap(strips[k], "row", k) for k in range(1, rows)]
        stacked = xor_order(jnp.stack(came)[:, :, :SEQ], 0, "row")
        return stacked.reshape(-1, strip).astype(WIDE)

    def backward_one(i):
        outs = [
            shaped((PAD, model), WIDE),
            shaped((PAD, model), LOW),
            shaped((PAD, 3 * span), LOW),
            shaped((PAD, model), LOW),
            shaped((8, model), WIDE),
            shaped((1, 3 * span), WIDE),
        ]
        acts = (vec, fed[0][i][3], closing[i][-1], came_two[i], dys[i], done[i][3], *head_owns, *head_rests)
        return run_kernel(
            functools.partial(second_kernel, (n, rows, heads, width)),
            (pos, *acts),
            outs,
            scratch=[pltpu.VMEM((rows, 4 * span, width), LOW), pltpu.VMEM((PAD, span), LOW)],
            )

    assert rows == 4
    down_held, up_grads = fence(down_held, up_grads)
    down_high = send_high(down_held)
    returned = [backward_one(0)]
    down_high, returned, down_held, up_held, came_two = fence(down_high, returned, down_held, up_held, came_two)

    down_low = send_low(down_held)
    down_two, down_three = add_half(down_held, down_high, True)
    down_three = swap(down_three, "row", 1)
    came_three = [swap(returned[0][3], "col", 1)]
    returned.append(backward_one(1))
    down_low, down_two, down_three, came_three, returned, up_held, vec = fence(
        down_low, down_two, down_three, came_three, returned, up_held, vec
    )

    up_high = send_high(up_held)
    down_zero, down_one = add_half(down_held, down_low, False)
    down_one = swap(down_one, "row", 1)
    down_two = swap(add_low(down_two, down_three), "row", 2)
    came_three = [*came_three, swap(returned[1][3], "col", 1)]
    attn_grad = run_kernel(
        functools.partial(attn_grad_kernel, (n, rows, heads, width)),
        (
            pos, *[r[2] for r in returned], *[d[2] for d in done], *[d[4] for d in done], *[r[1] for r in returned],
        ),
        [shaped((rows, head_count * parts // n, width), LOW) for _ in range(n)],
        scratch=[pltpu.VMEM((span, model), LOW)],
    )
    attn_held = start_reduce(split_sources(attn_grad, 4 * heads))
    up_high, down_one, down_two, came_three, attn_held, tops = fence(
        up_high, down_one, down_two, came_three, attn_held, [f[-2] for f in closing]
    )

    up_low = send_low(up_held)
    up_two, up_three = add_half(up_held, up_high, True)
    up_three = swap(up_three, "row", 1)
    top_far = [swap(t, "col", 1) for t in tops]
    grad_strips, sums_one = run_kernel(
        functools.partial(last_kernel, (rows, width, images)),
        (
            pos, vec, *[d[1] for d in done], *[r[3] for r in returned], *came_three, *[r[0] for r in returned],
        ),
        [shaped((rows, images, PAD, strip), LOW), shaped((8, model), WIDE)],
    )
    up_low, up_two, up_three, top_far, grad_strips, sums_one, attn_held = fence(
        up_low, up_two, up_three, top_far, grad_strips, sums_one, attn_held
    )

    attn_high = send_high(attn_held)
    up_zero, up_one = add_half(up_held, up_low, False)
    up_one = swap(up_one, "row", 1)
    up_two = swap(add_low(up_two, up_three), "row", 2)
    top = jnp.stack([f[3 if len(turns) > 1 else 7] + t.astype(WIDE) for f, t in zip(closing, top_far)], axis=1).astype(LOW)
    attn_high, up_one, up_two, grad_strips, top, down_zero = fence(attn_high, up_one, up_two, grad_strips, top, down_zero)

    attn_low = send_low(attn_held)
    attn_two, attn_three = add_half(attn_held, attn_high, True)
    attn_three = swap(attn_three, "row", 1)
    result = from_images(top)
    attn_low, attn_two, attn_three, result, up_zero, grad_strips = fence(
        attn_low, attn_two, attn_three, result, up_zero, grad_strips
    )

    attn_zero, attn_one = add_half(attn_held, attn_low, False)
    attn_one = swap(attn_one, "row", 1)
    attn_two = swap(add_low(attn_two, attn_three), "row", 2)
    grad_tokens = from_images(grad_strips)
    feed_down = (down_zero, [down_one, down_two])
    feed_up = (up_zero, [up_one, up_two])
    attn = (attn_zero, [attn_one, attn_two])
    grad_scale = grad_gain / math.sqrt(tokens.shape[0] * parts)

    unit_lanes = unit_count // width * width
    places = []
    for d in range(parts):
        if split:
            turn = 0 if d < n // 2 else 1
            low, high = turns[turn]
            places.append([(turn, (u * (high - low) + d - low) * block, block) for u in range(steps)])
        else:
            places.append([(0, d * unit_count, unit_count)])
    unit_inputs = [f[2] for group in fed for f in group]
    lanes = max(unit_count, 2 * heads * chunk, 12 * chunk)
    tiny = run_kernel(
        functools.partial(collect_kernel, (rows, heads, chunk, parts, width, images, split, places)),
        (
            jnp.stack([col, me, row_index]).astype(jnp.int32), sums_one, *[r[4] for r in returned],
            *[f[6] for f in fed[0]], *[r[5] for r in returned], *unit_inputs,
        ),
        [shaped((parts, 8, lanes), WIDE)],
    )[0]
    tiny = scatter([tiny[d] for d in range(parts)], "dp")
    for bit in bits_of("row"):
        tiny = tiny + swap(tiny, "row", bit)
    flat_up = lambda a: jnp.swapaxes(a, -1, -2)
    small_args = (b_qkv, flat_up(b_up), vectors, state_qkv_bias, flat_up(state_up_bias), state_vectors)
    small_kinds = (b_qkv.shape, flat_up(b_up).shape, vectors.shape)
    small_done = run_kernel(
        functools.partial(small_adam_kernel, (heads, groups, chunk, grad_scale)),
        (jnp.stack([row_index, row_index]).astype(jnp.int32), tiny, *small_args),
        [shaped(k, WIDE) for k in (*small_kinds, *small_kinds)] + [shaped((2, *k), WIDE) for k in small_kinds],
    )

    def adam(reduced, owns, states, ranges):
        first, pieces = reduced
        outs = []
        for size, _ in ranges:
            outs += [shaped((size, width), WIDE), shaped((size, width), WIDE), shaped((2, size, width), WIDE)]
        args = (first, *pieces, *owns, *states)
        return run_kernel(
            functools.partial(adam_kernel, (len(pieces), [r[0] for r in ranges], grad_scale)),
            args,
            outs,
            in_specs=[whole(a) for a in args],
        )

    state_rows = lambda a, order: a.transpose(order).reshape(2, -1, width)
    out_count = out_own.shape[0]
    down_done = adam(feed_down, [down_own], [state_rows(state_down, (0, 1, 2, 3))], [(unit_count, 0)])
    up_done = adam(feed_up, [up_own], [state_rows(state_up, (0, 2, 3, 1))], [(unit_count, 0)])
    attn_done = adam(
        attn,
        [qkv_own, out_own],
        [state_rows(state_qkv, (0, 2, 3, 4, 1)), state_rows(state_out, (0, 1, 2, 3))],
        [(qkv_count, 0), (out_count, 0)],
    )

    def shape_all(which):
        lead = (2,) if which == 2 else ()
        more = (0,) if which == 2 else ()
        move = lambda order: (*more, *[o + len(lead) for o in order])
        return (
            attn_done[which].reshape(*lead, 3, heads, chunk, width).transpose(move((3, 0, 1, 2))),
            small_done[3 * which],
            attn_done[3 + which].reshape(*lead, *w_out.shape),
            up_done[which].reshape(*lead, groups, chunk, width).transpose(move((2, 0, 1))),
            flat_up(small_done[3 * which + 1]),
            down_done[which].reshape(*lead, *w_down.shape),
            small_done[3 * which + 2],
        )

    return (result, grad_tokens, *shape_all(0), *shape_all(1), *shape_all(2))


def solution(mesh):
    placed = (
        P("dp", ("row", "col")),
        P("dp", ("row", "col")),
        P("row", None, "col", "dp"),
        P(None, "col", "dp"),
        P("col", "dp", "row"),
        P("row", "col", "dp"),
        P("col", "dp"),
        P("col", "dp", "row"),
        P(None, ("row", "col"), "dp"),
        P(None, "row", None, "col", "dp"),
        P(None, None, "col", "dp"),
        P(None, "col", "dp", "row"),
        P(None, "row", "col", "dp"),
        P(None, "col", "dp"),
        P(None, "col", "dp", "row"),
        P(None, None, ("row", "col"), "dp"),
    )
    params = placed[2:9]
    return jax.shard_map(
        on_device,
        mesh=mesh,
        in_specs=placed,
        out_specs=(placed[0], placed[0], *params, *params, *placed[9:]),
        check_vma=False,
    )
```

```python
import functools
import math

import jax
import jax.numpy as jnp
from jax import lax
from jax.experimental import pallas as pl
from jax.experimental.pallas import tpu as pltpu
from jax.sharding import PartitionSpec as P

HD = 64
SEQ = 197
PAD = 208
STEP = 10

norm_eps = 1e-06
beta_first = 0.9
beta_second = 0.999
learn_rate = 0.01
weight_decay = 0.05
adam_eps = 1e-08
grad_gain = 32.0

LOW = jnp.bfloat16
WIDE = jnp.float32


def swap(values, name, bit):
    count = lax.axis_size(name)
    return lax.ppermute(values, name, [(i, i ^ bit) for i in range(count)])


def bits_of(name):
    bits, bit = [], 1
    while bit < lax.axis_size(name):
        bits.append(bit)
        bit *= 2
    return bits


def after(value, *others):
    return lax.optimization_barrier((value, *others))[0]


def planes(values):
    blocks = {0: values}
    for bit in reversed(bits_of("dp")[:-1]):
        for place in list(blocks):
            blocks[place ^ bit] = swap(blocks[place], "dp", bit)
    return [blocks[d] for d in range(len(blocks))]


def across(values):
    return swap(values, "dp", lax.axis_size("dp") // 2)


def add_low(left, right):
    return (left.astype(WIDE) + right.astype(WIDE)).astype(left.dtype)


def join(held, name, bit):
    return {d: add_low(held[d], swap(held[d ^ bit], name, bit)) for d in held if not d & bit}


def scatter(blocks, name):
    held = dict(enumerate(blocks))
    for bit in bits_of(name):
        held = join(held, name, bit)
    return held[0]


def xor_order(values, axis, name):
    mine = lax.axis_index(name)
    shape = values.shape
    for bit in bits_of(name):
        split = values.reshape(shape[:axis] + (shape[axis] // (2 * bit), 2, bit) + shape[axis + 1 :])
        flipped = jnp.flip(split, axis + 1)
        values = jnp.where((mine & bit) > 0, flipped, split).reshape(shape)
    return values


def adam_step(weight_old, gradient, first_old, second_old, decay_on):
    first_moment = beta_first * first_old + (1.0 - beta_first) * gradient
    second_moment = beta_second * second_old + (1.0 - beta_second) * gradient * gradient
    first_hat = first_moment / (1.0 - beta_first**STEP)
    second_hat = second_moment / (1.0 - beta_second**STEP)
    change = -learn_rate * (first_hat / (jnp.sqrt(second_hat) + adam_eps) + decay_on * weight_old)
    return change, first_moment, second_moment


def adam_kernel(spec, first, *refs):
    count, sizes, grad_scale = spec
    pieces, refs = refs[:count], refs[count:]
    weights, states, outs = refs[: len(sizes)], refs[len(sizes) : 2 * len(sizes)], refs[2 * len(sizes) :]
    at = 0
    for i, size in enumerate(sizes):
        lines = slice(at, at + size)
        at += size
        total = first[lines].astype(WIDE)
        for piece in pieces:
            total = total + piece[lines].astype(WIDE)
        gradient = total * grad_scale
        change, low_moment, high_moment = adam_step(
            weights[i][...].astype(WIDE), gradient, states[i][0], states[i][1], weight_decay
        )
        outs[3 * i][...] = gradient
        outs[3 * i + 1][...] = change
        outs[3 * i + 2][0] = low_moment
        outs[3 * i + 2][1] = high_moment


def collect_kernel(spec, pos, ones, *refs):
    rows, heads, chunk, parts, width, images = spec
    twos, dys, packs, refs = refs[:images], refs[images : 2 * images], refs[2 * images : 3 * images], refs[3 * images :]
    units, out, = refs[:-1], refs[-1]
    low_col, me, row = pos[0] == 0, pos[1], pos[2]
    out[...] = jnp.zeros_like(out)
    add = lambda items: functools.reduce(lambda a, b: a + b, items)
    two = add([t[0:3, :] for t in twos])
    lines = [ones[0:1, :], ones[1:2, :], two[0:1], two[1:2], two[2:3], add([d[...] for d in dys])]
    pack = add([p[...] for p in packs])
    span = heads * HD
    half = width // 2
    unit_total = add([u[...] for u in units])
    each = unit_total.shape[2] // parts
    def put(d, line, pieces):
        value = jnp.concatenate(pieces, axis=1)
        short = out.shape[2] - value.shape[1]
        if short:
            value = jnp.concatenate([value, jnp.zeros((1, short), WIDE)], axis=1)
        out[pl.ds(d, 1), pl.ds(line, 1), :] = value[None]

    for owner in range(parts):
        d = me ^ owner
        spots = [part * span + h * HD + owner * chunk for part in (0, 2) for h in range(heads)]
        put(d, 0, [pack[:, at : at + chunk] for at in spots])
        put(d, 1, [unit_total[u][:, owner * each : (owner + 1) * each] for u in range(unit_total.shape[0])])
        for k in range(rows):
            pieces = []
            for v in range(6):
                for j in range(2):
                    at = k * width + j * HD + owner * chunk
                    near, far = lines[v][:, at : at + chunk], lines[v][:, at + half : at + half + chunk]
                    pieces.append(jnp.where(low_col, near, far))
            put(d, 4 + (row ^ k), pieces)


def small_adam_kernel(spec, pos, tiny, *refs):
    heads, groups, chunk, grad_scale = spec
    row = pos[2]
    weights, states, grads, changes, fresh = (refs[3 * i : 3 * i + 3] for i in range(5))
    for part in range(2):
        for h in range(heads):
            at = (part * heads + h) * chunk
            grads[0][part, h : h + 1, :] = tiny[0:1, at : at + chunk] * grad_scale
    side = lax.broadcasted_iota(jnp.int32, (groups, chunk), 0)
    table = jnp.zeros((groups, chunk), WIDE)
    for g in range(groups):
        table = jnp.where(side == g, tiny[1:2, g * chunk : (g + 1) * chunk], table)
    grads[1][...] = table.T * grad_scale
    mine = tiny[pl.ds(4 + row, 1), :] * grad_scale
    for v in range(6):
        for j in range(2):
            at = (v * 2 + j) * chunk
            grads[2][v, j : j + 1, :] = mine[:, at : at + chunk]
    for i in range(3):
        change, low_moment, high_moment = adam_step(weights[i][...].astype(WIDE), grads[i][...], states[i][0], states[i][1], 0.0)
        changes[i][...] = change
        fresh[i][0] = low_moment
        fresh[i][1] = high_moment


def dot_nt(left, right):
    return lax.dot_general(left, right, (((1,), (1,)), ((), ())), preferred_element_type=WIDE)


def dot_nn(left, right):
    return lax.dot_general(left, right, (((1,), (0,)), ((), ())), preferred_element_type=WIDE)


def dot_tn(left, right):
    return lax.dot_general(left, right, (((0,), (0,)), ((), ())), preferred_element_type=WIDE)


def moments_of(stream):
    center = jnp.mean(stream, axis=-1, keepdims=True)
    offset = stream - center
    inv_std = lax.rsqrt(jnp.mean(offset * offset, axis=-1, keepdims=True) + norm_eps)
    return offset * inv_std, inv_std


def norm_backward(grad_norm, scaled, inv_std, gain):
    weighted = grad_norm * gain
    return inv_std * (
        weighted
        - jnp.mean(weighted, axis=-1, keepdims=True)
        - scaled * jnp.mean(weighted * scaled, axis=-1, keepdims=True)
    )


def lay_strips(low_col, near, far, rows):
    pieces = []
    for k in range(rows):
        mine, other = near(k), far(k)
        pieces.append(jnp.where(low_col, mine, other))
        pieces.append(jnp.where(low_col, other, mine))
    return jnp.concatenate(pieces, axis=1)


def soft(scores):
    lane = lax.broadcasted_iota(jnp.int32, scores.shape, 1)
    scores = jnp.where(lane < SEQ, scores * (1.0 / math.sqrt(HD)), -1e30)
    raised = jnp.exp(scores - jnp.max(scores, axis=-1, keepdims=True))
    return raised * (1.0 / jnp.sum(raised, axis=-1, keepdims=True))


class Source:
    def __init__(self, refs, count):
        self.refs, self.count = refs, count

    def block(self, k, first, size):
        at = first + (self.count if k == 2 else 0)
        return self.refs[(k + 1) // 2][at : at + size, :]


def lay_heads(target, sources, me, groups, rows):
    own = HD // len(sources)
    for k in range(rows):
        for d, source in enumerate(sources):
            place = me ^ d if len(sources) > 1 else 0
            for g in range(groups):
                at = g * HD + place * own
                if len(sources) > 1:
                    at = pl.multiple_of(at, own)
                target[k, pl.ds(at, own), :] = source.block(k, g * own, own)


def first_kernel(spec, pos, near, far, *refs):
    n, rows, heads, width = spec
    count = 4 * heads * HD // n
    sources = [Source([refs[d], refs[n + d], refs[2 * n + d]], count) for d in range(n)]
    vec_o, x_o, normed_o, packed_o, att_o, part_o, qkv_s = refs[3 * n :]
    low_col, me = pos[0] == 0, pos[1]
    small = refs[2 * n][count:, :].astype(WIDE)
    for d in range(1, n):
        small = small + refs[2 * n + d][count:, :].astype(WIDE)
    each = small.shape[0] // rows
    vec = jnp.concatenate([small[k * each : k * each + 6] for k in range(rows)], axis=1)
    vec_o[0:6, :] = vec
    lay_heads(qkv_s, sources, me, 4 * heads, rows)
    stream = lay_strips(low_col, lambda k: near[k, 0], lambda k: far[k, 0], rows)
    x_o[...] = stream
    scaled, _ = moments_of(stream.astype(WIDE))
    normed = (scaled * vec[0:1] + vec[1:2]).astype(LOW)
    normed_o[...] = normed
    span = heads * HD
    lines = span // width
    for part in range(3):
        total = dot_nt(normed[:, :width], qkv_s[0, part * span : (part + 1) * span, :])
        for k in range(1, rows):
            total = total + dot_nt(normed[:, k * width : (k + 1) * width], qkv_s[k, part * span : (part + 1) * span, :])
        if part != 1:
            line = 6 + (lines if part == 2 else 0)
            total = total + jnp.concatenate([small[line + i : line + i + 1] for i in range(lines)], axis=1)
        packed_o[:, part * span : (part + 1) * span] = total.astype(LOW)
    two = 2 * HD
    lane = lax.broadcasted_iota(jnp.int32, (1, two), 1)
    for pair in range(heads // 2):
        at = pair * two
        queries = packed_o[:, at : at + two]
        key_rows = packed_o[:, span + at : span + at + two]
        values = packed_o[:, 2 * span + at : 2 * span + at + two]
        halves = []
        for side in range(2):
            mask = (lane < HD) if side == 0 else (lane >= HD)
            probs = soft(dot_nt(jnp.where(mask, queries, jnp.zeros_like(queries)), key_rows))
            halves.append(dot_nn(probs.astype(LOW), values))
        att_o[:, at : at + two] = jnp.where(lane < HD, halves[0], halves[1]).astype(LOW)
    for k in range(rows):
        part_o[:, k * width : (k + 1) * width] = dot_nn(att_o[...], qkv_s[k, 3 * span :, :]).astype(LOW)


def row_blocks(ref, row, parts, rows):
    return [jnp.concatenate([ref[d, row ^ k] for d in range(parts)], axis=0) for k in range(rows)]


def feed_kernel(spec, pos, vec, small, x, part, came, near, far, up, down, *refs):
    parts, rows, width = spec
    mid, normed, dy, dy_sum_o, units_o, hid_o, unit_sum_o, top_o, far_o, back_o, mixed_s, back_s = refs
    low_col, row = pos[0] == 0, pos[2]
    step = pl.program_id(0)

    @pl.when(step == 0)
    def _():
        dy[...] = lay_strips(low_col, lambda k: near[k, 0], lambda k: far[k, 0], rows)
        dy_sum_o[...] = jnp.sum(dy[...].astype(WIDE), axis=0, keepdims=True)
        middle = x[...].astype(WIDE) + (part[...].astype(WIDE) + came[...].astype(WIDE) + vec[2:3, :])
        mid[...] = middle
        scaled, _ = moments_of(middle)
        normed[...] = (scaled * vec[3:4, :] + vec[4:5, :]).astype(LOW)
        mixed_s[...] = jnp.zeros_like(mixed_s)
        back_s[...] = jnp.zeros_like(back_s)

    up_rows, down_rows = row_blocks(up, row, parts, rows), row_blocks(down, row, parts, rows)
    hidden = dot_nt(normed[:, :width], up_rows[0])
    for k in range(1, rows):
        hidden = hidden + dot_nt(normed[:, k * width : (k + 1) * width], up_rows[k])
    active, slope = gelu_both(hidden + small[0])
    active = active.astype(LOW)
    units_o[0] = active
    grad = dot_nt(dy[:, :width], down_rows[0])
    for k in range(1, rows):
        grad = grad + dot_nt(dy[:, k * width : (k + 1) * width], down_rows[k])
    grad = (grad * slope).astype(LOW)
    hid_o[0] = grad
    unit_sum_o[0] = jnp.sum(grad.astype(WIDE), axis=0, keepdims=True)
    for k in range(rows):
        at = slice(k * width, (k + 1) * width)
        mixed_s[:, at] += dot_nn(active, down_rows[k])
        back_s[:, at] += dot_nn(grad, up_rows[k])

    @pl.when(step == pl.num_programs(0) - 1)
    def _():
        back_o[...] = back_s[...].astype(LOW)
        half = width // 2
        for k in range(rows):
            left, right = slice(k * width, k * width + half), slice(k * width + half, (k + 1) * width)
            base = mid[...] + vec[5:6, :]
            top_l, top_r = mixed_s[:, left] + base[:, left], mixed_s[:, right] + base[:, right]
            top_o[k] = jnp.where(low_col, top_l, top_r)
            far_o[k] = jnp.where(low_col, mixed_s[:, right], mixed_s[:, left]).astype(LOW)


def feed_grad_kernel(spec, pos, *refs):
    parts, rows, width = spec
    hids, units, normeds, dys, out = refs[0:2], refs[2:4], refs[4:6], refs[6:8], refs[8]
    row = pos[2]

    def write(left, right):
        total = dot_tn(left[0][0], right[0][...]) + dot_tn(left[1][0], right[1][...])
        block = total.shape[0] // parts
        for d in range(parts):
            for k in range(rows):
                out[d, row ^ k] = total[d * block : (d + 1) * block, k * width : (k + 1) * width].astype(LOW)

    half = pl.num_programs(0) // 2

    @pl.when(pl.program_id(0) < half)
    def _():
        write(hids, normeds)

    @pl.when(pl.program_id(0) >= half)
    def _():
        write(units, dys)


def second_kernel(spec, pos, vec, mid, back, came, dy, packed, *refs):
    n, rows, heads, width = spec
    count = 4 * heads * HD // n
    sources = [Source([refs[d], refs[n + d], refs[2 * n + d]], count) for d in range(n)]
    dmid_o, dz_o, dpacked_o, back_o, sums_o, psum_o, qkv_s, datt_s = refs[3 * n :]
    me = pos[1]
    lay_heads(qkv_s, sources, me, 4 * heads, rows)
    span = heads * HD
    grad_norm = back[...].astype(WIDE) + came[...].astype(WIDE)
    scaled, inv_std = moments_of(mid[...])
    dmid = dy[...].astype(WIDE) + norm_backward(grad_norm, scaled, inv_std, vec[3:4, :])
    dmid_o[...] = dmid
    dz = dmid.astype(LOW)
    dz_o[...] = dz
    sums_o[0:1, :] = jnp.sum(dz.astype(WIDE), axis=0, keepdims=True)
    sums_o[1:2, :] = jnp.sum(grad_norm * scaled, axis=0, keepdims=True)
    sums_o[2:3, :] = jnp.sum(grad_norm, axis=0, keepdims=True)
    total = dot_nt(dz[:, :width], qkv_s[0, 3 * span :, :])
    for k in range(1, rows):
        total = total + dot_nt(dz[:, k * width : (k + 1) * width], qkv_s[k, 3 * span :, :])
    datt_s[...] = total.astype(LOW)
    two = 2 * HD
    scale = 1.0 / math.sqrt(HD)
    lane = lax.broadcasted_iota(jnp.int32, (1, two), 1)
    for pair in range(heads // 2):
        at = pair * two
        queries = packed[:, at : at + two]
        key_rows = packed[:, span + at : span + at + two]
        values = packed[:, 2 * span + at : 2 * span + at + two]
        grads = datt_s[:, at : at + two]
        dqs, dks, dvs = [], [], []
        for side in range(2):
            mask = (lane < HD) if side == 0 else (lane >= HD)
            probs = soft(dot_nt(jnp.where(mask, queries, jnp.zeros_like(queries)), key_rows))
            dprobs = dot_nt(jnp.where(mask, grads, jnp.zeros_like(grads)), values)
            dscores = probs * (dprobs - jnp.sum(dprobs * probs, axis=-1, keepdims=True))
            dscores = dscores.astype(LOW)
            dqs.append(dot_nn(dscores, key_rows))
            dks.append(dot_tn(dscores, queries))
            dvs.append(dot_tn(probs.astype(LOW), grads))
        first = lane < HD
        dpacked_o[:, at : at + two] = (jnp.where(first, dqs[0], dqs[1]) * scale).astype(LOW)
        dpacked_o[:, span + at : span + at + two] = (jnp.where(first, dks[0], dks[1]) * scale).astype(LOW)
        dpacked_o[:, 2 * span + at : 2 * span + at + two] = jnp.where(first, dvs[0], dvs[1]).astype(LOW)
    psum_o[...] = jnp.sum(dpacked_o[...].astype(WIDE), axis=0, keepdims=True)
    for k in range(rows):
        back_o[:, k * width : (k + 1) * width] = dot_nn(dpacked_o[...], qkv_s[k, : 3 * span, :]).astype(LOW)


def attn_grad_kernel(spec, pos, *refs):
    n, rows, heads, width = spec
    dpacked, normed, att, dz = refs[0:2], refs[2:4], refs[4:6], refs[6:8]
    outs, total_s = refs[8 : 8 + n], refs[8 + n]
    me = pos[1]
    span = heads * HD
    own = HD // n
    for part in range(4):
        if part < 3:
            at = slice(part * span, (part + 1) * span)
            total = dot_tn(dpacked[0][:, at], normed[0][...]) + dot_tn(dpacked[1][:, at], normed[1][...])
        else:
            total = dot_tn(att[0][...], dz[0][...]) + dot_tn(att[1][...], dz[1][...])
        total_s[...] = total.astype(LOW)
        for d in range(n):
            place = me ^ d if n > 1 else 0
            for g in range(heads):
                line = g * HD + place * own
                if n > 1:
                    line = pl.multiple_of(line, own)
                value = total_s[pl.ds(line, own), :]
                to = (part * heads + g) * own
                for k in range(rows):
                    outs[d][k, to : to + own, :] = value[:, k * width : (k + 1) * width]


def gelu_both(values):
    tail = 0.5 * (1.0 + lax.erf(values * (1.0 / math.sqrt(2.0))))
    bell = jnp.exp(values * values * -0.5) * (1.0 / math.sqrt(2.0 * math.pi))
    return values * tail, tail + values * bell


def last_kernel(spec, pos, vec, *refs):
    rows, width, images = spec
    x, back, came, dmid = (refs[i * images : (i + 1) * images] for i in range(4))
    out_o, sums_o = refs[4 * images :]
    low_col = pos[0] == 0
    half = width // 2
    for i in range(images):
        scaled, inv_std = moments_of(x[i][...].astype(WIDE))
        grad_norm = back[i][...].astype(WIDE) + came[i][...].astype(WIDE)
        value = dmid[i][...] + norm_backward(grad_norm, scaled, inv_std, vec[0:1, :])
        gain_sum = jnp.sum(grad_norm * scaled, axis=0, keepdims=True)
        shift_sum = jnp.sum(grad_norm, axis=0, keepdims=True)
        if i == 0:
            sums_o[0:1, :] = gain_sum
            sums_o[1:2, :] = shift_sum
        else:
            sums_o[0:1, :] += gain_sum
            sums_o[1:2, :] += shift_sum
        for k in range(rows):
            left, right = value[:, k * width : k * width + half], value[:, k * width + half : (k + 1) * width]
            out_o[k, i] = jnp.where(low_col, left, right).astype(LOW)


ROOM = 56 * 1024 * 1024


def whole(array):
    zeros = (0,) * len(array.shape)
    return pl.BlockSpec(tuple(array.shape), lambda *_: zeros)


def run_kernel(body, args, outs, scratch=(), grid=None, in_specs=None, out_specs=None):
    if in_specs is None:
        in_specs = [pl.BlockSpec(memory_space=pltpu.SMEM)] + [whole(a) for a in args[1:]]
    if out_specs is None:
        out_specs = [whole(o) for o in outs]
    return pl.pallas_call(
        body,
        grid=grid or (1,),
        in_specs=in_specs,
        out_specs=out_specs,
        out_shape=outs,
        scratch_shapes=list(scratch),
        compiler_params=pltpu.CompilerParams(vmem_limit_bytes=ROOM),
        cost_estimate=pl.CostEstimate(flops=1024, bytes_accessed=1024, transcendentals=0),
    )(*args)


def shaped(shape, kind):
    return jax.ShapeDtypeStruct(shape, kind)


def on_device(
    tokens, cotangent, w_qkv, b_qkv, w_out, w_up, b_up, w_down, vectors,
    state_qkv, state_qkv_bias, state_out, state_up, state_up_bias, state_down, state_vectors,
):
    parts, rows = lax.axis_size("dp"), lax.axis_size("row")
    col, row_index, me = lax.axis_index("col"), lax.axis_index("row"), lax.axis_index("dp")
    low_col = col == 0
    width = w_qkv.shape[0]
    heads, chunk = w_qkv.shape[2], w_qkv.shape[3]
    groups = w_up.shape[1]
    strip = tokens.shape[1]
    images = tokens.shape[0] // (SEQ * rows)
    model = rows * width
    span = heads * HD
    pos = jnp.stack([col, me, row_index]).astype(jnp.int32)

    qkv_own = w_qkv.transpose(1, 2, 3, 0).reshape(-1, width)
    out_own = w_out.reshape(-1, width)
    up_own = w_up.transpose(1, 2, 0).reshape(-1, width)
    down_own = w_down.reshape(-1, width)
    qkv_count, unit_count = qkv_own.shape[0], up_own.shape[0]
    head_own = jnp.concatenate([qkv_own, out_own])
    head_count = head_own.shape[0]

    at_me = (jnp.arange(parts) == me)[:, None]
    vec_own = jnp.where(at_me, vectors[:, :, None, :], 0).reshape(6, -1)
    vec_far = swap(vec_own, "col", 1)
    vec_pair = jnp.stack([jnp.where(low_col, vec_own, vec_far), jnp.where(low_col, vec_far, vec_own)])
    bias_own = jnp.where(at_me, b_qkv[:, :, None, :], 0).reshape(-1, width)
    unit_own = jnp.where(at_me, b_up.reshape(1, -1), 0).reshape(-1, width)
    small_count = 6 + bias_own.shape[0] + unit_own.shape[0]
    small_each = small_count + -small_count % 16

    def to_send(stream, extra):
        blocks = stream.astype(LOW).reshape(rows, images, SEQ, strip)
        blocks = jnp.pad(blocks, ((0, 0), (0, 0), (0, PAD - SEQ), (0, 0)))
        if extra is not None:
            extra = jnp.pad(extra, ((0, 0), (0, 2), (0, 0)))
            blocks = jnp.concatenate([blocks, jnp.broadcast_to(extra, (rows, *extra.shape))], axis=2)
        return [lax.dynamic_index_in_dim(blocks, row_index ^ k, 0, False) for k in range(rows)]

    def send_images(blocks):
        return [blocks[0]] + [swap(block, "row", k) for k, block in enumerate(blocks) if k]

    def near_two(values):
        return [swap(values, "row", 1), swap(values, "row", 2)]

    token = [pos]

    def fence(*values):
        token[0], *values = lax.optimization_barrier((token[0], *values))
        return values

    assert rows == 4 and images == 2 and lax.axis_size("col") == 2
    feed_all = lax.all_gather(jnp.concatenate([up_own, down_own]), ("dp", "row"), axis=0).reshape(parts, rows, -1, width)
    head_two = near_two(head_own)
    head_x = across(head_own)
    head_plane = planes(head_own)
    token_blocks, dy_blocks = to_send(tokens, vec_pair), to_send(cotangent, None)
    small_same = jnp.pad(jnp.concatenate([bias_own, unit_own]), ((6, small_each - small_count), (0, 0)))
    head_two, head_x, head_plane, token_blocks = fence(head_two, head_x, head_plane, token_blocks)

    head_three = swap(head_two[1], "row", 1)
    came = send_images(token_blocks)
    head_pair = jnp.concatenate(head_two)
    head_pair_x = across(head_pair)
    head_three, came, head_pair_x, head_pair, head_x = fence(head_three, came, head_pair_x, head_pair, head_x)

    small_rows = jnp.stack([jnp.concatenate([b[0, PAD : PAD + 6], b[1, PAD : PAD + 6]], axis=1) for b in came])
    small_rows = jnp.pad(small_rows, ((0, 0), (0, small_each - 6), (0, 0))) + small_same
    head_third = jnp.concatenate([head_three, small_rows.reshape(-1, width)])
    near = jnp.stack([block[:, :PAD] for block in came])
    far = swap(near, "col", 1)
    head_third_x = across(head_third)
    head_own_planes = [*head_plane, *planes(head_x)]
    head_pair_planes = [*planes(head_pair), *planes(head_pair_x)]
    head_third_x, head_third, head_own_planes, head_pair_planes, far, near, dy_blocks = fence(
        head_third_x, head_third, head_own_planes, head_pair_planes, far, near, dy_blocks
    )

    head_third_planes = [*planes(head_third), *planes(head_third_x)]

    split = chunk % 16 == 0
    n = parts if split else 1
    head_weights = [*head_own_planes, *head_pair_planes, *head_third_planes]
    if not split:
        def merge(blocks, lead):
            both = xor_order(jnp.stack(blocks), 0, "dp").reshape(parts, lead, blocks[0].shape[0] // lead, width)
            return both.transpose(1, 0, 2, 3).reshape(-1, width)

        def merge_some(blocks, count, lead, number):
            return [merge([b[k * count : (k + 1) * count] for b in blocks], lead) for k in range(number)]

        small_sum = sum(b[head_count:].astype(WIDE) for b in head_third_planes).astype(LOW)
        head_weights = [
            merge(head_own_planes, 4 * heads),
            jnp.concatenate(merge_some(head_pair_planes, head_count, 4 * heads, 2)),
            jnp.concatenate([*merge_some(head_third_planes, head_count, 4 * heads, 1), small_sum]),
        ]
    head_small = [b[head_count * parts // n :] for b in head_weights[2 * n :]]
    scalars = pl.BlockSpec(memory_space=pltpu.SMEM)
    head_specs = [pl.BlockSpec((head_count * parts // n, width), lambda *_: (0, 0))] * n + [whole(w) for w in head_weights[n:]]
    full, low_full = shaped((PAD, model), WIDE), shaped((PAD, model), LOW)

    def forward_one(i):
        strips = pl.BlockSpec((rows, 1, PAD, strip), lambda *_: (0, i, 0, 0))
        outs = [
            shaped((8, model), WIDE),
            low_full,
            low_full,
            shaped((PAD, 3 * span), LOW),
            shaped((PAD, span), LOW),
            low_full,
        ]
        return run_kernel(
            functools.partial(first_kernel, (n, rows, heads, width)),
            (token[0], near, far, *head_weights),
            outs,
            scratch=[pltpu.VMEM((rows, 4 * span, width), LOW)],
            in_specs=[scalars, strips, strips, *head_specs],
        )

    done = [forward_one(0)]
    done, dy_blocks = fence(done, dy_blocks)

    came_one = [swap(done[0][5], "col", 1)]
    dy_came = send_images(dy_blocks)
    done.append(forward_one(1))
    vec = done[0][0]
    unit_rows = sum(b[6 + bias_own.shape[0] :][: unit_own.shape[0]].astype(WIDE) for b in head_small)
    steps = 4
    block = unit_count // steps
    unit_rows = unit_rows.reshape(parts, steps, block).transpose(1, 0, 2).reshape(steps, 1, parts * block)
    done, came_one, dy_came, unit_rows = fence(done, came_one, dy_came, unit_rows)

    came_one = [*came_one, swap(done[1][5], "col", 1)]
    near_dy = jnp.stack(dy_came)
    far_dy = swap(near_dy, "col", 1)
    far_dy, near_dy, came_one = fence(far_dy, near_dy, came_one)

    unit_spec = pl.BlockSpec((1, PAD, parts * block), lambda u: (u, 0, 0))
    unit_sum_spec = pl.BlockSpec((1, 1, parts * block), lambda u: (u, 0, 0))
    unit_shape = (steps, PAD, parts * block)

    def feed_one(i):
        strips = pl.BlockSpec((rows, 1, PAD, strip), lambda *_: (0, i, 0, 0))
        outs = [
            full,
            low_full,
            low_full,
            shaped((1, model), WIDE),
            shaped(unit_shape, LOW),
            shaped(unit_shape, LOW),
            shaped((steps, 1, parts * block), WIDE),
            shaped((rows, PAD, strip), WIDE),
            shaped((rows, PAD, strip), LOW),
            low_full,
        ]
        out_specs = [whole(o) for o in outs]
        out_specs[4], out_specs[5], out_specs[6] = unit_spec, unit_spec, unit_sum_spec
        acts = (done[i][1], done[i][5], came_one[i])
        return run_kernel(
            functools.partial(feed_kernel, (parts, rows, width)),
            (token[0], vec, unit_rows, *acts, near_dy, far_dy, feed_all, feed_all),
            outs,
            scratch=[pltpu.VMEM((PAD, model), WIDE), pltpu.VMEM((PAD, model), WIDE)],
            grid=(steps,),
            in_specs=[
                scalars, whole(vec), unit_sum_spec, *[whole(a) for a in acts], strips, strips,
                pl.BlockSpec((parts, rows, block, width), lambda u: (0, 0, u, 0)),
                pl.BlockSpec((parts, rows, block, width), lambda u: (0, 0, u + steps, 0)),
            ],
            out_specs=out_specs,
        )

    fed = [feed_one(0)]
    fed, came_one = fence(fed, came_one)
    came_two = [swap(fed[0][9], "col", 1)]
    fed.append(feed_one(1))
    fed, came_two = fence(fed, came_two)

    came_two = [*came_two, swap(fed[1][9], "col", 1)]
    early = pl.BlockSpec((1, PAD, parts * block), lambda u: (jnp.minimum(u, steps - 1), 0, 0))
    late = pl.BlockSpec((1, PAD, parts * block), lambda u: (jnp.maximum(u - steps, 0), 0, 0))
    feed_grad = run_kernel(
        functools.partial(feed_grad_kernel, (parts, rows, width)),
        (token[0], *[f[5] for f in fed], *[f[4] for f in fed], *[f[1] for f in fed], *[f[2] for f in fed]),
        [shaped((parts, rows, 2 * unit_count, width), LOW)],
        grid=(2 * steps,),
        in_specs=[scalars, early, early, late, late, *[whole(low_full)] * 4],
        out_specs=[pl.BlockSpec((parts, rows, block, width), lambda u: (0, 0, u, 0))],
    )[0]
    feed_grad, came_two, fed = fence(feed_grad, came_two, fed)
    feed_total = lax.psum_scatter(feed_grad.reshape(-1, width), ("dp", "row"), scatter_dimension=0, tiled=True)

    def fold(blocks):
        held = dict(enumerate(blocks))
        for bit in bits_of("dp")[:-1]:
            held = join(held, "dp", bit)
        return held[0]

    def ordered(blocks, lead):
        if n == parts:
            return blocks
        both = blocks[0].reshape(rows, lead, parts, -1, width).transpose(2, 0, 1, 3, 4)
        both = xor_order(both.reshape(parts, rows, -1, width), 0, "dp")
        return [both[d] for d in range(parts)]

    half_rows = rows // 2

    def sum_high(near_sum, came_part):
        return [add_low(near_sum[half_rows + k], came_part[k]) for k in range(half_rows)]

    def sum_low(near_sum, came_part):
        return [add_low(near_sum[k], came_part[k]) for k in range(half_rows)]

    def from_images(strips):
        came = [strips[0]] + [swap(strips[k], "row", k) for k in range(1, rows)]
        stacked = xor_order(jnp.stack(came)[:, :, :SEQ], 0, "row")
        return stacked.reshape(-1, strip).astype(WIDE)

    def backward_one(i):
        outs = [full, low_full, shaped((PAD, 3 * span), LOW), low_full, shaped((8, model), WIDE), shaped((1, 3 * span), WIDE)]
        acts = (vec, fed[i][0], fed[i][9], came_two[i], fed[i][2], done[i][3])
        return run_kernel(
            functools.partial(second_kernel, (n, rows, heads, width)),
            (token[0], *acts, *head_weights),
            outs,
            scratch=[pltpu.VMEM((rows, 4 * span, width), LOW), pltpu.VMEM((PAD, span), LOW)],
            in_specs=[scalars, *[whole(a) for a in acts], *head_specs],
        )

    top_far = swap(jnp.stack([f[8] for f in fed]), "col", 1)
    returned = [backward_one(0)]
    returned, top_far = fence(returned, top_far)

    came_three = [swap(returned[0][3], "col", 1)]
    top = jnp.stack([f[7] + t.astype(WIDE) for f, t in zip(fed, top_far)], axis=1).astype(LOW)
    result = from_images(top)
    returned.append(backward_one(1))
    returned, came_three, result = fence(returned, came_three, result)

    came_three = [*came_three, swap(returned[1][3], "col", 1)]
    attn_grad = run_kernel(
        functools.partial(attn_grad_kernel, (n, rows, heads, width)),
        (
            token[0], *[r[2] for r in returned], *[d[2] for d in done], *[d[4] for d in done], *[r[1] for r in returned],
        ),
        [shaped((rows, head_count * parts // n, width), LOW) for _ in range(n)],
        scratch=[pltpu.VMEM((span, model), LOW)],
    )
    attn_grad, came_three = fence(attn_grad, came_three)

    attn_blocks = ordered(attn_grad, 4 * heads)
    attn_far, attn_near = fold(attn_blocks[parts // 2 :]), fold(attn_blocks[: parts // 2])
    grad_strips, sums_one = run_kernel(
        functools.partial(last_kernel, (rows, width, images)),
        (
            token[0], vec, *[d[1] for d in done], *[r[3] for r in returned], *came_three, *[r[0] for r in returned],
        ),
        [shaped((rows, images, PAD, strip), LOW), shaped((8, model), WIDE)],
    )
    attn_far, attn_near, grad_strips, sums_one = fence(attn_far, attn_near, grad_strips, sums_one)

    grad_scale = grad_gain / math.sqrt(tokens.shape[0] * parts)

    lanes = max(unit_count, 2 * heads * chunk, 12 * chunk)
    tiny = run_kernel(
        functools.partial(collect_kernel, (rows, heads, chunk, parts, width, images)),
        (
            token[0], sums_one, *[r[4] for r in returned],
            *[f[3] for f in fed], *[r[5] for r in returned], *[f[6] for f in fed],
        ),
        [shaped((parts, 8, lanes), WIDE)],
    )[0]
    attn_high = across(attn_far[half_rows:])
    tiny = functools.reduce(lambda a, b: a + b, [tiny[0]] + [swap(tiny[d], "dp", d) for d in range(1, parts)])
    def adam(reduced, owns, states, ranges):
        first, pieces = reduced
        outs = []
        for size, _ in ranges:
            outs += [shaped((size, width), WIDE), shaped((size, width), WIDE), shaped((2, size, width), WIDE)]
        args = (first, *pieces, *owns, *states)
        return run_kernel(
            functools.partial(adam_kernel, (len(pieces), [r[0] for r in ranges], grad_scale)),
            args,
            outs,
            in_specs=[whole(a) for a in args],
        )

    state_rows = lambda a, order: a.transpose(order).reshape(2, -1, width)
    out_count = out_own.shape[0]
    attn_high, attn_far, attn_near, grad_strips, tiny = fence(attn_high, attn_far, attn_near, grad_strips, tiny)

    attn_low = across(attn_far[:half_rows])
    attn_two, attn_three = sum_high(attn_near, attn_high)
    attn_three = swap(attn_three, "row", 1)
    grad_tokens = from_images(grad_strips)
    attn_low, attn_two, attn_three, attn_near, grad_tokens, tiny = fence(
        attn_low, attn_two, attn_three, attn_near, grad_tokens, tiny
    )

    attn_zero, attn_one = sum_low(attn_near, attn_low)
    attn_one = swap(attn_one, "row", 1)
    attn_two = swap(add_low(attn_two, attn_three), "row", 2)
    tiny = (tiny + swap(tiny, "row", 1)) + (swap(tiny, "row", 2) + swap(tiny, "row", 3))
    attn_zero, attn_one, attn_two, tiny = fence(attn_zero, attn_one, attn_two, tiny)
    feed_done = adam(
        (feed_total, []),
        [up_own, down_own],
        [state_rows(state_up, (0, 2, 3, 1)), state_rows(state_down, (0, 1, 2, 3))],
        [(unit_count, 0), (unit_count, 0)],
    )

    flat_up = lambda a: jnp.swapaxes(a, -1, -2)
    small_args = (b_qkv, flat_up(b_up), vectors, state_qkv_bias, flat_up(state_up_bias), state_vectors)
    small_kinds = (b_qkv.shape, flat_up(b_up).shape, vectors.shape)
    small_done = run_kernel(
        functools.partial(small_adam_kernel, (heads, groups, chunk, grad_scale)),
        (token[0], tiny, *small_args),
        [shaped(k, WIDE) for k in (*small_kinds, *small_kinds)] + [shaped((2, *k), WIDE) for k in small_kinds],
    )

    attn_done = adam(
        (attn_zero, [attn_one, attn_two]),
        [qkv_own, out_own],
        [state_rows(state_qkv, (0, 2, 3, 4, 1)), state_rows(state_out, (0, 1, 2, 3))],
        [(qkv_count, 0), (out_count, 0)],
    )

    def shape_all(which):
        lead = (2,) if which == 2 else ()
        more = (0,) if which == 2 else ()
        move = lambda order: (*more, *[o + len(lead) for o in order])
        return (
            attn_done[which].reshape(*lead, 3, heads, chunk, width).transpose(move((3, 0, 1, 2))),
            small_done[3 * which],
            attn_done[3 + which].reshape(*lead, *w_out.shape),
            feed_done[which].reshape(*lead, groups, chunk, width).transpose(move((2, 0, 1))),
            flat_up(small_done[3 * which + 1]),
            feed_done[3 + which].reshape(*lead, *w_down.shape),
            small_done[3 * which + 2],
        )

    return (result, grad_tokens, *shape_all(0), *shape_all(1), *shape_all(2))


def solution(mesh):
    placed = (
        P("dp", ("row", "col")),
        P("dp", ("row", "col")),
        P("row", None, "col", "dp"),
        P(None, "col", "dp"),
        P("col", "dp", "row"),
        P("row", "col", "dp"),
        P("col", "dp"),
        P("col", "dp", "row"),
        P(None, ("row", "col"), "dp"),
        P(None, "row", None, "col", "dp"),
        P(None, None, "col", "dp"),
        P(None, "col", "dp", "row"),
        P(None, "row", "col", "dp"),
        P(None, "col", "dp"),
        P(None, "col", "dp", "row"),
        P(None, None, ("row", "col"), "dp"),
    )
    params = placed[2:9]
    return jax.shard_map(
        on_device,
        mesh=mesh,
        in_specs=placed,
        out_specs=(placed[0], placed[0], *params, *params, *placed[9:]),
        check_vma=False,
    )
```

```python
import functools
import math

import jax
import jax.numpy as jnp
from jax import lax
from jax.experimental import pallas as pl
from jax.experimental.pallas import tpu as pltpu
from jax.sharding import PartitionSpec as P

HD = 64
SEQ = 197
PAD = 208
STEP = 10

norm_eps = 1e-06
beta_first = 0.9
beta_second = 0.999
learn_rate = 0.01
weight_decay = 0.05
adam_eps = 1e-08
grad_gain = 32.0

LOW = jnp.bfloat16
WIDE = jnp.float32


def swap(values, name, bit):
    count = lax.axis_size(name)
    return lax.ppermute(values, name, [(i, i ^ bit) for i in range(count)])


def bits_of(name):
    bits, bit = [], 1
    while bit < lax.axis_size(name):
        bits.append(bit)
        bit *= 2
    return bits


def after(value, *others):
    return lax.optimization_barrier((value, *others))[0]


def planes(values):
    blocks = {0: values}
    for bit in reversed(bits_of("dp")[:-1]):
        for place in list(blocks):
            blocks[place ^ bit] = swap(blocks[place], "dp", bit)
    return [blocks[d] for d in range(len(blocks))]


def across(values):
    return swap(values, "dp", lax.axis_size("dp") // 2)


def add_low(left, right):
    return (left.astype(WIDE) + right.astype(WIDE)).astype(left.dtype)


def join(held, name, bit):
    return {d: add_low(held[d], swap(held[d ^ bit], name, bit)) for d in held if not d & bit}


def scatter(blocks, name):
    held = dict(enumerate(blocks))
    for bit in bits_of(name):
        held = join(held, name, bit)
    return held[0]


def xor_order(values, axis, name):
    mine = lax.axis_index(name)
    shape = values.shape
    for bit in bits_of(name):
        split = values.reshape(shape[:axis] + (shape[axis] // (2 * bit), 2, bit) + shape[axis + 1 :])
        flipped = jnp.flip(split, axis + 1)
        values = jnp.where((mine & bit) > 0, flipped, split).reshape(shape)
    return values


def adam_step(weight_old, gradient, first_old, second_old, decay_on):
    first_moment = beta_first * first_old + (1.0 - beta_first) * gradient
    second_moment = beta_second * second_old + (1.0 - beta_second) * gradient * gradient
    first_hat = first_moment / (1.0 - beta_first**STEP)
    second_hat = second_moment / (1.0 - beta_second**STEP)
    change = -learn_rate * (first_hat / (jnp.sqrt(second_hat) + adam_eps) + decay_on * weight_old)
    return change, first_moment, second_moment


def adam_kernel(spec, first, *refs):
    count, sizes, grad_scale = spec
    pieces, refs = refs[:count], refs[count:]
    weights, states, outs = refs[: len(sizes)], refs[len(sizes) : 2 * len(sizes)], refs[2 * len(sizes) :]
    at = 0
    for i, size in enumerate(sizes):
        lines = slice(at, at + size)
        at += size
        total = first[lines].astype(WIDE)
        for piece in pieces:
            total = total + piece[lines].astype(WIDE)
        gradient = total * grad_scale
        change, low_moment, high_moment = adam_step(
            weights[i][...].astype(WIDE), gradient, states[i][0], states[i][1], weight_decay
        )
        outs[3 * i][...] = gradient
        outs[3 * i + 1][...] = change
        outs[3 * i + 2][0] = low_moment
        outs[3 * i + 2][1] = high_moment


def collect_kernel(spec, pos, ones, *refs):
    rows, heads, chunk, parts, width, images = spec
    twos, dys, packs, refs = refs[:images], refs[images : 2 * images], refs[2 * images : 3 * images], refs[3 * images :]
    units, out, = refs[:-1], refs[-1]
    low_col, me, row = pos[0] == 0, pos[1], pos[2]
    out[...] = jnp.zeros_like(out)
    add = lambda items: functools.reduce(lambda a, b: a + b, items)
    two = add([t[0:3, :] for t in twos])
    lines = [ones[0:1, :], ones[1:2, :], two[0:1], two[1:2], two[2:3], add([d[...] for d in dys])]
    pack = add([p[...] for p in packs])
    span = heads * HD
    half = width // 2
    unit_total = add([u[...] for u in units])
    each = unit_total.shape[2] // parts
    def put(d, line, pieces):
        value = jnp.concatenate(pieces, axis=1)
        short = out.shape[2] - value.shape[1]
        if short:
            value = jnp.concatenate([value, jnp.zeros((1, short), WIDE)], axis=1)
        out[pl.ds(d, 1), pl.ds(line, 1), :] = value[None]

    for owner in range(parts):
        d = me ^ owner
        spots = [part * span + h * HD + owner * chunk for part in (0, 2) for h in range(heads)]
        put(d, 0, [pack[:, at : at + chunk] for at in spots])
        put(d, 1, [unit_total[u][:, owner * each : (owner + 1) * each] for u in range(unit_total.shape[0])])
        for k in range(rows):
            pieces = []
            for v in range(6):
                for j in range(2):
                    at = k * width + j * HD + owner * chunk
                    near, far = lines[v][:, at : at + chunk], lines[v][:, at + half : at + half + chunk]
                    pieces.append(jnp.where(low_col, near, far))
            put(d, 4 + (row ^ k), pieces)


def small_adam_kernel(spec, pos, tiny, *refs):
    heads, groups, chunk, grad_scale = spec
    row = pos[2]
    weights, states, grads, changes, fresh = (refs[3 * i : 3 * i + 3] for i in range(5))
    for part in range(2):
        for h in range(heads):
            at = (part * heads + h) * chunk
            grads[0][part, h : h + 1, :] = tiny[0:1, at : at + chunk] * grad_scale
    side = lax.broadcasted_iota(jnp.int32, (groups, chunk), 0)
    table = jnp.zeros((groups, chunk), WIDE)
    for g in range(groups):
        table = jnp.where(side == g, tiny[1:2, g * chunk : (g + 1) * chunk], table)
    grads[1][...] = table.T * grad_scale
    mine = tiny[pl.ds(4 + row, 1), :] * grad_scale
    for v in range(6):
        for j in range(2):
            at = (v * 2 + j) * chunk
            grads[2][v, j : j + 1, :] = mine[:, at : at + chunk]
    for i in range(3):
        change, low_moment, high_moment = adam_step(weights[i][...].astype(WIDE), grads[i][...], states[i][0], states[i][1], 0.0)
        changes[i][...] = change
        fresh[i][0] = low_moment
        fresh[i][1] = high_moment


def dot_nt(left, right):
    return lax.dot_general(left, right, (((1,), (1,)), ((), ())), preferred_element_type=WIDE)


def dot_nn(left, right):
    return lax.dot_general(left, right, (((1,), (0,)), ((), ())), preferred_element_type=WIDE)


def dot_tn(left, right):
    return lax.dot_general(left, right, (((0,), (0,)), ((), ())), preferred_element_type=WIDE)


def moments_of(stream):
    center = jnp.mean(stream, axis=-1, keepdims=True)
    offset = stream - center
    inv_std = lax.rsqrt(jnp.mean(offset * offset, axis=-1, keepdims=True) + norm_eps)
    return offset * inv_std, inv_std


def norm_backward(grad_norm, scaled, inv_std, gain):
    weighted = grad_norm * gain
    return inv_std * (
        weighted
        - jnp.mean(weighted, axis=-1, keepdims=True)
        - scaled * jnp.mean(weighted * scaled, axis=-1, keepdims=True)
    )


def lay_strips(low_col, near, far, rows):
    pieces = []
    for k in range(rows):
        mine, other = near(k), far(k)
        pieces.append(jnp.where(low_col, mine, other))
        pieces.append(jnp.where(low_col, other, mine))
    return jnp.concatenate(pieces, axis=1)


def soft(scores):
    lane = lax.broadcasted_iota(jnp.int32, scores.shape, 1)
    scores = jnp.where(lane < SEQ, scores * (1.0 / math.sqrt(HD)), -1e30)
    raised = jnp.exp(scores - jnp.max(scores, axis=-1, keepdims=True))
    return raised * (1.0 / jnp.sum(raised, axis=-1, keepdims=True))


class Source:
    def __init__(self, refs, count):
        self.refs, self.count = refs, count

    def block(self, k, first, size):
        at = first + (self.count if k == 2 else 0)
        return self.refs[(k + 1) // 2][at : at + size, :]


def lay_heads(target, sources, me, groups, rows):
    own = HD // len(sources)
    for k in range(rows):
        for d, source in enumerate(sources):
            place = me ^ d if len(sources) > 1 else 0
            for g in range(groups):
                at = g * HD + place * own
                if len(sources) > 1:
                    at = pl.multiple_of(at, own)
                target[k, pl.ds(at, own), :] = source.block(k, g * own, own)


def first_kernel(spec, pos, near, far, *refs):
    n, rows, heads, width = spec
    count = 4 * heads * HD // n
    sources = [Source([refs[d], refs[n + d], refs[2 * n + d]], count) for d in range(n)]
    vec_o, x_o, normed_o, packed_o, att_o, part_o, qkv_s = refs[3 * n :]
    low_col, me = pos[0] == 0, pos[1]
    small = refs[2 * n][count:, :].astype(WIDE)
    for d in range(1, n):
        small = small + refs[2 * n + d][count:, :].astype(WIDE)
    each = small.shape[0] // rows
    vec = jnp.concatenate([small[k * each : k * each + 6] for k in range(rows)], axis=1)
    vec_o[0:6, :] = vec
    lay_heads(qkv_s, sources, me, 4 * heads, rows)
    stream = lay_strips(low_col, lambda k: near[k, 0], lambda k: far[k, 0], rows)
    x_o[...] = stream
    scaled, _ = moments_of(stream.astype(WIDE))
    normed = (scaled * vec[0:1] + vec[1:2]).astype(LOW)
    normed_o[...] = normed
    span = heads * HD
    lines = span // width
    for part in range(3):
        total = dot_nt(normed[:, :width], qkv_s[0, part * span : (part + 1) * span, :])
        for k in range(1, rows):
            total = total + dot_nt(normed[:, k * width : (k + 1) * width], qkv_s[k, part * span : (part + 1) * span, :])
        if part != 1:
            line = 6 + (lines if part == 2 else 0)
            total = total + jnp.concatenate([small[line + i : line + i + 1] for i in range(lines)], axis=1)
        packed_o[:, part * span : (part + 1) * span] = total.astype(LOW)
    two = 2 * HD
    lane = lax.broadcasted_iota(jnp.int32, (1, two), 1)
    for pair in range(heads // 2):
        at = pair * two
        queries = packed_o[:, at : at + two]
        key_rows = packed_o[:, span + at : span + at + two]
        values = packed_o[:, 2 * span + at : 2 * span + at + two]
        halves = []
        for side in range(2):
            mask = (lane < HD) if side == 0 else (lane >= HD)
            probs = soft(dot_nt(jnp.where(mask, queries, jnp.zeros_like(queries)), key_rows))
            halves.append(dot_nn(probs.astype(LOW), values))
        att_o[:, at : at + two] = jnp.where(lane < HD, halves[0], halves[1]).astype(LOW)
    for k in range(rows):
        part_o[:, k * width : (k + 1) * width] = dot_nn(att_o[...], qkv_s[k, 3 * span :, :]).astype(LOW)


def row_blocks(ref, row, parts, rows):
    return [jnp.concatenate([ref[d, row ^ k] for d in range(parts)], axis=0) for k in range(rows)]


def feed_kernel(spec, pos, vec, small, x, part, came, near, far, up, down, *refs):
    parts, rows, width = spec
    mid, normed, dy, dy_sum_o, units_o, hid_o, unit_sum_o, top_o, far_o, back_o, mixed_s, back_s = refs
    low_col, row = pos[0] == 0, pos[2]
    step = pl.program_id(0)

    @pl.when(step == 0)
    def _():
        dy[...] = lay_strips(low_col, lambda k: near[k, 0], lambda k: far[k, 0], rows)
        dy_sum_o[...] = jnp.sum(dy[...].astype(WIDE), axis=0, keepdims=True)
        middle = x[...].astype(WIDE) + (part[...].astype(WIDE) + came[...].astype(WIDE) + vec[2:3, :])
        mid[...] = middle
        scaled, _ = moments_of(middle)
        normed[...] = (scaled * vec[3:4, :] + vec[4:5, :]).astype(LOW)
        mixed_s[...] = jnp.zeros_like(mixed_s)
        back_s[...] = jnp.zeros_like(back_s)

    up_rows, down_rows = row_blocks(up, row, parts, rows), row_blocks(down, row, parts, rows)
    hidden = dot_nt(normed[:, :width], up_rows[0])
    for k in range(1, rows):
        hidden = hidden + dot_nt(normed[:, k * width : (k + 1) * width], up_rows[k])
    active, slope = gelu_both(hidden + small[0])
    active = active.astype(LOW)
    units_o[0] = active
    grad = dot_nt(dy[:, :width], down_rows[0])
    for k in range(1, rows):
        grad = grad + dot_nt(dy[:, k * width : (k + 1) * width], down_rows[k])
    grad = (grad * slope).astype(LOW)
    hid_o[0] = grad
    unit_sum_o[0] = jnp.sum(grad.astype(WIDE), axis=0, keepdims=True)
    for k in range(rows):
        at = slice(k * width, (k + 1) * width)
        mixed_s[:, at] += dot_nn(active, down_rows[k])
        back_s[:, at] += dot_nn(grad, up_rows[k])

    @pl.when(step == pl.num_programs(0) - 1)
    def _():
        back_o[...] = back_s[...].astype(LOW)
        half = width // 2
        for k in range(rows):
            left, right = slice(k * width, k * width + half), slice(k * width + half, (k + 1) * width)
            base = mid[...] + vec[5:6, :]
            top_l, top_r = mixed_s[:, left] + base[:, left], mixed_s[:, right] + base[:, right]
            top_o[k] = jnp.where(low_col, top_l, top_r)
            far_o[k] = jnp.where(low_col, mixed_s[:, right], mixed_s[:, left]).astype(LOW)


def feed_grad_kernel(spec, pos, *refs):
    parts, rows, width = spec
    hids, units, normeds, dys, out = refs[0:2], refs[2:4], refs[4:6], refs[6:8], refs[8]
    row = pos[2]

    def write(left, right):
        total = dot_tn(left[0][0], right[0][...]) + dot_tn(left[1][0], right[1][...])
        block = total.shape[0] // parts
        for d in range(parts):
            for k in range(rows):
                out[d, row ^ k] = total[d * block : (d + 1) * block, k * width : (k + 1) * width].astype(LOW)

    half = pl.num_programs(0) // 2

    @pl.when(pl.program_id(0) < half)
    def _():
        write(hids, normeds)

    @pl.when(pl.program_id(0) >= half)
    def _():
        write(units, dys)


def second_kernel(spec, pos, vec, mid, back, came, dy, packed, *refs):
    n, rows, heads, width = spec
    count = 4 * heads * HD // n
    sources = [Source([refs[d], refs[n + d], refs[2 * n + d]], count) for d in range(n)]
    dmid_o, dz_o, dpacked_o, back_o, sums_o, psum_o, qkv_s, datt_s = refs[3 * n :]
    me = pos[1]
    lay_heads(qkv_s, sources, me, 4 * heads, rows)
    span = heads * HD
    grad_norm = back[...].astype(WIDE) + came[...].astype(WIDE)
    scaled, inv_std = moments_of(mid[...])
    dmid = dy[...].astype(WIDE) + norm_backward(grad_norm, scaled, inv_std, vec[3:4, :])
    dmid_o[...] = dmid
    dz = dmid.astype(LOW)
    dz_o[...] = dz
    sums_o[0:1, :] = jnp.sum(dz.astype(WIDE), axis=0, keepdims=True)
    sums_o[1:2, :] = jnp.sum(grad_norm * scaled, axis=0, keepdims=True)
    sums_o[2:3, :] = jnp.sum(grad_norm, axis=0, keepdims=True)
    total = dot_nt(dz[:, :width], qkv_s[0, 3 * span :, :])
    for k in range(1, rows):
        total = total + dot_nt(dz[:, k * width : (k + 1) * width], qkv_s[k, 3 * span :, :])
    datt_s[...] = total.astype(LOW)
    two = 2 * HD
    scale = 1.0 / math.sqrt(HD)
    lane = lax.broadcasted_iota(jnp.int32, (1, two), 1)
    for pair in range(heads // 2):
        at = pair * two
        queries = packed[:, at : at + two]
        key_rows = packed[:, span + at : span + at + two]
        values = packed[:, 2 * span + at : 2 * span + at + two]
        grads = datt_s[:, at : at + two]
        dqs, dks, dvs = [], [], []
        for side in range(2):
            mask = (lane < HD) if side == 0 else (lane >= HD)
            probs = soft(dot_nt(jnp.where(mask, queries, jnp.zeros_like(queries)), key_rows))
            dprobs = dot_nt(jnp.where(mask, grads, jnp.zeros_like(grads)), values)
            dscores = probs * (dprobs - jnp.sum(dprobs * probs, axis=-1, keepdims=True))
            dscores = dscores.astype(LOW)
            dqs.append(dot_nn(dscores, key_rows))
            dks.append(dot_tn(dscores, queries))
            dvs.append(dot_tn(probs.astype(LOW), grads))
        first = lane < HD
        dpacked_o[:, at : at + two] = (jnp.where(first, dqs[0], dqs[1]) * scale).astype(LOW)
        dpacked_o[:, span + at : span + at + two] = (jnp.where(first, dks[0], dks[1]) * scale).astype(LOW)
        dpacked_o[:, 2 * span + at : 2 * span + at + two] = jnp.where(first, dvs[0], dvs[1]).astype(LOW)
    psum_o[...] = jnp.sum(dpacked_o[...].astype(WIDE), axis=0, keepdims=True)
    for k in range(rows):
        back_o[:, k * width : (k + 1) * width] = dot_nn(dpacked_o[...], qkv_s[k, : 3 * span, :]).astype(LOW)


def attn_grad_kernel(spec, pos, *refs):
    n, rows, heads, width = spec
    dpacked, normed, att, dz = refs[0:2], refs[2:4], refs[4:6], refs[6:8]
    outs, total_s = refs[8 : 8 + n], refs[8 + n]
    me = pos[1]
    span = heads * HD
    own = HD // n
    for part in range(4):
        if part < 3:
            at = slice(part * span, (part + 1) * span)
            total = dot_tn(dpacked[0][:, at], normed[0][...]) + dot_tn(dpacked[1][:, at], normed[1][...])
        else:
            total = dot_tn(att[0][...], dz[0][...]) + dot_tn(att[1][...], dz[1][...])
        total_s[...] = total.astype(LOW)
        for d in range(n):
            place = me ^ d if n > 1 else 0
            for g in range(heads):
                line = g * HD + place * own
                if n > 1:
                    line = pl.multiple_of(line, own)
                value = total_s[pl.ds(line, own), :]
                to = (part * heads + g) * own
                for k in range(rows):
                    outs[d][k, to : to + own, :] = value[:, k * width : (k + 1) * width]


def gelu_both(values):
    tail = 0.5 * (1.0 + lax.erf(values * (1.0 / math.sqrt(2.0))))
    bell = jnp.exp(values * values * -0.5) * (1.0 / math.sqrt(2.0 * math.pi))
    return values * tail, tail + values * bell


def last_kernel(spec, pos, vec, *refs):
    rows, width, images = spec
    x, back, came, dmid = (refs[i * images : (i + 1) * images] for i in range(4))
    out_o, sums_o = refs[4 * images :]
    low_col = pos[0] == 0
    half = width // 2
    for i in range(images):
        scaled, inv_std = moments_of(x[i][...].astype(WIDE))
        grad_norm = back[i][...].astype(WIDE) + came[i][...].astype(WIDE)
        value = dmid[i][...] + norm_backward(grad_norm, scaled, inv_std, vec[0:1, :])
        gain_sum = jnp.sum(grad_norm * scaled, axis=0, keepdims=True)
        shift_sum = jnp.sum(grad_norm, axis=0, keepdims=True)
        if i == 0:
            sums_o[0:1, :] = gain_sum
            sums_o[1:2, :] = shift_sum
        else:
            sums_o[0:1, :] += gain_sum
            sums_o[1:2, :] += shift_sum
        for k in range(rows):
            left, right = value[:, k * width : k * width + half], value[:, k * width + half : (k + 1) * width]
            out_o[k, i] = jnp.where(low_col, left, right).astype(LOW)


ROOM = 56 * 1024 * 1024


def whole(array):
    zeros = (0,) * len(array.shape)
    return pl.BlockSpec(tuple(array.shape), lambda *_: zeros)


def run_kernel(body, args, outs, scratch=(), grid=None, in_specs=None, out_specs=None):
    if in_specs is None:
        in_specs = [pl.BlockSpec(memory_space=pltpu.SMEM)] + [whole(a) for a in args[1:]]
    if out_specs is None:
        out_specs = [whole(o) for o in outs]
    return pl.pallas_call(
        body,
        grid=grid or (1,),
        in_specs=in_specs,
        out_specs=out_specs,
        out_shape=outs,
        scratch_shapes=list(scratch),
        compiler_params=pltpu.CompilerParams(vmem_limit_bytes=ROOM),
        cost_estimate=pl.CostEstimate(flops=1024, bytes_accessed=1024, transcendentals=0),
    )(*args)


def shaped(shape, kind):
    return jax.ShapeDtypeStruct(shape, kind)


def on_device(
    tokens, cotangent, w_qkv, b_qkv, w_out, w_up, b_up, w_down, vectors,
    state_qkv, state_qkv_bias, state_out, state_up, state_up_bias, state_down, state_vectors,
):
    parts, rows = lax.axis_size("dp"), lax.axis_size("row")
    col, row_index, me = lax.axis_index("col"), lax.axis_index("row"), lax.axis_index("dp")
    low_col = col == 0
    width = w_qkv.shape[0]
    heads, chunk = w_qkv.shape[2], w_qkv.shape[3]
    groups = w_up.shape[1]
    strip = tokens.shape[1]
    images = tokens.shape[0] // (SEQ * rows)
    model = rows * width
    span = heads * HD
    pos = jnp.stack([col, me, row_index]).astype(jnp.int32)

    qkv_own = w_qkv.transpose(1, 2, 3, 0).reshape(-1, width)
    out_own = w_out.reshape(-1, width)
    up_own = w_up.transpose(1, 2, 0).reshape(-1, width)
    down_own = w_down.reshape(-1, width)
    qkv_count, unit_count = qkv_own.shape[0], up_own.shape[0]
    head_own = jnp.concatenate([qkv_own, out_own])
    head_count = head_own.shape[0]

    at_me = (jnp.arange(parts) == me)[:, None]
    vec_own = jnp.where(at_me, vectors[:, :, None, :], 0).reshape(6, -1)
    vec_far = swap(vec_own, "col", 1)
    vec_pair = jnp.stack([jnp.where(low_col, vec_own, vec_far), jnp.where(low_col, vec_far, vec_own)])
    bias_own = jnp.where(at_me, b_qkv[:, :, None, :], 0).reshape(-1, width)
    unit_own = jnp.where(at_me, b_up.reshape(1, -1), 0).reshape(-1, width)
    small_count = 6 + bias_own.shape[0] + unit_own.shape[0]
    small_each = small_count + -small_count % 16

    def to_send(stream, extra):
        blocks = stream.astype(LOW).reshape(rows, images, SEQ, strip)
        blocks = jnp.pad(blocks, ((0, 0), (0, 0), (0, PAD - SEQ), (0, 0)))
        if extra is not None:
            extra = jnp.pad(extra, ((0, 0), (0, 2), (0, 0)))
            blocks = jnp.concatenate([blocks, jnp.broadcast_to(extra, (rows, *extra.shape))], axis=2)
        return [lax.dynamic_index_in_dim(blocks, row_index ^ k, 0, False) for k in range(rows)]

    def send_images(blocks):
        return [blocks[0]] + [swap(block, "row", k) for k, block in enumerate(blocks) if k]

    def near_two(values):
        return [swap(values, "row", 1), swap(values, "row", 2)]

    token = [pos]

    def fence(*values):
        token[0], *values = lax.optimization_barrier((token[0], *values))
        return values

    assert rows == 4 and images == 2 and lax.axis_size("col") == 2
    feed_all = lax.all_gather(jnp.concatenate([up_own, down_own]), ("dp", "row"), axis=0).reshape(parts, rows, -1, width)
    head_two = near_two(head_own)
    head_x = across(head_own)
    head_plane = planes(head_own)
    token_blocks, dy_blocks = to_send(tokens, vec_pair), to_send(cotangent, None)
    small_same = jnp.pad(jnp.concatenate([bias_own, unit_own]), ((6, small_each - small_count), (0, 0)))
    head_two, head_x, head_plane, token_blocks = fence(head_two, head_x, head_plane, token_blocks)

    head_three = swap(head_two[1], "row", 1)
    came = send_images(token_blocks)
    head_pair = jnp.concatenate(head_two)
    head_pair_x = across(head_pair)
    head_three, came, head_pair_x, head_pair, head_x = fence(head_three, came, head_pair_x, head_pair, head_x)

    small_rows = jnp.stack([jnp.concatenate([b[0, PAD : PAD + 6], b[1, PAD : PAD + 6]], axis=1) for b in came])
    small_rows = jnp.pad(small_rows, ((0, 0), (0, small_each - 6), (0, 0))) + small_same
    head_third = jnp.concatenate([head_three, small_rows.reshape(-1, width)])
    near = jnp.stack([block[:, :PAD] for block in came])
    far = swap(near, "col", 1)
    head_third_x = across(head_third)
    head_own_planes = [*head_plane, *planes(head_x)]
    head_pair_planes = [*planes(head_pair), *planes(head_pair_x)]
    dy_came = send_images(dy_blocks)
    head_third_x, head_third, head_own_planes, head_pair_planes, far, near, dy_came = fence(
        head_third_x, head_third, head_own_planes, head_pair_planes, far, near, dy_came
    )

    head_third_planes = [*planes(head_third), *planes(head_third_x)]

    split = chunk % 16 == 0
    n = parts if split else 1
    head_weights = [*head_own_planes, *head_pair_planes, *head_third_planes]
    if not split:
        def merge(blocks, lead):
            both = xor_order(jnp.stack(blocks), 0, "dp").reshape(parts, lead, blocks[0].shape[0] // lead, width)
            return both.transpose(1, 0, 2, 3).reshape(-1, width)

        def merge_some(blocks, count, lead, number):
            return [merge([b[k * count : (k + 1) * count] for b in blocks], lead) for k in range(number)]

        small_sum = sum(b[head_count:].astype(WIDE) for b in head_third_planes).astype(LOW)
        head_weights = [
            merge(head_own_planes, 4 * heads),
            jnp.concatenate(merge_some(head_pair_planes, head_count, 4 * heads, 2)),
            jnp.concatenate([*merge_some(head_third_planes, head_count, 4 * heads, 1), small_sum]),
        ]
    head_small = [b[head_count * parts // n :] for b in head_weights[2 * n :]]
    scalars = pl.BlockSpec(memory_space=pltpu.SMEM)
    head_specs = [pl.BlockSpec((head_count * parts // n, width), lambda *_: (0, 0))] * n + [whole(w) for w in head_weights[n:]]
    full, low_full = shaped((PAD, model), WIDE), shaped((PAD, model), LOW)

    def forward_one(i):
        strips = pl.BlockSpec((rows, 1, PAD, strip), lambda *_: (0, i, 0, 0))
        outs = [
            shaped((8, model), WIDE),
            low_full,
            low_full,
            shaped((PAD, 3 * span), LOW),
            shaped((PAD, span), LOW),
            low_full,
        ]
        return run_kernel(
            functools.partial(first_kernel, (n, rows, heads, width)),
            (token[0], near, far, *head_weights),
            outs,
            scratch=[pltpu.VMEM((rows, 4 * span, width), LOW)],
            in_specs=[scalars, strips, strips, *head_specs],
        )

    near_dy = jnp.stack(dy_came)
    far_dy = swap(near_dy, "col", 1)
    done = [forward_one(0)]
    done, far_dy, near_dy = fence(done, far_dy, near_dy)

    came_one = [swap(done[0][5], "col", 1)]
    done.append(forward_one(1))
    vec = done[0][0]
    unit_rows = sum(b[6 + bias_own.shape[0] :][: unit_own.shape[0]].astype(WIDE) for b in head_small)
    steps = 4
    block = unit_count // steps
    unit_rows = unit_rows.reshape(parts, steps, block).transpose(1, 0, 2).reshape(steps, 1, parts * block)
    done, came_one, unit_rows = fence(done, came_one, unit_rows)

    came_one = [*came_one, swap(done[1][5], "col", 1)]

    unit_spec = pl.BlockSpec((1, PAD, parts * block), lambda u: (u, 0, 0))
    unit_sum_spec = pl.BlockSpec((1, 1, parts * block), lambda u: (u, 0, 0))
    unit_shape = (steps, PAD, parts * block)

    def feed_one(i):
        strips = pl.BlockSpec((rows, 1, PAD, strip), lambda *_: (0, i, 0, 0))
        outs = [
            full,
            low_full,
            low_full,
            shaped((1, model), WIDE),
            shaped(unit_shape, LOW),
            shaped(unit_shape, LOW),
            shaped((steps, 1, parts * block), WIDE),
            shaped((rows, PAD, strip), WIDE),
            shaped((rows, PAD, strip), LOW),
            low_full,
        ]
        out_specs = [whole(o) for o in outs]
        out_specs[4], out_specs[5], out_specs[6] = unit_spec, unit_spec, unit_sum_spec
        acts = (done[i][1], done[i][5], came_one[i])
        return run_kernel(
            functools.partial(feed_kernel, (parts, rows, width)),
            (token[0], vec, unit_rows, *acts, near_dy, far_dy, feed_all, feed_all),
            outs,
            scratch=[pltpu.VMEM((PAD, model), WIDE), pltpu.VMEM((PAD, model), WIDE)],
            grid=(steps,),
            in_specs=[
                scalars, whole(vec), unit_sum_spec, *[whole(a) for a in acts], strips, strips,
                pl.BlockSpec((parts, rows, block, width), lambda u: (0, 0, u, 0)),
                pl.BlockSpec((parts, rows, block, width), lambda u: (0, 0, u + steps, 0)),
            ],
            out_specs=out_specs,
        )

    fed = [feed_one(0)]
    fed, came_one = fence(fed, came_one)
    came_two = [swap(fed[0][9], "col", 1)]
    fed.append(feed_one(1))
    fed, came_two = fence(fed, came_two)

    came_two = [*came_two, swap(fed[1][9], "col", 1)]
    early = pl.BlockSpec((1, PAD, parts * block), lambda u: (jnp.minimum(u, steps - 1), 0, 0))
    late = pl.BlockSpec((1, PAD, parts * block), lambda u: (jnp.maximum(u - steps, 0), 0, 0))
    feed_grad = run_kernel(
        functools.partial(feed_grad_kernel, (parts, rows, width)),
        (token[0], *[f[5] for f in fed], *[f[4] for f in fed], *[f[1] for f in fed], *[f[2] for f in fed]),
        [shaped((parts, rows, 2 * unit_count, width), LOW)],
        grid=(2 * steps,),
        in_specs=[scalars, early, early, late, late, *[whole(low_full)] * 4],
        out_specs=[pl.BlockSpec((parts, rows, block, width), lambda u: (0, 0, u, 0))],
    )[0]
    feed_grad, fed = fence(feed_grad, fed)
    feed_total = lax.psum_scatter(feed_grad.reshape(-1, width), ("dp", "row"), scatter_dimension=0, tiled=True)

    def fold(blocks):
        held = dict(enumerate(blocks))
        for bit in bits_of("dp")[:-1]:
            held = join(held, "dp", bit)
        return held[0]

    def ordered(blocks, lead):
        if n == parts:
            return blocks
        both = blocks[0].reshape(rows, lead, parts, -1, width).transpose(2, 0, 1, 3, 4)
        both = xor_order(both.reshape(parts, rows, -1, width), 0, "dp")
        return [both[d] for d in range(parts)]

    half_rows = rows // 2

    def sum_high(near_sum, came_part):
        return [add_low(near_sum[half_rows + k], came_part[k]) for k in range(half_rows)]

    def sum_low(near_sum, came_part):
        return [add_low(near_sum[k], came_part[k]) for k in range(half_rows)]

    def from_images(strips):
        came = [strips[0]] + [swap(strips[k], "row", k) for k in range(1, rows)]
        stacked = xor_order(jnp.stack(came)[:, :, :SEQ], 0, "row")
        return stacked.reshape(-1, strip).astype(WIDE)

    def backward_one(i):
        outs = [full, low_full, shaped((PAD, 3 * span), LOW), low_full, shaped((8, model), WIDE), shaped((1, 3 * span), WIDE)]
        acts = (vec, fed[i][0], fed[i][9], came_two[i], fed[i][2], done[i][3])
        return run_kernel(
            functools.partial(second_kernel, (n, rows, heads, width)),
            (token[0], *acts, *head_weights),
            outs,
            scratch=[pltpu.VMEM((rows, 4 * span, width), LOW), pltpu.VMEM((PAD, span), LOW)],
            in_specs=[scalars, *[whole(a) for a in acts], *head_specs],
        )

    top_far = swap(jnp.stack([f[8] for f in fed]), "col", 1)
    returned = [backward_one(0)]
    returned, top_far = fence(returned, top_far)

    came_three = [swap(returned[0][3], "col", 1)]
    top = jnp.stack([f[7] + t.astype(WIDE) for f, t in zip(fed, top_far)], axis=1).astype(LOW)
    result = from_images(top)
    returned.append(backward_one(1))
    returned, came_three, result = fence(returned, came_three, result)

    came_three = [*came_three, swap(returned[1][3], "col", 1)]
    attn_grad = run_kernel(
        functools.partial(attn_grad_kernel, (n, rows, heads, width)),
        (
            token[0], *[r[2] for r in returned], *[d[2] for d in done], *[d[4] for d in done], *[r[1] for r in returned],
        ),
        [shaped((rows, head_count * parts // n, width), LOW) for _ in range(n)],
        scratch=[pltpu.VMEM((span, model), LOW)],
    )
    attn_grad, came_three = fence(attn_grad, came_three)

    attn_blocks = ordered(attn_grad, 4 * heads)
    attn_far, attn_near = fold(attn_blocks[parts // 2 :]), fold(attn_blocks[: parts // 2])
    grad_strips, sums_one = run_kernel(
        functools.partial(last_kernel, (rows, width, images)),
        (
            token[0], vec, *[d[1] for d in done], *[r[3] for r in returned], *came_three, *[r[0] for r in returned],
        ),
        [shaped((rows, images, PAD, strip), LOW), shaped((8, model), WIDE)],
    )
    attn_far, attn_near, grad_strips, sums_one = fence(attn_far, attn_near, grad_strips, sums_one)

    grad_scale = grad_gain / math.sqrt(tokens.shape[0] * parts)

    lanes = max(unit_count, 2 * heads * chunk, 12 * chunk)
    tiny = run_kernel(
        functools.partial(collect_kernel, (rows, heads, chunk, parts, width, images)),
        (
            token[0], sums_one, *[r[4] for r in returned],
            *[f[3] for f in fed], *[r[5] for r in returned], *[f[6] for f in fed],
        ),
        [shaped((parts, 8, lanes), WIDE)],
    )[0]
    attn_high = across(attn_far[half_rows:])
    tiny = functools.reduce(lambda a, b: a + b, [tiny[0]] + [swap(tiny[d], "dp", d) for d in range(1, parts)])
    def adam(reduced, owns, states, ranges):
        first, pieces = reduced
        outs = []
        for size, _ in ranges:
            outs += [shaped((size, width), WIDE), shaped((size, width), WIDE), shaped((2, size, width), WIDE)]
        args = (first, *pieces, *owns, *states)
        return run_kernel(
            functools.partial(adam_kernel, (len(pieces), [r[0] for r in ranges], grad_scale)),
            args,
            outs,
            in_specs=[whole(a) for a in args],
        )

    state_rows = lambda a, order: a.transpose(order).reshape(2, -1, width)
    out_count = out_own.shape[0]
    attn_high, attn_far, attn_near, grad_strips, tiny = fence(attn_high, attn_far, attn_near, grad_strips, tiny)

    attn_low = across(attn_far[:half_rows])
    attn_two, attn_three = sum_high(attn_near, attn_high)
    attn_three = swap(attn_three, "row", 1)
    grad_tokens = from_images(grad_strips)
    attn_low, attn_two, attn_three, attn_near, grad_tokens, tiny = fence(
        attn_low, attn_two, attn_three, attn_near, grad_tokens, tiny
    )

    attn_zero, attn_one = sum_low(attn_near, attn_low)
    attn_one = swap(attn_one, "row", 1)
    attn_two = swap(add_low(attn_two, attn_three), "row", 2)
    tiny = (tiny + swap(tiny, "row", 1)) + (swap(tiny, "row", 2) + swap(tiny, "row", 3))
    attn_zero, attn_one, attn_two, tiny = fence(attn_zero, attn_one, attn_two, tiny)
    feed_done = adam(
        (feed_total, []),
        [up_own, down_own],
        [state_rows(state_up, (0, 2, 3, 1)), state_rows(state_down, (0, 1, 2, 3))],
        [(unit_count, 0), (unit_count, 0)],
    )

    flat_up = lambda a: jnp.swapaxes(a, -1, -2)
    small_args = (b_qkv, flat_up(b_up), vectors, state_qkv_bias, flat_up(state_up_bias), state_vectors)
    small_kinds = (b_qkv.shape, flat_up(b_up).shape, vectors.shape)
    small_done = run_kernel(
        functools.partial(small_adam_kernel, (heads, groups, chunk, grad_scale)),
        (token[0], tiny, *small_args),
        [shaped(k, WIDE) for k in (*small_kinds, *small_kinds)] + [shaped((2, *k), WIDE) for k in small_kinds],
    )

    attn_done = adam(
        (attn_zero, [attn_one, attn_two]),
        [qkv_own, out_own],
        [state_rows(state_qkv, (0, 2, 3, 4, 1)), state_rows(state_out, (0, 1, 2, 3))],
        [(qkv_count, 0), (out_count, 0)],
    )

    def shape_all(which):
        lead = (2,) if which == 2 else ()
        more = (0,) if which == 2 else ()
        move = lambda order: (*more, *[o + len(lead) for o in order])
        return (
            attn_done[which].reshape(*lead, 3, heads, chunk, width).transpose(move((3, 0, 1, 2))),
            small_done[3 * which],
            attn_done[3 + which].reshape(*lead, *w_out.shape),
            feed_done[which].reshape(*lead, groups, chunk, width).transpose(move((2, 0, 1))),
            flat_up(small_done[3 * which + 1]),
            feed_done[3 + which].reshape(*lead, *w_down.shape),
            small_done[3 * which + 2],
        )

    return (result, grad_tokens, *shape_all(0), *shape_all(1), *shape_all(2))


def solution(mesh):
    placed = (
        P("dp", ("row", "col")),
        P("dp", ("row", "col")),
        P("row", None, "col", "dp"),
        P(None, "col", "dp"),
        P("col", "dp", "row"),
        P("row", "col", "dp"),
        P("col", "dp"),
        P("col", "dp", "row"),
        P(None, ("row", "col"), "dp"),
        P(None, "row", None, "col", "dp"),
        P(None, None, "col", "dp"),
        P(None, "col", "dp", "row"),
        P(None, "row", "col", "dp"),
        P(None, "col", "dp"),
        P(None, "col", "dp", "row"),
        P(None, None, ("row", "col"), "dp"),
    )
    params = placed[2:9]
    return jax.shard_map(
        on_device,
        mesh=mesh,
        in_specs=placed,
        out_specs=(placed[0], placed[0], *params, *params, *placed[9:]),
        check_vma=False,
    )
```

```python
import functools
import math

import jax
import jax.numpy as jnp
from jax import lax
from jax.experimental import pallas as pl
from jax.experimental.pallas import tpu as pltpu
from jax.sharding import PartitionSpec as P

HD = 64
SEQ = 197
PAD = 208
STEP = 10

norm_eps = 1e-06
beta_first = 0.9
beta_second = 0.999
learn_rate = 0.01
weight_decay = 0.05
adam_eps = 1e-08
grad_gain = 32.0

LOW = jnp.bfloat16
WIDE = jnp.float32


def swap(values, name, bit):
    count = lax.axis_size(name)
    return lax.ppermute(values, name, [(i, i ^ bit) for i in range(count)])


def bits_of(name):
    bits, bit = [], 1
    while bit < lax.axis_size(name):
        bits.append(bit)
        bit *= 2
    return bits


def after(value, *others):
    return lax.optimization_barrier((value, *others))[0]


def planes(values):
    blocks = {0: values}
    for bit in reversed(bits_of("dp")[:-1]):
        for place in list(blocks):
            blocks[place ^ bit] = swap(blocks[place], "dp", bit)
    return [blocks[d] for d in range(len(blocks))]


def across(values):
    return swap(values, "dp", lax.axis_size("dp") // 2)


def add_low(left, right):
    return (left.astype(WIDE) + right.astype(WIDE)).astype(left.dtype)


def join(held, name, bit):
    return {d: add_low(held[d], swap(held[d ^ bit], name, bit)) for d in held if not d & bit}


def scatter(blocks, name):
    held = dict(enumerate(blocks))
    for bit in bits_of(name):
        held = join(held, name, bit)
    return held[0]


def xor_order(values, axis, name):
    mine = lax.axis_index(name)
    shape = values.shape
    for bit in bits_of(name):
        split = values.reshape(shape[:axis] + (shape[axis] // (2 * bit), 2, bit) + shape[axis + 1 :])
        flipped = jnp.flip(split, axis + 1)
        values = jnp.where((mine & bit) > 0, flipped, split).reshape(shape)
    return values


def adam_step(weight_old, gradient, first_old, second_old, decay_on):
    first_moment = beta_first * first_old + (1.0 - beta_first) * gradient
    second_moment = beta_second * second_old + (1.0 - beta_second) * gradient * gradient
    first_hat = first_moment / (1.0 - beta_first**STEP)
    second_hat = second_moment / (1.0 - beta_second**STEP)
    change = -learn_rate * (first_hat / (jnp.sqrt(second_hat) + adam_eps) + decay_on * weight_old)
    return change, first_moment, second_moment


def adam_kernel(spec, first, *refs):
    count, sizes, grad_scale = spec
    pieces, refs = refs[:count], refs[count:]
    weights, states, outs = refs[: len(sizes)], refs[len(sizes) : 2 * len(sizes)], refs[2 * len(sizes) :]
    at = 0
    for i, size in enumerate(sizes):
        lines = slice(at, at + size)
        at += size
        total = first[lines].astype(WIDE)
        for piece in pieces:
            total = total + piece[lines].astype(WIDE)
        gradient = total * grad_scale
        change, low_moment, high_moment = adam_step(
            weights[i][...].astype(WIDE), gradient, states[i][0], states[i][1], weight_decay
        )
        outs[3 * i][...] = gradient
        outs[3 * i + 1][...] = change
        outs[3 * i + 2][0] = low_moment
        outs[3 * i + 2][1] = high_moment


def collect_kernel(spec, pos, ones, *refs):
    rows, heads, chunk, parts, width, images = spec
    twos, dys, packs, refs = refs[:images], refs[images : 2 * images], refs[2 * images : 3 * images], refs[3 * images :]
    units, out, = refs[:-1], refs[-1]
    low_col, me, row = pos[0] == 0, pos[1], pos[2]
    out[...] = jnp.zeros_like(out)
    add = lambda items: functools.reduce(lambda a, b: a + b, items)
    two = add([t[0:3, :] for t in twos])
    lines = [ones[0:1, :], ones[1:2, :], two[0:1], two[1:2], two[2:3], add([d[...] for d in dys])]
    pack = add([p[...] for p in packs])
    span = heads * HD
    half = width // 2
    unit_total = add([u[...] for u in units])
    each = unit_total.shape[2] // parts
    def put(d, line, pieces):
        value = jnp.concatenate(pieces, axis=1)
        short = out.shape[2] - value.shape[1]
        if short:
            value = jnp.concatenate([value, jnp.zeros((1, short), WIDE)], axis=1)
        out[pl.ds(d, 1), pl.ds(line, 1), :] = value[None]

    for owner in range(parts):
        d = me ^ owner
        spots = [part * span + h * HD + owner * chunk for part in (0, 2) for h in range(heads)]
        put(d, 0, [pack[:, at : at + chunk] for at in spots])
        put(d, 1, [unit_total[u][:, owner * each : (owner + 1) * each] for u in range(unit_total.shape[0])])
        for k in range(rows):
            pieces = []
            for v in range(6):
                for j in range(2):
                    at = k * width + j * HD + owner * chunk
                    near, far = lines[v][:, at : at + chunk], lines[v][:, at + half : at + half + chunk]
                    pieces.append(jnp.where(low_col, near, far))
            put(d, 4 + (row ^ k), pieces)


def small_adam_kernel(spec, pos, tiny, *refs):
    heads, groups, chunk, grad_scale = spec
    row = pos[2]
    weights, states, grads, changes, fresh = (refs[3 * i : 3 * i + 3] for i in range(5))
    for part in range(2):
        for h in range(heads):
            at = (part * heads + h) * chunk
            grads[0][part, h : h + 1, :] = tiny[0:1, at : at + chunk] * grad_scale
    side = lax.broadcasted_iota(jnp.int32, (groups, chunk), 0)
    table = jnp.zeros((groups, chunk), WIDE)
    for g in range(groups):
        table = jnp.where(side == g, tiny[1:2, g * chunk : (g + 1) * chunk], table)
    grads[1][...] = table.T * grad_scale
    mine = tiny[pl.ds(4 + row, 1), :] * grad_scale
    for v in range(6):
        for j in range(2):
            at = (v * 2 + j) * chunk
            grads[2][v, j : j + 1, :] = mine[:, at : at + chunk]
    for i in range(3):
        change, low_moment, high_moment = adam_step(weights[i][...].astype(WIDE), grads[i][...], states[i][0], states[i][1], 0.0)
        changes[i][...] = change
        fresh[i][0] = low_moment
        fresh[i][1] = high_moment


def dot_nt(left, right):
    return lax.dot_general(left, right, (((1,), (1,)), ((), ())), preferred_element_type=WIDE)


def dot_nn(left, right):
    return lax.dot_general(left, right, (((1,), (0,)), ((), ())), preferred_element_type=WIDE)


def dot_tn(left, right):
    return lax.dot_general(left, right, (((0,), (0,)), ((), ())), preferred_element_type=WIDE)


def moments_of(stream):
    center = jnp.mean(stream, axis=-1, keepdims=True)
    offset = stream - center
    inv_std = lax.rsqrt(jnp.mean(offset * offset, axis=-1, keepdims=True) + norm_eps)
    return offset * inv_std, inv_std


def norm_backward(grad_norm, scaled, inv_std, gain):
    weighted = grad_norm * gain
    return inv_std * (
        weighted
        - jnp.mean(weighted, axis=-1, keepdims=True)
        - scaled * jnp.mean(weighted * scaled, axis=-1, keepdims=True)
    )


def lay_strips(low_col, near, far, rows):
    pieces = []
    for k in range(rows):
        mine, other = near(k), far(k)
        pieces.append(jnp.where(low_col, mine, other))
        pieces.append(jnp.where(low_col, other, mine))
    return jnp.concatenate(pieces, axis=1)


def soft(scores):
    lane = lax.broadcasted_iota(jnp.int32, scores.shape, 1)
    scores = jnp.where(lane < SEQ, scores * (1.0 / math.sqrt(HD)), -1e30)
    raised = jnp.exp(scores - jnp.max(scores, axis=-1, keepdims=True))
    return raised * (1.0 / jnp.sum(raised, axis=-1, keepdims=True))


class Source:
    def __init__(self, refs, count):
        self.refs, self.count = refs, count

    def block(self, k, first, size):
        at = first + (self.count if k == 2 else 0)
        return self.refs[(k + 1) // 2][at : at + size, :]


def lay_heads(target, sources, me, groups, rows):
    own = HD // len(sources)
    for k in range(rows):
        for d, source in enumerate(sources):
            place = me ^ d if len(sources) > 1 else 0
            for g in range(groups):
                at = g * HD + place * own
                if len(sources) > 1:
                    at = pl.multiple_of(at, own)
                target[k, pl.ds(at, own), :] = source.block(k, g * own, own)


def first_kernel(spec, pos, near, far, *refs):
    n, rows, heads, width = spec
    count = 4 * heads * HD // n
    sources = [Source([refs[d], refs[n + d], refs[2 * n + d]], count) for d in range(n)]
    vec_o, x_o, normed_o, packed_o, att_o, part_o, qkv_s = refs[3 * n :]
    low_col, me = pos[0] == 0, pos[1]
    small = refs[2 * n][count:, :].astype(WIDE)
    for d in range(1, n):
        small = small + refs[2 * n + d][count:, :].astype(WIDE)
    each = small.shape[0] // rows
    vec = jnp.concatenate([small[k * each : k * each + 6] for k in range(rows)], axis=1)
    vec_o[0:6, :] = vec
    lay_heads(qkv_s, sources, me, 4 * heads, rows)
    stream = lay_strips(low_col, lambda k: near[k, 0], lambda k: far[k, 0], rows)
    x_o[...] = stream
    scaled, _ = moments_of(stream.astype(WIDE))
    normed = (scaled * vec[0:1] + vec[1:2]).astype(LOW)
    normed_o[...] = normed
    span = heads * HD
    lines = span // width
    for part in range(3):
        total = dot_nt(normed[:, :width], qkv_s[0, part * span : (part + 1) * span, :])
        for k in range(1, rows):
            total = total + dot_nt(normed[:, k * width : (k + 1) * width], qkv_s[k, part * span : (part + 1) * span, :])
        if part != 1:
            line = 6 + (lines if part == 2 else 0)
            total = total + jnp.concatenate([small[line + i : line + i + 1] for i in range(lines)], axis=1)
        packed_o[:, part * span : (part + 1) * span] = total.astype(LOW)
    two = 2 * HD
    lane = lax.broadcasted_iota(jnp.int32, (1, two), 1)
    for pair in range(heads // 2):
        at = pair * two
        queries = packed_o[:, at : at + two]
        key_rows = packed_o[:, span + at : span + at + two]
        values = packed_o[:, 2 * span + at : 2 * span + at + two]
        halves = []
        for side in range(2):
            mask = (lane < HD) if side == 0 else (lane >= HD)
            probs = soft(dot_nt(jnp.where(mask, queries, jnp.zeros_like(queries)), key_rows))
            halves.append(dot_nn(probs.astype(LOW), values))
        att_o[:, at : at + two] = jnp.where(lane < HD, halves[0], halves[1]).astype(LOW)
    for k in range(rows):
        part_o[:, k * width : (k + 1) * width] = dot_nn(att_o[...], qkv_s[k, 3 * span :, :]).astype(LOW)


def row_blocks(ref, row, parts, rows):
    return [jnp.concatenate([ref[d, row ^ k] for d in range(parts)], axis=0) for k in range(rows)]


def feed_kernel(spec, pos, vec, small, x, part, came, near, far, up, down, *refs):
    parts, rows, width = spec
    mid, normed, dy, dy_sum_o, units_o, hid_o, unit_sum_o, top_o, far_o, back_o, mixed_s, back_s = refs
    low_col, row = pos[0] == 0, pos[2]
    step = pl.program_id(0)

    @pl.when(step == 0)
    def _():
        dy[...] = lay_strips(low_col, lambda k: near[k, 0], lambda k: far[k, 0], rows)
        dy_sum_o[...] = jnp.sum(dy[...].astype(WIDE), axis=0, keepdims=True)
        middle = x[...].astype(WIDE) + (part[...].astype(WIDE) + came[...].astype(WIDE) + vec[2:3, :])
        mid[...] = middle
        scaled, _ = moments_of(middle)
        normed[...] = (scaled * vec[3:4, :] + vec[4:5, :]).astype(LOW)
        mixed_s[...] = jnp.zeros_like(mixed_s)
        back_s[...] = jnp.zeros_like(back_s)

    up_rows, down_rows = row_blocks(up, row, parts, rows), row_blocks(down, row, parts, rows)
    hidden = dot_nt(normed[:, :width], up_rows[0])
    for k in range(1, rows):
        hidden = hidden + dot_nt(normed[:, k * width : (k + 1) * width], up_rows[k])
    active, slope = gelu_both(hidden + small[0])
    active = active.astype(LOW)
    units_o[0] = active
    grad = dot_nt(dy[:, :width], down_rows[0])
    for k in range(1, rows):
        grad = grad + dot_nt(dy[:, k * width : (k + 1) * width], down_rows[k])
    grad = (grad * slope).astype(LOW)
    hid_o[0] = grad
    unit_sum_o[0] = jnp.sum(grad.astype(WIDE), axis=0, keepdims=True)
    for k in range(rows):
        at = slice(k * width, (k + 1) * width)
        mixed_s[:, at] += dot_nn(active, down_rows[k])
        back_s[:, at] += dot_nn(grad, up_rows[k])

    @pl.when(step == pl.num_programs(0) - 1)
    def _():
        back_o[...] = back_s[...].astype(LOW)
        half = width // 2
        for k in range(rows):
            left, right = slice(k * width, k * width + half), slice(k * width + half, (k + 1) * width)
            base = mid[...] + vec[5:6, :]
            top_l, top_r = mixed_s[:, left] + base[:, left], mixed_s[:, right] + base[:, right]
            top_o[k] = jnp.where(low_col, top_l, top_r)
            far_o[k] = jnp.where(low_col, mixed_s[:, right], mixed_s[:, left]).astype(LOW)


def feed_grad_kernel(spec, pos, *refs):
    parts, rows, width, groups = spec
    hids, units, normeds, dys, out = refs[0:2], refs[2:4], refs[4:6], refs[6:8], refs[8]
    row = pos[2]

    def write(left, right):
        wide = [jnp.concatenate([ref[g] for g in range(groups)], axis=1) for ref in left]
        total = dot_tn(jnp.concatenate(wide, axis=0), jnp.concatenate([ref[...] for ref in right], axis=0))
        block = total.shape[0] // (groups * parts)
        for g in range(groups):
            for d in range(parts):
                at = (g * parts + d) * block
                for k in range(rows):
                    value = total[at : at + block, k * width : (k + 1) * width]
                    out[d, row ^ k, g * block : (g + 1) * block, :] = value.astype(LOW)

    half = pl.num_programs(0) // 2

    @pl.when(pl.program_id(0) < half)
    def _():
        write(hids, normeds)

    @pl.when(pl.program_id(0) >= half)
    def _():
        write(units, dys)


def second_kernel(spec, pos, vec, mid, back, came, dy, packed, *refs):
    n, rows, heads, width = spec
    count = 4 * heads * HD // n
    sources = [Source([refs[d], refs[n + d], refs[2 * n + d]], count) for d in range(n)]
    dmid_o, dz_o, dpacked_o, back_o, sums_o, psum_o, qkv_s, datt_s = refs[3 * n :]
    me = pos[1]
    lay_heads(qkv_s, sources, me, 4 * heads, rows)
    span = heads * HD
    grad_norm = back[...].astype(WIDE) + came[...].astype(WIDE)
    scaled, inv_std = moments_of(mid[...])
    dmid = dy[...].astype(WIDE) + norm_backward(grad_norm, scaled, inv_std, vec[3:4, :])
    dmid_o[...] = dmid
    dz = dmid.astype(LOW)
    dz_o[...] = dz
    sums_o[0:1, :] = jnp.sum(dz.astype(WIDE), axis=0, keepdims=True)
    sums_o[1:2, :] = jnp.sum(grad_norm * scaled, axis=0, keepdims=True)
    sums_o[2:3, :] = jnp.sum(grad_norm, axis=0, keepdims=True)
    total = dot_nt(dz[:, :width], qkv_s[0, 3 * span :, :])
    for k in range(1, rows):
        total = total + dot_nt(dz[:, k * width : (k + 1) * width], qkv_s[k, 3 * span :, :])
    datt_s[...] = total.astype(LOW)
    two = 2 * HD
    scale = 1.0 / math.sqrt(HD)
    lane = lax.broadcasted_iota(jnp.int32, (1, two), 1)
    for pair in range(heads // 2):
        at = pair * two
        queries = packed[:, at : at + two]
        key_rows = packed[:, span + at : span + at + two]
        values = packed[:, 2 * span + at : 2 * span + at + two]
        grads = datt_s[:, at : at + two]
        dqs, dks, dvs = [], [], []
        for side in range(2):
            mask = (lane < HD) if side == 0 else (lane >= HD)
            probs = soft(dot_nt(jnp.where(mask, queries, jnp.zeros_like(queries)), key_rows))
            dprobs = dot_nt(jnp.where(mask, grads, jnp.zeros_like(grads)), values)
            dscores = probs * (dprobs - jnp.sum(dprobs * probs, axis=-1, keepdims=True))
            dscores = dscores.astype(LOW)
            dqs.append(dot_nn(dscores, key_rows))
            dks.append(dot_tn(dscores, queries))
            dvs.append(dot_tn(probs.astype(LOW), grads))
        first = lane < HD
        dpacked_o[:, at : at + two] = (jnp.where(first, dqs[0], dqs[1]) * scale).astype(LOW)
        dpacked_o[:, span + at : span + at + two] = (jnp.where(first, dks[0], dks[1]) * scale).astype(LOW)
        dpacked_o[:, 2 * span + at : 2 * span + at + two] = jnp.where(first, dvs[0], dvs[1]).astype(LOW)
    psum_o[...] = jnp.sum(dpacked_o[...].astype(WIDE), axis=0, keepdims=True)
    for k in range(rows):
        back_o[:, k * width : (k + 1) * width] = dot_nn(dpacked_o[...], qkv_s[k, : 3 * span, :]).astype(LOW)


def attn_grad_kernel(spec, pos, *refs):
    n, rows, heads, width = spec
    dpacked, normed, att, dz = refs[0:2], refs[2:4], refs[4:6], refs[6:8]
    outs, total_s = refs[8 : 8 + n], refs[8 + n]
    me = pos[1]
    span = heads * HD
    own = HD // n
    for part in range(4):
        if part < 3:
            at = slice(part * span, (part + 1) * span)
            total = dot_tn(dpacked[0][:, at], normed[0][...]) + dot_tn(dpacked[1][:, at], normed[1][...])
        else:
            total = dot_tn(att[0][...], dz[0][...]) + dot_tn(att[1][...], dz[1][...])
        total_s[...] = total.astype(LOW)
        for d in range(n):
            place = me ^ d if n > 1 else 0
            for g in range(heads):
                line = g * HD + place * own
                if n > 1:
                    line = pl.multiple_of(line, own)
                value = total_s[pl.ds(line, own), :]
                to = (part * heads + g) * own
                for k in range(rows):
                    outs[d][k, to : to + own, :] = value[:, k * width : (k + 1) * width]


def gelu_both(values):
    tail = 0.5 * (1.0 + lax.erf(values * (1.0 / math.sqrt(2.0))))
    bell = jnp.exp(values * values * -0.5) * (1.0 / math.sqrt(2.0 * math.pi))
    return values * tail, tail + values * bell


def last_kernel(spec, pos, vec, *refs):
    rows, width, images = spec
    x, back, came, dmid = (refs[i * images : (i + 1) * images] for i in range(4))
    out_o, sums_o = refs[4 * images :]
    low_col = pos[0] == 0
    half = width // 2
    for i in range(images):
        scaled, inv_std = moments_of(x[i][...].astype(WIDE))
        grad_norm = back[i][...].astype(WIDE) + came[i][...].astype(WIDE)
        value = dmid[i][...] + norm_backward(grad_norm, scaled, inv_std, vec[0:1, :])
        gain_sum = jnp.sum(grad_norm * scaled, axis=0, keepdims=True)
        shift_sum = jnp.sum(grad_norm, axis=0, keepdims=True)
        if i == 0:
            sums_o[0:1, :] = gain_sum
            sums_o[1:2, :] = shift_sum
        else:
            sums_o[0:1, :] += gain_sum
            sums_o[1:2, :] += shift_sum
        for k in range(rows):
            left, right = value[:, k * width : k * width + half], value[:, k * width + half : (k + 1) * width]
            out_o[k, i] = jnp.where(low_col, left, right).astype(LOW)


ROOM = 56 * 1024 * 1024


def whole(array):
    zeros = (0,) * len(array.shape)
    return pl.BlockSpec(tuple(array.shape), lambda *_: zeros)


def run_kernel(body, args, outs, scratch=(), grid=None, in_specs=None, out_specs=None):
    if in_specs is None:
        in_specs = [pl.BlockSpec(memory_space=pltpu.SMEM)] + [whole(a) for a in args[1:]]
    if out_specs is None:
        out_specs = [whole(o) for o in outs]
    return pl.pallas_call(
        body,
        grid=grid or (1,),
        in_specs=in_specs,
        out_specs=out_specs,
        out_shape=outs,
        scratch_shapes=list(scratch),
        compiler_params=pltpu.CompilerParams(vmem_limit_bytes=ROOM),
        cost_estimate=pl.CostEstimate(flops=1024, bytes_accessed=1024, transcendentals=0),
    )(*args)


def shaped(shape, kind):
    return jax.ShapeDtypeStruct(shape, kind)


def on_device(
    tokens, cotangent, w_qkv, b_qkv, w_out, w_up, b_up, w_down, vectors,
    state_qkv, state_qkv_bias, state_out, state_up, state_up_bias, state_down, state_vectors,
):
    parts, rows = lax.axis_size("dp"), lax.axis_size("row")
    col, row_index, me = lax.axis_index("col"), lax.axis_index("row"), lax.axis_index("dp")
    low_col = col == 0
    width = w_qkv.shape[0]
    heads, chunk = w_qkv.shape[2], w_qkv.shape[3]
    groups = w_up.shape[1]
    strip = tokens.shape[1]
    images = tokens.shape[0] // (SEQ * rows)
    model = rows * width
    span = heads * HD
    pos = jnp.stack([col, me, row_index]).astype(jnp.int32)

    qkv_own = w_qkv.transpose(1, 2, 3, 0).reshape(-1, width)
    out_own = w_out.reshape(-1, width)
    up_own = w_up.transpose(1, 2, 0).reshape(-1, width)
    down_own = w_down.reshape(-1, width)
    qkv_count, unit_count = qkv_own.shape[0], up_own.shape[0]
    head_own = jnp.concatenate([qkv_own, out_own])
    head_count = head_own.shape[0]

    at_me = (jnp.arange(parts) == me)[:, None]
    vec_own = jnp.where(at_me, vectors[:, :, None, :], 0).reshape(6, -1)
    vec_far = swap(vec_own, "col", 1)
    vec_pair = jnp.stack([jnp.where(low_col, vec_own, vec_far), jnp.where(low_col, vec_far, vec_own)])
    bias_own = jnp.where(at_me, b_qkv[:, :, None, :], 0).reshape(-1, width)
    unit_own = jnp.where(at_me, b_up.reshape(1, -1), 0).reshape(-1, width)
    small_count = 6 + bias_own.shape[0] + unit_own.shape[0]
    small_each = small_count + -small_count % 16

    def to_send(stream, extra):
        blocks = stream.astype(LOW).reshape(rows, images, SEQ, strip)
        blocks = jnp.pad(blocks, ((0, 0), (0, 0), (0, PAD - SEQ), (0, 0)))
        if extra is not None:
            extra = jnp.pad(extra, ((0, 0), (0, 2), (0, 0)))
            blocks = jnp.concatenate([blocks, jnp.broadcast_to(extra, (rows, *extra.shape))], axis=2)
        return [lax.dynamic_index_in_dim(blocks, row_index ^ k, 0, False) for k in range(rows)]

    def send_images(blocks):
        return [blocks[0]] + [swap(block, "row", k) for k, block in enumerate(blocks) if k]

    def near_two(values):
        return [swap(values, "row", 1), swap(values, "row", 2)]

    token = [pos]

    def fence(*values):
        token[0], *values = lax.optimization_barrier((token[0], *values))
        return values

    assert rows == 4 and images == 2 and lax.axis_size("col") == 2
    feed_all = lax.all_gather(jnp.concatenate([after(up_own, head_own), down_own]), ("dp", "row"), axis=0).reshape(parts, rows, -1, width)
    head_two = near_two(head_own)
    head_x = across(head_own)
    head_plane = planes(head_own)
    token_blocks, dy_blocks = to_send(tokens, vec_pair), to_send(cotangent, None)
    small_same = jnp.pad(jnp.concatenate([bias_own, unit_own]), ((6, small_each - small_count), (0, 0)))
    head_two, head_x, head_plane, token_blocks = fence(head_two, head_x, head_plane, token_blocks)

    head_three = swap(head_two[1], "row", 1)
    came = send_images(token_blocks)
    head_pair = jnp.concatenate(head_two)
    head_pair_x = across(head_pair)
    head_three, came, head_pair_x, head_pair, head_x = fence(head_three, came, head_pair_x, head_pair, head_x)

    small_rows = jnp.stack([jnp.concatenate([b[0, PAD : PAD + 6], b[1, PAD : PAD + 6]], axis=1) for b in came])
    small_rows = jnp.pad(small_rows, ((0, 0), (0, small_each - 6), (0, 0))) + small_same
    head_third = jnp.concatenate([head_three, small_rows.reshape(-1, width)])
    near = jnp.stack([block[:, :PAD] for block in came])
    far = swap(near, "col", 1)
    head_third_x = across(head_third)
    head_own_planes = [*head_plane, *planes(head_x)]
    head_pair_planes = [*planes(head_pair), *planes(head_pair_x)]
    dy_came = send_images(dy_blocks)
    head_third_x, head_third, head_own_planes, head_pair_planes, far, near, dy_came = fence(
        head_third_x, head_third, head_own_planes, head_pair_planes, far, near, dy_came
    )

    head_third_planes = [*planes(head_third), *planes(head_third_x)]

    split = chunk % 16 == 0
    n = parts if split else 1
    head_weights = [*head_own_planes, *head_pair_planes, *head_third_planes]
    if not split:
        def merge(blocks, lead):
            both = xor_order(jnp.stack(blocks), 0, "dp").reshape(parts, lead, blocks[0].shape[0] // lead, width)
            return both.transpose(1, 0, 2, 3).reshape(-1, width)

        def merge_some(blocks, count, lead, number):
            return [merge([b[k * count : (k + 1) * count] for b in blocks], lead) for k in range(number)]

        small_sum = sum(b[head_count:].astype(WIDE) for b in head_third_planes).astype(LOW)
        head_weights = [
            merge(head_own_planes, 4 * heads),
            jnp.concatenate(merge_some(head_pair_planes, head_count, 4 * heads, 2)),
            jnp.concatenate([*merge_some(head_third_planes, head_count, 4 * heads, 1), small_sum]),
        ]
    head_small = [b[head_count * parts // n :] for b in head_weights[2 * n :]]
    scalars = pl.BlockSpec(memory_space=pltpu.SMEM)
    head_specs = [pl.BlockSpec((head_count * parts // n, width), lambda *_: (0, 0))] * n + [whole(w) for w in head_weights[n:]]
    full, low_full = shaped((PAD, model), WIDE), shaped((PAD, model), LOW)

    def forward_one(i):
        strips = pl.BlockSpec((rows, 1, PAD, strip), lambda *_: (0, i, 0, 0))
        outs = [
            shaped((8, model), WIDE),
            low_full,
            low_full,
            shaped((PAD, 3 * span), LOW),
            shaped((PAD, span), LOW),
            low_full,
        ]
        return run_kernel(
            functools.partial(first_kernel, (n, rows, heads, width)),
            (token[0], near, far, *head_weights),
            outs,
            scratch=[pltpu.VMEM((rows, 4 * span, width), LOW)],
            in_specs=[scalars, strips, strips, *head_specs],
        )

    near_dy = jnp.stack(dy_came)
    far_dy = swap(near_dy, "col", 1)
    done = [forward_one(0)]
    done, far_dy, near_dy = fence(done, far_dy, near_dy)

    came_one = [swap(done[0][5], "col", 1)]
    done.append(forward_one(1))
    vec = done[0][0]
    unit_rows = sum(b[6 + bias_own.shape[0] :][: unit_own.shape[0]].astype(WIDE) for b in head_small)
    steps = 4
    block = unit_count // steps
    unit_rows = unit_rows.reshape(parts, steps, block).transpose(1, 0, 2).reshape(steps, 1, parts * block)
    done, came_one, unit_rows = fence(done, came_one, unit_rows)

    came_one = [*came_one, swap(done[1][5], "col", 1)]

    unit_spec = pl.BlockSpec((1, PAD, parts * block), lambda u: (u, 0, 0))
    unit_sum_spec = pl.BlockSpec((1, 1, parts * block), lambda u: (u, 0, 0))
    unit_shape = (steps, PAD, parts * block)

    def feed_one(i):
        strips = pl.BlockSpec((rows, 1, PAD, strip), lambda *_: (0, i, 0, 0))
        outs = [
            full,
            low_full,
            low_full,
            shaped((1, model), WIDE),
            shaped(unit_shape, LOW),
            shaped(unit_shape, LOW),
            shaped((steps, 1, parts * block), WIDE),
            shaped((rows, PAD, strip), WIDE),
            shaped((rows, PAD, strip), LOW),
            low_full,
        ]
        out_specs = [whole(o) for o in outs]
        out_specs[4], out_specs[5], out_specs[6] = unit_spec, unit_spec, unit_sum_spec
        acts = (done[i][1], done[i][5], came_one[i])
        return run_kernel(
            functools.partial(feed_kernel, (parts, rows, width)),
            (token[0], vec, unit_rows, *acts, near_dy, far_dy, feed_all, feed_all),
            outs,
            scratch=[pltpu.VMEM((PAD, model), WIDE), pltpu.VMEM((PAD, model), WIDE)],
            grid=(steps,),
            in_specs=[
                scalars, whole(vec), unit_sum_spec, *[whole(a) for a in acts], strips, strips,
                pl.BlockSpec((parts, rows, block, width), lambda u: (0, 0, u, 0)),
                pl.BlockSpec((parts, rows, block, width), lambda u: (0, 0, u + steps, 0)),
            ],
            out_specs=out_specs,
        )

    fed = [feed_one(0)]
    fed, came_one = fence(fed, came_one)
    came_two = [swap(fed[0][9], "col", 1)]
    fed.append(feed_one(1))
    fed, came_two = fence(fed, came_two)

    came_two = [*came_two, swap(fed[1][9], "col", 1)]
    turns = steps // 2
    early = pl.BlockSpec((2, PAD, parts * block), lambda u: (jnp.minimum(u, turns - 1), 0, 0))
    late = pl.BlockSpec((2, PAD, parts * block), lambda u: (jnp.maximum(u - turns, 0), 0, 0))
    feed_grad = run_kernel(
        functools.partial(feed_grad_kernel, (parts, rows, width, 2)),
        (token[0], *[f[5] for f in fed], *[f[4] for f in fed], *[f[1] for f in fed], *[f[2] for f in fed]),
        [shaped((parts, rows, 2 * unit_count, width), LOW)],
        grid=(2 * turns,),
        in_specs=[scalars, early, early, late, late, *[whole(low_full)] * 4],
        out_specs=[pl.BlockSpec((parts, rows, 2 * block, width), lambda u: (0, 0, u, 0))],
    )[0]
    feed_grad, fed, came_two = fence(feed_grad, fed, came_two)
    feed_total = lax.psum_scatter(feed_grad.reshape(-1, width), ("dp", "row"), scatter_dimension=0, tiled=True)

    def fold(blocks):
        held = dict(enumerate(blocks))
        for bit in bits_of("dp")[:-1]:
            held = join(held, "dp", bit)
        return held[0]

    def ordered(blocks, lead):
        if n == parts:
            return blocks
        both = blocks[0].reshape(rows, lead, parts, -1, width).transpose(2, 0, 1, 3, 4)
        both = xor_order(both.reshape(parts, rows, -1, width), 0, "dp")
        return [both[d] for d in range(parts)]

    half_rows = rows // 2

    def sum_high(near_sum, came_part):
        return [add_low(near_sum[half_rows + k], came_part[k]) for k in range(half_rows)]

    def sum_low(near_sum, came_part):
        return [add_low(near_sum[k], came_part[k]) for k in range(half_rows)]

    def from_images(strips):
        came = [strips[0]] + [swap(strips[k], "row", k) for k in range(1, rows)]
        stacked = xor_order(jnp.stack(came)[:, :, :SEQ], 0, "row")
        return stacked.reshape(-1, strip).astype(WIDE)

    def backward_one(i):
        outs = [full, low_full, shaped((PAD, 3 * span), LOW), low_full, shaped((8, model), WIDE), shaped((1, 3 * span), WIDE)]
        acts = (vec, fed[i][0], fed[i][9], came_two[i], fed[i][2], done[i][3])
        return run_kernel(
            functools.partial(second_kernel, (n, rows, heads, width)),
            (token[0], *acts, *head_weights),
            outs,
            scratch=[pltpu.VMEM((rows, 4 * span, width), LOW), pltpu.VMEM((PAD, span), LOW)],
            in_specs=[scalars, *[whole(a) for a in acts], *head_specs],
        )

    top_far = swap(jnp.stack([f[8] for f in fed]), "col", 1)
    returned = [backward_one(0)]
    returned, top_far = fence(returned, top_far)

    came_three = [swap(returned[0][3], "col", 1)]
    top = jnp.stack([f[7] + t.astype(WIDE) for f, t in zip(fed, top_far)], axis=1).astype(LOW)
    result = from_images(top)
    returned.append(backward_one(1))
    returned, came_three, result = fence(returned, came_three, result)

    came_three = [*came_three, swap(returned[1][3], "col", 1)]
    attn_grad = run_kernel(
        functools.partial(attn_grad_kernel, (n, rows, heads, width)),
        (
            token[0], *[r[2] for r in returned], *[d[2] for d in done], *[d[4] for d in done], *[r[1] for r in returned],
        ),
        [shaped((rows, head_count * parts // n, width), LOW) for _ in range(n)],
        scratch=[pltpu.VMEM((span, model), LOW)],
    )
    attn_grad, came_three = fence(attn_grad, came_three)

    attn_blocks = ordered(attn_grad, 4 * heads)
    attn_far, attn_near = fold(attn_blocks[parts // 2 :]), fold(attn_blocks[: parts // 2])
    grad_strips, sums_one = run_kernel(
        functools.partial(last_kernel, (rows, width, images)),
        (
            token[0], vec, *[d[1] for d in done], *[r[3] for r in returned], *came_three, *[r[0] for r in returned],
        ),
        [shaped((rows, images, PAD, strip), LOW), shaped((8, model), WIDE)],
    )
    attn_far, attn_near, grad_strips, sums_one = fence(attn_far, attn_near, grad_strips, sums_one)

    grad_scale = grad_gain / math.sqrt(tokens.shape[0] * parts)

    lanes = max(unit_count, 2 * heads * chunk, 12 * chunk)
    tiny = run_kernel(
        functools.partial(collect_kernel, (rows, heads, chunk, parts, width, images)),
        (
            token[0], sums_one, *[r[4] for r in returned],
            *[f[3] for f in fed], *[r[5] for r in returned], *[f[6] for f in fed],
        ),
        [shaped((parts, 8, lanes), WIDE)],
    )[0]
    attn_high = across(attn_far[half_rows:])
    tiny = functools.reduce(lambda a, b: a + b, [tiny[0]] + [swap(tiny[d], "dp", d) for d in range(1, parts)])
    def adam(reduced, owns, states, ranges):
        first, pieces = reduced
        outs = []
        for size, _ in ranges:
            outs += [shaped((size, width), WIDE), shaped((size, width), WIDE), shaped((2, size, width), WIDE)]
        args = (first, *pieces, *owns, *states)
        return run_kernel(
            functools.partial(adam_kernel, (len(pieces), [r[0] for r in ranges], grad_scale)),
            args,
            outs,
            in_specs=[whole(a) for a in args],
        )

    state_rows = lambda a, order: a.transpose(order).reshape(2, -1, width)
    out_count = out_own.shape[0]
    attn_high, attn_far, attn_near, grad_strips, tiny = fence(attn_high, attn_far, attn_near, grad_strips, tiny)

    attn_low = across(attn_far[:half_rows])
    attn_two, attn_three = sum_high(attn_near, attn_high)
    attn_three = swap(attn_three, "row", 1)
    grad_tokens = from_images(grad_strips)
    tiny = (tiny + swap(tiny, "row", 1)) + (swap(tiny, "row", 2) + swap(tiny, "row", 3))
    attn_low, attn_two, attn_three, attn_near, grad_tokens, tiny = fence(
        attn_low, attn_two, attn_three, attn_near, grad_tokens, tiny
    )

    attn_zero, attn_one = sum_low(attn_near, attn_low)
    attn_one = swap(attn_one, "row", 1)
    attn_two = swap(add_low(attn_two, attn_three), "row", 2)
    attn_zero, attn_one, attn_two = fence(attn_zero, attn_one, attn_two)
    feed_done = adam(
        (feed_total, []),
        [up_own, down_own],
        [state_rows(state_up, (0, 2, 3, 1)), state_rows(state_down, (0, 1, 2, 3))],
        [(unit_count, 0), (unit_count, 0)],
    )

    flat_up = lambda a: jnp.swapaxes(a, -1, -2)
    small_args = (b_qkv, flat_up(b_up), vectors, state_qkv_bias, flat_up(state_up_bias), state_vectors)
    small_kinds = (b_qkv.shape, flat_up(b_up).shape, vectors.shape)
    small_done = run_kernel(
        functools.partial(small_adam_kernel, (heads, groups, chunk, grad_scale)),
        (token[0], tiny, *small_args),
        [shaped(k, WIDE) for k in (*small_kinds, *small_kinds)] + [shaped((2, *k), WIDE) for k in small_kinds],
    )

    attn_done = adam(
        (attn_zero, [attn_one, attn_two]),
        [qkv_own, out_own],
        [state_rows(state_qkv, (0, 2, 3, 4, 1)), state_rows(state_out, (0, 1, 2, 3))],
        [(qkv_count, 0), (out_count, 0)],
    )

    def shape_all(which):
        lead = (2,) if which == 2 else ()
        more = (0,) if which == 2 else ()
        move = lambda order: (*more, *[o + len(lead) for o in order])
        return (
            attn_done[which].reshape(*lead, 3, heads, chunk, width).transpose(move((3, 0, 1, 2))),
            small_done[3 * which],
            attn_done[3 + which].reshape(*lead, *w_out.shape),
            feed_done[which].reshape(*lead, groups, chunk, width).transpose(move((2, 0, 1))),
            flat_up(small_done[3 * which + 1]),
            feed_done[3 + which].reshape(*lead, *w_down.shape),
            small_done[3 * which + 2],
        )

    return (result, grad_tokens, *shape_all(0), *shape_all(1), *shape_all(2))


def solution(mesh):
    placed = (
        P("dp", ("row", "col")),
        P("dp", ("row", "col")),
        P("row", None, "col", "dp"),
        P(None, "col", "dp"),
        P("col", "dp", "row"),
        P("row", "col", "dp"),
        P("col", "dp"),
        P("col", "dp", "row"),
        P(None, ("row", "col"), "dp"),
        P(None, "row", None, "col", "dp"),
        P(None, None, "col", "dp"),
        P(None, "col", "dp", "row"),
        P(None, "row", "col", "dp"),
        P(None, "col", "dp"),
        P(None, "col", "dp", "row"),
        P(None, None, ("row", "col"), "dp"),
    )
    params = placed[2:9]
    return jax.shard_map(
        on_device,
        mesh=mesh,
        in_specs=placed,
        out_specs=(placed[0], placed[0], *params, *params, *placed[9:]),
        check_vma=False,
    )
```

```python
import functools
import math

import jax
import jax.numpy as jnp
from jax import lax
from jax.experimental import pallas as pl
from jax.experimental.pallas import tpu as pltpu
from jax.sharding import PartitionSpec as P

HD = 64
SEQ = 197
PAD = 208
STEP = 10

norm_eps = 1e-06
beta_first = 0.9
beta_second = 0.999
learn_rate = 0.01
weight_decay = 0.05
adam_eps = 1e-08
grad_gain = 32.0

LOW = jnp.bfloat16
WIDE = jnp.float32


def swap(values, name, bit):
    count = lax.axis_size(name)
    return lax.ppermute(values, name, [(i, i ^ bit) for i in range(count)])


def bits_of(name):
    bits, bit = [], 1
    while bit < lax.axis_size(name):
        bits.append(bit)
        bit *= 2
    return bits


def after(value, *others):
    return lax.optimization_barrier((value, *others))[0]


def planes(values):
    blocks = {0: values}
    for bit in reversed(bits_of("dp")[:-1]):
        for place in list(blocks):
            blocks[place ^ bit] = swap(blocks[place], "dp", bit)
    return [blocks[d] for d in range(len(blocks))]


def across(values):
    return swap(values, "dp", lax.axis_size("dp") // 2)


def add_low(left, right):
    return (left.astype(WIDE) + right.astype(WIDE)).astype(left.dtype)


def join(held, name, bit):
    return {d: add_low(held[d], swap(held[d ^ bit], name, bit)) for d in held if not d & bit}


def scatter(blocks, name):
    held = dict(enumerate(blocks))
    for bit in bits_of(name):
        held = join(held, name, bit)
    return held[0]


def xor_order(values, axis, name):
    mine = lax.axis_index(name)
    shape = values.shape
    for bit in bits_of(name):
        split = values.reshape(shape[:axis] + (shape[axis] // (2 * bit), 2, bit) + shape[axis + 1 :])
        flipped = jnp.flip(split, axis + 1)
        values = jnp.where((mine & bit) > 0, flipped, split).reshape(shape)
    return values


def adam_step(weight_old, gradient, first_old, second_old, decay_on):
    first_moment = beta_first * first_old + (1.0 - beta_first) * gradient
    second_moment = beta_second * second_old + (1.0 - beta_second) * gradient * gradient
    first_hat = first_moment / (1.0 - beta_first**STEP)
    second_hat = second_moment / (1.0 - beta_second**STEP)
    change = -learn_rate * (first_hat / (jnp.sqrt(second_hat) + adam_eps) + decay_on * weight_old)
    return change, first_moment, second_moment


def adam_kernel(spec, first, *refs):
    count, sizes, grad_scale = spec
    pieces, refs = refs[:count], refs[count:]
    weights, states, outs = refs[: len(sizes)], refs[len(sizes) : 2 * len(sizes)], refs[2 * len(sizes) :]
    at = 0
    for i, size in enumerate(sizes):
        lines = slice(at, at + size)
        at += size
        total = first[lines].astype(WIDE)
        for piece in pieces:
            total = total + piece[lines].astype(WIDE)
        gradient = total * grad_scale
        change, low_moment, high_moment = adam_step(
            weights[i][...].astype(WIDE), gradient, states[i][0], states[i][1], weight_decay
        )
        outs[3 * i][...] = gradient
        outs[3 * i + 1][...] = change
        outs[3 * i + 2][0] = low_moment
        outs[3 * i + 2][1] = high_moment


def join_kernel(qkv, out, up, down, head_o, feed_o):
    head_o[: qkv.shape[0], :] = qkv[...]
    head_o[qkv.shape[0] :, :] = out[...]
    feed_o[: up.shape[0], :] = up[...]
    feed_o[up.shape[0] :, :] = down[...]


def collect_kernel(spec, pos, ones, *refs):
    rows, heads, chunk, parts, width, images = spec
    twos, dys, packs, refs = refs[:images], refs[images : 2 * images], refs[2 * images : 3 * images], refs[3 * images :]
    units, out, = refs[:-1], refs[-1]
    low_col, me, row = pos[0] == 0, pos[1], pos[2]
    out[...] = jnp.zeros_like(out)
    add = lambda items: functools.reduce(lambda a, b: a + b, items)
    two = add([t[0:3, :] for t in twos])
    lines = [ones[0:1, :], ones[1:2, :], two[0:1], two[1:2], two[2:3], add([d[...] for d in dys])]
    pack = add([p[...] for p in packs])
    span = heads * HD
    half = width // 2
    unit_total = add([u[...] for u in units])
    each = unit_total.shape[2] // parts
    def put(d, line, pieces):
        value = jnp.concatenate(pieces, axis=1)
        short = out.shape[2] - value.shape[1]
        if short:
            value = jnp.concatenate([value, jnp.zeros((1, short), WIDE)], axis=1)
        out[pl.ds(d, 1), pl.ds(line, 1), :] = value[None]

    for owner in range(parts):
        d = me ^ owner
        spots = [part * span + h * HD + owner * chunk for part in (0, 2) for h in range(heads)]
        put(d, 0, [pack[:, at : at + chunk] for at in spots])
        put(d, 1, [unit_total[u][:, owner * each : (owner + 1) * each] for u in range(unit_total.shape[0])])
        for k in range(rows):
            pieces = []
            for v in range(6):
                for j in range(2):
                    at = k * width + j * HD + owner * chunk
                    near, far = lines[v][:, at : at + chunk], lines[v][:, at + half : at + half + chunk]
                    pieces.append(jnp.where(low_col, near, far))
            put(d, 4 + (row ^ k), pieces)


def small_adam_kernel(spec, pos, tiny, *refs):
    heads, groups, chunk, grad_scale = spec
    row = pos[2]
    weights, states, grads, changes, fresh = (refs[3 * i : 3 * i + 3] for i in range(5))
    for part in range(2):
        for h in range(heads):
            at = (part * heads + h) * chunk
            grads[0][part, h : h + 1, :] = tiny[0:1, at : at + chunk] * grad_scale
    side = lax.broadcasted_iota(jnp.int32, (groups, chunk), 0)
    table = jnp.zeros((groups, chunk), WIDE)
    for g in range(groups):
        table = jnp.where(side == g, tiny[1:2, g * chunk : (g + 1) * chunk], table)
    grads[1][...] = table.T * grad_scale
    mine = tiny[pl.ds(4 + row, 1), :] * grad_scale
    for v in range(6):
        for j in range(2):
            at = (v * 2 + j) * chunk
            grads[2][v, j : j + 1, :] = mine[:, at : at + chunk]
    for i in range(3):
        change, low_moment, high_moment = adam_step(weights[i][...].astype(WIDE), grads[i][...], states[i][0], states[i][1], 0.0)
        changes[i][...] = change
        fresh[i][0] = low_moment
        fresh[i][1] = high_moment


def dot_nt(left, right):
    return lax.dot_general(left, right, (((1,), (1,)), ((), ())), preferred_element_type=WIDE)


def dot_nn(left, right):
    return lax.dot_general(left, right, (((1,), (0,)), ((), ())), preferred_element_type=WIDE)


def dot_tn(left, right):
    return lax.dot_general(left, right, (((0,), (0,)), ((), ())), preferred_element_type=WIDE)


def moments_of(stream):
    center = jnp.mean(stream, axis=-1, keepdims=True)
    offset = stream - center
    inv_std = lax.rsqrt(jnp.mean(offset * offset, axis=-1, keepdims=True) + norm_eps)
    return offset * inv_std, inv_std


def norm_backward(grad_norm, scaled, inv_std, gain):
    weighted = grad_norm * gain
    return inv_std * (
        weighted
        - jnp.mean(weighted, axis=-1, keepdims=True)
        - scaled * jnp.mean(weighted * scaled, axis=-1, keepdims=True)
    )


def lay_strips(low_col, near, far, rows):
    pieces = []
    for k in range(rows):
        mine, other = near(k), far(k)
        pieces.append(jnp.where(low_col, mine, other))
        pieces.append(jnp.where(low_col, other, mine))
    return jnp.concatenate(pieces, axis=1)


def soft(scores):
    lane = lax.broadcasted_iota(jnp.int32, scores.shape, 1)
    scores = jnp.where(lane < SEQ, scores * (1.0 / math.sqrt(HD)), -1e30)
    raised = jnp.exp(scores - jnp.max(scores, axis=-1, keepdims=True))
    return raised * (1.0 / jnp.sum(raised, axis=-1, keepdims=True))


class Source:
    def __init__(self, refs, count):
        self.refs, self.count = refs, count

    def block(self, k, first, size):
        at = first + (self.count if k == 2 else 0)
        return self.refs[(k + 1) // 2][at : at + size, :]


def lay_heads(target, sources, me, groups, rows):
    own = HD // len(sources)
    for k in range(rows):
        for d, source in enumerate(sources):
            place = me ^ d if len(sources) > 1 else 0
            for g in range(groups):
                at = g * HD + place * own
                if len(sources) > 1:
                    at = pl.multiple_of(at, own)
                target[k, pl.ds(at, own), :] = source.block(k, g * own, own)


def first_kernel(spec, pos, near, far, *refs):
    n, rows, heads, width = spec
    count = 4 * heads * HD // n
    sources = [Source([refs[d], refs[n + d], refs[2 * n + d]], count) for d in range(n)]
    vec_o, x_o, normed_o, packed_o, att_o, part_o, qkv_s = refs[3 * n :]
    low_col, me = pos[0] == 0, pos[1]
    small = refs[2 * n][count:, :].astype(WIDE)
    for d in range(1, n):
        small = small + refs[2 * n + d][count:, :].astype(WIDE)
    each = small.shape[0] // rows
    vec = jnp.concatenate([small[k * each : k * each + 6] for k in range(rows)], axis=1)
    vec_o[0:6, :] = vec
    lay_heads(qkv_s, sources, me, 4 * heads, rows)
    stream = lay_strips(low_col, lambda k: near[k, 0], lambda k: far[k, 0], rows)
    x_o[...] = stream
    scaled, _ = moments_of(stream.astype(WIDE))
    normed = (scaled * vec[0:1] + vec[1:2]).astype(LOW)
    normed_o[...] = normed
    span = heads * HD
    lines = span // width
    for part in range(3):
        total = dot_nt(normed[:, :width], qkv_s[0, part * span : (part + 1) * span, :])
        for k in range(1, rows):
            total = total + dot_nt(normed[:, k * width : (k + 1) * width], qkv_s[k, part * span : (part + 1) * span, :])
        if part != 1:
            line = 6 + (lines if part == 2 else 0)
            total = total + jnp.concatenate([small[line + i : line + i + 1] for i in range(lines)], axis=1)
        packed_o[:, part * span : (part + 1) * span] = total.astype(LOW)
    two = 2 * HD
    lane = lax.broadcasted_iota(jnp.int32, (1, two), 1)
    for pair in range(heads // 2):
        at = pair * two
        queries = packed_o[:, at : at + two]
        key_rows = packed_o[:, span + at : span + at + two]
        values = packed_o[:, 2 * span + at : 2 * span + at + two]
        halves = []
        for side in range(2):
            mask = (lane < HD) if side == 0 else (lane >= HD)
            probs = soft(dot_nt(jnp.where(mask, queries, jnp.zeros_like(queries)), key_rows))
            halves.append(dot_nn(probs.astype(LOW), values))
        att_o[:, at : at + two] = jnp.where(lane < HD, halves[0], halves[1]).astype(LOW)
    for k in range(rows):
        part_o[:, k * width : (k + 1) * width] = dot_nn(att_o[...], qkv_s[k, 3 * span :, :]).astype(LOW)


def row_blocks(ref, row, parts, rows):
    return [jnp.concatenate([ref[d, row ^ k] for d in range(parts)], axis=0) for k in range(rows)]


def feed_kernel(spec, pos, vec, small, x, part, came, near, far, up, down, *refs):
    parts, rows, width = spec
    mid, normed, dy, dy_sum_o, units_o, hid_o, unit_sum_o, top_o, far_o, back_o, mixed_s, back_s = refs
    low_col, row = pos[0] == 0, pos[2]
    step = pl.program_id(0)

    @pl.when(step == 0)
    def _():
        dy[...] = lay_strips(low_col, lambda k: near[k, 0], lambda k: far[k, 0], rows)
        dy_sum_o[...] = jnp.sum(dy[...].astype(WIDE), axis=0, keepdims=True)
        middle = x[...].astype(WIDE) + (part[...].astype(WIDE) + came[...].astype(WIDE) + vec[2:3, :])
        mid[...] = middle
        scaled, _ = moments_of(middle)
        normed[...] = (scaled * vec[3:4, :] + vec[4:5, :]).astype(LOW)
        mixed_s[...] = jnp.zeros_like(mixed_s)
        back_s[...] = jnp.zeros_like(back_s)

    up_rows, down_rows = row_blocks(up, row, parts, rows), row_blocks(down, row, parts, rows)
    hidden = dot_nt(normed[:, :width], up_rows[0])
    for k in range(1, rows):
        hidden = hidden + dot_nt(normed[:, k * width : (k + 1) * width], up_rows[k])
    active, slope = gelu_both(hidden + small[0])
    active = active.astype(LOW)
    units_o[0] = active
    grad = dot_nt(dy[:, :width], down_rows[0])
    for k in range(1, rows):
        grad = grad + dot_nt(dy[:, k * width : (k + 1) * width], down_rows[k])
    grad = (grad * slope).astype(LOW)
    hid_o[0] = grad
    unit_sum_o[0] = jnp.sum(grad.astype(WIDE), axis=0, keepdims=True)
    for k in range(rows):
        at = slice(k * width, (k + 1) * width)
        mixed_s[:, at] += dot_nn(active, down_rows[k])
        back_s[:, at] += dot_nn(grad, up_rows[k])

    @pl.when(step == pl.num_programs(0) - 1)
    def _():
        back_o[...] = back_s[...].astype(LOW)
        half = width // 2
        for k in range(rows):
            left, right = slice(k * width, k * width + half), slice(k * width + half, (k + 1) * width)
            base = mid[...] + vec[5:6, :]
            top_l, top_r = mixed_s[:, left] + base[:, left], mixed_s[:, right] + base[:, right]
            top_o[k] = jnp.where(low_col, top_l, top_r)
            far_o[k] = jnp.where(low_col, mixed_s[:, right], mixed_s[:, left]).astype(LOW)


def feed_grad_kernel(spec, pos, *refs):
    parts, rows, width, groups = spec
    hids, units, normeds, dys, out = refs[0:2], refs[2:4], refs[4:6], refs[6:8], refs[8]
    row = pos[2]

    def write(left, right):
        wide = [jnp.concatenate([ref[g] for g in range(groups)], axis=1) for ref in left]
        total = dot_tn(jnp.concatenate(wide, axis=0), jnp.concatenate([ref[...] for ref in right], axis=0))
        block = total.shape[0] // (groups * parts)
        for g in range(groups):
            for d in range(parts):
                at = (g * parts + d) * block
                for k in range(rows):
                    value = total[at : at + block, k * width : (k + 1) * width]
                    out[d, row ^ k, g * block : (g + 1) * block, :] = value.astype(LOW)

    half = pl.num_programs(0) // 2

    @pl.when(pl.program_id(0) < half)
    def _():
        write(hids, normeds)

    @pl.when(pl.program_id(0) >= half)
    def _():
        write(units, dys)


def second_kernel(spec, pos, vec, mid, back, came, dy, packed, *refs):
    n, rows, heads, width = spec
    count = 4 * heads * HD // n
    sources = [Source([refs[d], refs[n + d], refs[2 * n + d]], count) for d in range(n)]
    dmid_o, dz_o, dpacked_o, back_o, sums_o, psum_o, qkv_s, datt_s = refs[3 * n :]
    me = pos[1]
    lay_heads(qkv_s, sources, me, 4 * heads, rows)
    span = heads * HD
    grad_norm = back[...].astype(WIDE) + came[...].astype(WIDE)
    scaled, inv_std = moments_of(mid[...])
    dmid = dy[...].astype(WIDE) + norm_backward(grad_norm, scaled, inv_std, vec[3:4, :])
    dmid_o[...] = dmid
    dz = dmid.astype(LOW)
    dz_o[...] = dz
    sums_o[0:1, :] = jnp.sum(dz.astype(WIDE), axis=0, keepdims=True)
    sums_o[1:2, :] = jnp.sum(grad_norm * scaled, axis=0, keepdims=True)
    sums_o[2:3, :] = jnp.sum(grad_norm, axis=0, keepdims=True)
    total = dot_nt(dz[:, :width], qkv_s[0, 3 * span :, :])
    for k in range(1, rows):
        total = total + dot_nt(dz[:, k * width : (k + 1) * width], qkv_s[k, 3 * span :, :])
    datt_s[...] = total.astype(LOW)
    two = 2 * HD
    scale = 1.0 / math.sqrt(HD)
    lane = lax.broadcasted_iota(jnp.int32, (1, two), 1)
    for pair in range(heads // 2):
        at = pair * two
        queries = packed[:, at : at + two]
        key_rows = packed[:, span + at : span + at + two]
        values = packed[:, 2 * span + at : 2 * span + at + two]
        grads = datt_s[:, at : at + two]
        dqs, dks, dvs = [], [], []
        for side in range(2):
            mask = (lane < HD) if side == 0 else (lane >= HD)
            probs = soft(dot_nt(jnp.where(mask, queries, jnp.zeros_like(queries)), key_rows))
            dprobs = dot_nt(jnp.where(mask, grads, jnp.zeros_like(grads)), values)
            dscores = probs * (dprobs - jnp.sum(dprobs * probs, axis=-1, keepdims=True))
            dscores = dscores.astype(LOW)
            dqs.append(dot_nn(dscores, key_rows))
            dks.append(dot_tn(dscores, queries))
            dvs.append(dot_tn(probs.astype(LOW), grads))
        first = lane < HD
        dpacked_o[:, at : at + two] = (jnp.where(first, dqs[0], dqs[1]) * scale).astype(LOW)
        dpacked_o[:, span + at : span + at + two] = (jnp.where(first, dks[0], dks[1]) * scale).astype(LOW)
        dpacked_o[:, 2 * span + at : 2 * span + at + two] = jnp.where(first, dvs[0], dvs[1]).astype(LOW)
    psum_o[...] = jnp.sum(dpacked_o[...].astype(WIDE), axis=0, keepdims=True)
    for k in range(rows):
        back_o[:, k * width : (k + 1) * width] = dot_nn(dpacked_o[...], qkv_s[k, : 3 * span, :]).astype(LOW)


def attn_grad_kernel(spec, pos, *refs):
    n, rows, heads, width = spec
    dpacked, normed, att, dz = refs[0:2], refs[2:4], refs[4:6], refs[6:8]
    outs, total_s = refs[8 : 8 + n], refs[8 + n]
    me = pos[1]
    span = heads * HD
    own = HD // n
    for part in range(4):
        if part < 3:
            at = slice(part * span, (part + 1) * span)
            total = dot_tn(dpacked[0][:, at], normed[0][...]) + dot_tn(dpacked[1][:, at], normed[1][...])
        else:
            total = dot_tn(att[0][...], dz[0][...]) + dot_tn(att[1][...], dz[1][...])
        total_s[...] = total.astype(LOW)
        for d in range(n):
            place = me ^ d if n > 1 else 0
            for g in range(heads):
                line = g * HD + place * own
                if n > 1:
                    line = pl.multiple_of(line, own)
                value = total_s[pl.ds(line, own), :]
                to = (part * heads + g) * own
                for k in range(rows):
                    outs[d][k, to : to + own, :] = value[:, k * width : (k + 1) * width]


def gelu_both(values):
    tail = 0.5 * (1.0 + lax.erf(values * (1.0 / math.sqrt(2.0))))
    bell = jnp.exp(values * values * -0.5) * (1.0 / math.sqrt(2.0 * math.pi))
    return values * tail, tail + values * bell


def last_kernel(spec, pos, vec, *refs):
    rows, width, images = spec
    x, back, came, dmid = (refs[i * images : (i + 1) * images] for i in range(4))
    out_o, sums_o = refs[4 * images :]
    low_col = pos[0] == 0
    half = width // 2
    for i in range(images):
        scaled, inv_std = moments_of(x[i][...].astype(WIDE))
        grad_norm = back[i][...].astype(WIDE) + came[i][...].astype(WIDE)
        value = dmid[i][...] + norm_backward(grad_norm, scaled, inv_std, vec[0:1, :])
        gain_sum = jnp.sum(grad_norm * scaled, axis=0, keepdims=True)
        shift_sum = jnp.sum(grad_norm, axis=0, keepdims=True)
        if i == 0:
            sums_o[0:1, :] = gain_sum
            sums_o[1:2, :] = shift_sum
        else:
            sums_o[0:1, :] += gain_sum
            sums_o[1:2, :] += shift_sum
        for k in range(rows):
            left, right = value[:, k * width : k * width + half], value[:, k * width + half : (k + 1) * width]
            out_o[k, i] = jnp.where(low_col, left, right).astype(LOW)


ROOM = 60 * 1024 * 1024


def whole(array):
    zeros = (0,) * len(array.shape)
    return pl.BlockSpec(tuple(array.shape), lambda *_: zeros)


def run_kernel(body, args, outs, scratch=(), grid=None, in_specs=None, out_specs=None):
    if in_specs is None:
        in_specs = [pl.BlockSpec(memory_space=pltpu.SMEM)] + [whole(a) for a in args[1:]]
    if out_specs is None:
        out_specs = [whole(o) for o in outs]
    return pl.pallas_call(
        body,
        grid=grid or (1,),
        in_specs=in_specs,
        out_specs=out_specs,
        out_shape=outs,
        scratch_shapes=list(scratch),
        compiler_params=pltpu.CompilerParams(vmem_limit_bytes=ROOM),
        cost_estimate=pl.CostEstimate(flops=1024, bytes_accessed=1024, transcendentals=0),
    )(*args)


def shaped(shape, kind):
    return jax.ShapeDtypeStruct(shape, kind)


def on_device(
    tokens, cotangent, w_qkv, b_qkv, w_out, w_up, b_up, w_down, vectors,
    state_qkv, state_qkv_bias, state_out, state_up, state_up_bias, state_down, state_vectors,
):
    parts, rows = lax.axis_size("dp"), lax.axis_size("row")
    col, row_index, me = lax.axis_index("col"), lax.axis_index("row"), lax.axis_index("dp")
    low_col = col == 0
    width = w_qkv.shape[0]
    heads, chunk = w_qkv.shape[2], w_qkv.shape[3]
    groups = w_up.shape[1]
    strip = tokens.shape[1]
    images = tokens.shape[0] // (SEQ * rows)
    model = rows * width
    span = heads * HD
    pos = jnp.stack([col, me, row_index]).astype(jnp.int32)

    qkv_own = w_qkv.transpose(1, 2, 3, 0).reshape(-1, width)
    out_own = w_out.reshape(-1, width)
    up_own = w_up.transpose(1, 2, 0).reshape(-1, width)
    down_own = w_down.reshape(-1, width)
    qkv_count, unit_count = qkv_own.shape[0], up_own.shape[0]
    head_own, feed_own = run_kernel(
        join_kernel,
        (qkv_own, out_own, up_own, down_own),
        [shaped((qkv_count + out_own.shape[0], width), LOW), shaped((2 * unit_count, width), LOW)],
        in_specs=[whole(a) for a in (qkv_own, out_own, up_own, down_own)],
    )
    head_count = head_own.shape[0]

    at_me = (jnp.arange(parts) == me)[:, None]
    vec_own = jnp.where(at_me, vectors[:, :, None, :], 0).reshape(6, -1)
    vec_far = swap(vec_own, "col", 1)
    vec_pair = jnp.stack([jnp.where(low_col, vec_own, vec_far), jnp.where(low_col, vec_far, vec_own)])
    bias_own = jnp.where(at_me, b_qkv[:, :, None, :], 0).reshape(-1, width)
    unit_own = jnp.where(at_me, b_up.reshape(1, -1), 0).reshape(-1, width)
    small_count = 6 + bias_own.shape[0] + unit_own.shape[0]
    small_each = small_count + -small_count % 16

    def to_send(stream, extra):
        blocks = stream.astype(LOW).reshape(rows, images, SEQ, strip)
        blocks = jnp.pad(blocks, ((0, 0), (0, 0), (0, PAD - SEQ), (0, 0)))
        if extra is not None:
            extra = jnp.pad(extra, ((0, 0), (0, 2), (0, 0)))
            blocks = jnp.concatenate([blocks, jnp.broadcast_to(extra, (rows, *extra.shape))], axis=2)
        return [lax.dynamic_index_in_dim(blocks, row_index ^ k, 0, False) for k in range(rows)]

    def send_images(blocks):
        return [blocks[0]] + [swap(block, "row", k) for k, block in enumerate(blocks) if k]

    def near_two(values):
        return [swap(values, "row", 1), swap(values, "row", 2)]

    token = [pos]

    def fence(*values):
        token[0], *values = lax.optimization_barrier((token[0], *values))
        return values

    assert rows == 4 and images == 2 and lax.axis_size("col") == 2
    feed_all = lax.all_gather(feed_own, ("dp", "row"), axis=0).reshape(parts, rows, -1, width)
    head_two = near_two(head_own)
    head_x = across(head_own)
    head_plane = planes(head_own)
    token_blocks, dy_blocks = to_send(tokens, vec_pair), to_send(cotangent, None)
    small_same = jnp.pad(jnp.concatenate([bias_own, unit_own]), ((6, small_each - small_count), (0, 0)))
    head_two, head_x, head_plane, token_blocks = fence(head_two, head_x, head_plane, token_blocks)

    head_three = swap(head_two[1], "row", 1)
    came = send_images(token_blocks)
    head_pair = jnp.concatenate(head_two)
    head_pair_x = across(head_pair)
    head_three, came, head_pair_x, head_pair, head_x = fence(head_three, came, head_pair_x, head_pair, head_x)

    small_rows = jnp.stack([jnp.concatenate([b[0, PAD : PAD + 6], b[1, PAD : PAD + 6]], axis=1) for b in came])
    small_rows = jnp.pad(small_rows, ((0, 0), (0, small_each - 6), (0, 0))) + small_same
    head_third = jnp.concatenate([head_three, small_rows.reshape(-1, width)])
    near = jnp.stack([block[:, :PAD] for block in came])
    far = swap(near, "col", 1)
    head_third_x = across(head_third)
    head_own_planes = [*head_plane, *planes(head_x)]
    head_pair_planes = [*planes(head_pair), *planes(head_pair_x)]
    dy_came = send_images(dy_blocks)
    head_third_x, head_third, head_own_planes, head_pair_planes, far, near, dy_came = fence(
        head_third_x, head_third, head_own_planes, head_pair_planes, far, near, dy_came
    )

    head_third_planes = [*planes(head_third), *planes(head_third_x)]

    split = chunk % 16 == 0
    n = parts if split else 1
    head_weights = [*head_own_planes, *head_pair_planes, *head_third_planes]
    if not split:
        def merge(blocks, lead):
            both = xor_order(jnp.stack(blocks), 0, "dp").reshape(parts, lead, blocks[0].shape[0] // lead, width)
            return both.transpose(1, 0, 2, 3).reshape(-1, width)

        def merge_some(blocks, count, lead, number):
            return [merge([b[k * count : (k + 1) * count] for b in blocks], lead) for k in range(number)]

        small_sum = sum(b[head_count:].astype(WIDE) for b in head_third_planes).astype(LOW)
        head_weights = [
            merge(head_own_planes, 4 * heads),
            jnp.concatenate(merge_some(head_pair_planes, head_count, 4 * heads, 2)),
            jnp.concatenate([*merge_some(head_third_planes, head_count, 4 * heads, 1), small_sum]),
        ]
    head_small = [b[head_count * parts // n :] for b in head_weights[2 * n :]]
    scalars = pl.BlockSpec(memory_space=pltpu.SMEM)
    head_specs = [pl.BlockSpec((head_count * parts // n, width), lambda *_: (0, 0))] * n + [whole(w) for w in head_weights[n:]]
    full, low_full = shaped((PAD, model), WIDE), shaped((PAD, model), LOW)

    def forward_one(i):
        strips = pl.BlockSpec((rows, 1, PAD, strip), lambda *_: (0, i, 0, 0))
        outs = [
            shaped((8, model), WIDE),
            low_full,
            low_full,
            shaped((PAD, 3 * span), LOW),
            shaped((PAD, span), LOW),
            low_full,
        ]
        return run_kernel(
            functools.partial(first_kernel, (n, rows, heads, width)),
            (token[0], near, far, *head_weights),
            outs,
            scratch=[pltpu.VMEM((rows, 4 * span, width), LOW)],
            in_specs=[scalars, strips, strips, *head_specs],
        )

    near_dy = jnp.stack(dy_came)
    far_dy = swap(near_dy, "col", 1)
    done = [forward_one(0)]
    done, far_dy, near_dy = fence(done, far_dy, near_dy)

    came_one = [swap(done[0][5], "col", 1)]
    done.append(forward_one(1))
    vec = done[0][0]
    unit_rows = sum(b[6 + bias_own.shape[0] :][: unit_own.shape[0]].astype(WIDE) for b in head_small)
    steps = 4
    block = unit_count // steps
    unit_rows = unit_rows.reshape(parts, steps, block).transpose(1, 0, 2).reshape(steps, 1, parts * block)
    done, came_one, unit_rows = fence(done, came_one, unit_rows)

    came_one = [*came_one, swap(done[1][5], "col", 1)]

    unit_spec = pl.BlockSpec((1, PAD, parts * block), lambda u: (u, 0, 0))
    unit_sum_spec = pl.BlockSpec((1, 1, parts * block), lambda u: (u, 0, 0))
    unit_shape = (steps, PAD, parts * block)

    def feed_one(i):
        strips = pl.BlockSpec((rows, 1, PAD, strip), lambda *_: (0, i, 0, 0))
        outs = [
            full,
            low_full,
            low_full,
            shaped((1, model), WIDE),
            shaped(unit_shape, LOW),
            shaped(unit_shape, LOW),
            shaped((steps, 1, parts * block), WIDE),
            shaped((rows, PAD, strip), WIDE),
            shaped((rows, PAD, strip), LOW),
            low_full,
        ]
        out_specs = [whole(o) for o in outs]
        out_specs[4], out_specs[5], out_specs[6] = unit_spec, unit_spec, unit_sum_spec
        acts = (done[i][1], done[i][5], came_one[i])
        return run_kernel(
            functools.partial(feed_kernel, (parts, rows, width)),
            (token[0], vec, unit_rows, *acts, near_dy, far_dy, feed_all, feed_all),
            outs,
            scratch=[pltpu.VMEM((PAD, model), WIDE), pltpu.VMEM((PAD, model), WIDE)],
            grid=(steps,),
            in_specs=[
                scalars, whole(vec), unit_sum_spec, *[whole(a) for a in acts], strips, strips,
                pl.BlockSpec((parts, rows, block, width), lambda u: (0, 0, u, 0)),
                pl.BlockSpec((parts, rows, block, width), lambda u: (0, 0, u + steps, 0)),
            ],
            out_specs=out_specs,
        )

    fed = [feed_one(0)]
    fed, came_one = fence(fed, came_one)
    came_two = [swap(fed[0][9], "col", 1)]
    fed.append(feed_one(1))
    fed, came_two = fence(fed, came_two)

    came_two = [*came_two, swap(fed[1][9], "col", 1)]
    turns = steps // 2
    early = pl.BlockSpec((2, PAD, parts * block), lambda u: (jnp.minimum(u, turns - 1), 0, 0))
    late = pl.BlockSpec((2, PAD, parts * block), lambda u: (jnp.maximum(u - turns, 0), 0, 0))
    feed_grad = run_kernel(
        functools.partial(feed_grad_kernel, (parts, rows, width, 2)),
        (token[0], *[f[5] for f in fed], *[f[4] for f in fed], *[f[1] for f in fed], *[f[2] for f in fed]),
        [shaped((parts, rows, 2 * unit_count, width), LOW)],
        grid=(2 * turns,),
        in_specs=[scalars, early, early, late, late, *[whole(low_full)] * 4],
        out_specs=[pl.BlockSpec((parts, rows, 2 * block, width), lambda u: (0, 0, u, 0))],
    )[0]
    feed_grad, fed, came_two = fence(feed_grad, fed, came_two)
    feed_total = lax.psum_scatter(feed_grad.reshape(-1, width), ("dp", "row"), scatter_dimension=0, tiled=True)

    def fold(blocks):
        held = dict(enumerate(blocks))
        for bit in bits_of("dp")[:-1]:
            held = join(held, "dp", bit)
        return held[0]

    def ordered(blocks, lead):
        if n == parts:
            return blocks
        both = blocks[0].reshape(rows, lead, parts, -1, width).transpose(2, 0, 1, 3, 4)
        both = xor_order(both.reshape(parts, rows, -1, width), 0, "dp")
        return [both[d] for d in range(parts)]

    half_rows = rows // 2

    def sum_high(near_sum, came_part):
        return [add_low(near_sum[half_rows + k], came_part[k]) for k in range(half_rows)]

    def sum_low(near_sum, came_part):
        return [add_low(near_sum[k], came_part[k]) for k in range(half_rows)]

    def from_images(strips):
        came = [strips[0]] + [swap(strips[k], "row", k) for k in range(1, rows)]
        stacked = xor_order(jnp.stack(came)[:, :, :SEQ], 0, "row")
        return stacked.reshape(-1, strip).astype(WIDE)

    def backward_one(i):
        outs = [full, low_full, shaped((PAD, 3 * span), LOW), low_full, shaped((8, model), WIDE), shaped((1, 3 * span), WIDE)]
        acts = (vec, fed[i][0], fed[i][9], came_two[i], fed[i][2], done[i][3])
        return run_kernel(
            functools.partial(second_kernel, (n, rows, heads, width)),
            (token[0], *acts, *head_weights),
            outs,
            scratch=[pltpu.VMEM((rows, 4 * span, width), LOW), pltpu.VMEM((PAD, span), LOW)],
            in_specs=[scalars, *[whole(a) for a in acts], *head_specs],
        )

    top_far = swap(jnp.stack([f[8] for f in fed]), "col", 1)
    returned = [backward_one(0)]
    returned, top_far = fence(returned, top_far)

    came_three = [swap(returned[0][3], "col", 1)]
    top = jnp.stack([f[7] + t.astype(WIDE) for f, t in zip(fed, top_far)], axis=1).astype(LOW)
    result = from_images(top)
    returned.append(backward_one(1))
    returned, came_three, result = fence(returned, came_three, result)

    came_three = [*came_three, swap(returned[1][3], "col", 1)]
    attn_grad = run_kernel(
        functools.partial(attn_grad_kernel, (n, rows, heads, width)),
        (
            token[0], *[r[2] for r in returned], *[d[2] for d in done], *[d[4] for d in done], *[r[1] for r in returned],
        ),
        [shaped((rows, head_count * parts // n, width), LOW) for _ in range(n)],
        scratch=[pltpu.VMEM((span, model), LOW)],
    )
    attn_grad, came_three = fence(attn_grad, came_three)

    attn_blocks = ordered(attn_grad, 4 * heads)
    attn_far, attn_near = fold(attn_blocks[parts // 2 :]), fold(attn_blocks[: parts // 2])
    grad_strips, sums_one = run_kernel(
        functools.partial(last_kernel, (rows, width, images)),
        (
            token[0], vec, *[d[1] for d in done], *[r[3] for r in returned], *came_three, *[r[0] for r in returned],
        ),
        [shaped((rows, images, PAD, strip), LOW), shaped((8, model), WIDE)],
    )
    attn_far, attn_near, grad_strips, sums_one = fence(attn_far, attn_near, grad_strips, sums_one)

    grad_scale = grad_gain / math.sqrt(tokens.shape[0] * parts)

    lanes = max(unit_count, 2 * heads * chunk, 12 * chunk)
    tiny = run_kernel(
        functools.partial(collect_kernel, (rows, heads, chunk, parts, width, images)),
        (
            token[0], sums_one, *[r[4] for r in returned],
            *[f[3] for f in fed], *[r[5] for r in returned], *[f[6] for f in fed],
        ),
        [shaped((parts, 8, lanes), WIDE)],
    )[0]
    attn_high = across(attn_far[half_rows:])
    tiny = functools.reduce(lambda a, b: a + b, [tiny[0]] + [swap(tiny[d], "dp", d) for d in range(1, parts)])
    def adam(reduced, owns, states, ranges):
        first, pieces = reduced
        outs = []
        for size, _ in ranges:
            outs += [shaped((size, width), WIDE), shaped((size, width), WIDE), shaped((2, size, width), WIDE)]
        args = (first, *pieces, *owns, *states)
        return run_kernel(
            functools.partial(adam_kernel, (len(pieces), [r[0] for r in ranges], grad_scale)),
            args,
            outs,
            in_specs=[whole(a) for a in args],
        )

    state_rows = lambda a, order: a.transpose(order).reshape(2, -1, width)
    out_count = out_own.shape[0]
    attn_high, attn_far, attn_near, grad_strips, tiny = fence(attn_high, attn_far, attn_near, grad_strips, tiny)

    attn_low = across(attn_far[:half_rows])
    attn_two, attn_three = sum_high(attn_near, attn_high)
    attn_three = swap(attn_three, "row", 1)
    grad_tokens = from_images(grad_strips)
    tiny = (tiny + swap(tiny, "row", 1)) + (swap(tiny, "row", 2) + swap(tiny, "row", 3))
    attn_low, attn_two, attn_three, attn_near, grad_tokens, tiny = fence(
        attn_low, attn_two, attn_three, attn_near, grad_tokens, tiny
    )

    attn_zero, attn_one = sum_low(attn_near, attn_low)
    attn_one = swap(attn_one, "row", 1)
    attn_two = swap(add_low(attn_two, attn_three), "row", 2)
    attn_zero, attn_one, attn_two = fence(attn_zero, attn_one, attn_two)
    feed_done = adam(
        (feed_total, []),
        [up_own, down_own],
        [state_rows(state_up, (0, 2, 3, 1)), state_rows(state_down, (0, 1, 2, 3))],
        [(unit_count, 0), (unit_count, 0)],
    )

    flat_up = lambda a: jnp.swapaxes(a, -1, -2)
    small_args = (b_qkv, flat_up(b_up), vectors, state_qkv_bias, flat_up(state_up_bias), state_vectors)
    small_kinds = (b_qkv.shape, flat_up(b_up).shape, vectors.shape)
    small_done = run_kernel(
        functools.partial(small_adam_kernel, (heads, groups, chunk, grad_scale)),
        (token[0], tiny, *small_args),
        [shaped(k, WIDE) for k in (*small_kinds, *small_kinds)] + [shaped((2, *k), WIDE) for k in small_kinds],
    )

    attn_done = adam(
        (attn_zero, [attn_one, attn_two]),
        [qkv_own, out_own],
        [state_rows(state_qkv, (0, 2, 3, 4, 1)), state_rows(state_out, (0, 1, 2, 3))],
        [(qkv_count, 0), (out_count, 0)],
    )

    def shape_all(which):
        lead = (2,) if which == 2 else ()
        more = (0,) if which == 2 else ()
        move = lambda order: (*more, *[o + len(lead) for o in order])
        return (
            attn_done[which].reshape(*lead, 3, heads, chunk, width).transpose(move((3, 0, 1, 2))),
            small_done[3 * which],
            attn_done[3 + which].reshape(*lead, *w_out.shape),
            feed_done[which].reshape(*lead, groups, chunk, width).transpose(move((2, 0, 1))),
            flat_up(small_done[3 * which + 1]),
            feed_done[3 + which].reshape(*lead, *w_down.shape),
            small_done[3 * which + 2],
        )

    return (result, grad_tokens, *shape_all(0), *shape_all(1), *shape_all(2))


def solution(mesh):
    placed = (
        P("dp", ("row", "col")),
        P("dp", ("row", "col")),
        P("row", None, "col", "dp"),
        P(None, "col", "dp"),
        P("col", "dp", "row"),
        P("row", "col", "dp"),
        P("col", "dp"),
        P("col", "dp", "row"),
        P(None, ("row", "col"), "dp"),
        P(None, "row", None, "col", "dp"),
        P(None, None, "col", "dp"),
        P(None, "col", "dp", "row"),
        P(None, "row", "col", "dp"),
        P(None, "col", "dp"),
        P(None, "col", "dp", "row"),
        P(None, None, ("row", "col"), "dp"),
    )
    params = placed[2:9]
    return jax.shard_map(
        on_device,
        mesh=mesh,
        in_specs=placed,
        out_specs=(placed[0], placed[0], *params, *params, *placed[9:]),
        check_vma=False,
    )
```

```python
import functools
import math

import jax
import jax.numpy as jnp
from jax import lax
from jax.experimental import pallas as pl
from jax.experimental.pallas import tpu as pltpu
from jax.sharding import PartitionSpec as P

HD = 64
SEQ = 197
PAD = 208
STEP = 10

norm_eps = 1e-06
beta_first = 0.9
beta_second = 0.999
learn_rate = 0.01
weight_decay = 0.05
adam_eps = 1e-08
grad_gain = 32.0

LOW = jnp.bfloat16
WIDE = jnp.float32


def swap(values, name, bit):
    count = lax.axis_size(name)
    return lax.ppermute(values, name, [(i, i ^ bit) for i in range(count)])


def bits_of(name):
    bits, bit = [], 1
    while bit < lax.axis_size(name):
        bits.append(bit)
        bit *= 2
    return bits


def after(value, *others):
    return lax.optimization_barrier((value, *others))[0]


def planes(values):
    blocks = {0: values}
    for bit in reversed(bits_of("dp")[:-1]):
        for place in list(blocks):
            blocks[place ^ bit] = swap(blocks[place], "dp", bit)
    return [blocks[d] for d in range(len(blocks))]


def across(values):
    return swap(values, "dp", lax.axis_size("dp") // 2)


def add_low(left, right):
    return (left.astype(WIDE) + right.astype(WIDE)).astype(left.dtype)


def join(held, name, bit):
    return {d: add_low(held[d], swap(held[d ^ bit], name, bit)) for d in held if not d & bit}


def scatter(blocks, name):
    held = dict(enumerate(blocks))
    for bit in bits_of(name):
        held = join(held, name, bit)
    return held[0]


def xor_order(values, axis, name):
    mine = lax.axis_index(name)
    shape = values.shape
    for bit in bits_of(name):
        split = values.reshape(shape[:axis] + (shape[axis] // (2 * bit), 2, bit) + shape[axis + 1 :])
        flipped = jnp.flip(split, axis + 1)
        values = jnp.where((mine & bit) > 0, flipped, split).reshape(shape)
    return values


def adam_step(weight_old, gradient, first_old, second_old, decay_on):
    first_moment = beta_first * first_old + (1.0 - beta_first) * gradient
    second_moment = beta_second * second_old + (1.0 - beta_second) * gradient * gradient
    first_hat = first_moment / (1.0 - beta_first**STEP)
    second_hat = second_moment / (1.0 - beta_second**STEP)
    change = -learn_rate * (first_hat / (jnp.sqrt(second_hat) + adam_eps) + decay_on * weight_old)
    return change, first_moment, second_moment


def adam_kernel(spec, first, *refs):
    count, sizes, grad_scale = spec
    pieces, refs = refs[:count], refs[count:]
    weights, states, outs = refs[: len(sizes)], refs[len(sizes) : 2 * len(sizes)], refs[2 * len(sizes) :]
    at = 0
    for i, size in enumerate(sizes):
        lines = slice(at, at + size)
        at += size
        total = first[lines].astype(WIDE)
        for piece in pieces:
            total = total + piece[lines].astype(WIDE)
        gradient = total * grad_scale
        change, low_moment, high_moment = adam_step(
            weights[i][...].astype(WIDE), gradient, states[i][0], states[i][1], weight_decay
        )
        outs[3 * i][...] = gradient
        outs[3 * i + 1][...] = change
        outs[3 * i + 2][0] = low_moment
        outs[3 * i + 2][1] = high_moment


def join_kernel(qkv, out, up, down, head_o, feed_o):
    head_o[: qkv.shape[0], :] = qkv[...]
    head_o[qkv.shape[0] :, :] = out[...]
    feed_o[: up.shape[0], :] = up[...]
    feed_o[up.shape[0] :, :] = down[...]


def collect_kernel(spec, pos, ones, *refs):
    rows, heads, chunk, parts, width, images = spec
    twos, dys, packs, refs = refs[:images], refs[images : 2 * images], refs[2 * images : 3 * images], refs[3 * images :]
    units, out, = refs[:-1], refs[-1]
    low_col, me, row = pos[0] == 0, pos[1], pos[2]
    out[...] = jnp.zeros_like(out)
    add = lambda items: functools.reduce(lambda a, b: a + b, items)
    two = add([t[0:3, :] for t in twos])
    lines = [ones[0:1, :], ones[1:2, :], two[0:1], two[1:2], two[2:3], add([d[...] for d in dys])]
    pack = add([p[...] for p in packs])
    span = heads * HD
    half = width // 2
    unit_total = add([u[...] for u in units])
    each = unit_total.shape[2] // parts
    def put(d, line, pieces):
        value = jnp.concatenate(pieces, axis=1)
        short = out.shape[2] - value.shape[1]
        if short:
            value = jnp.concatenate([value, jnp.zeros((1, short), WIDE)], axis=1)
        out[pl.ds(d, 1), pl.ds(line, 1), :] = value[None]

    for owner in range(parts):
        d = me ^ owner
        spots = [part * span + h * HD + owner * chunk for part in (0, 2) for h in range(heads)]
        put(d, 0, [pack[:, at : at + chunk] for at in spots])
        put(d, 1, [unit_total[u][:, owner * each : (owner + 1) * each] for u in range(unit_total.shape[0])])
        for k in range(rows):
            pieces = []
            for v in range(6):
                for j in range(2):
                    at = k * width + j * HD + owner * chunk
                    near, far = lines[v][:, at : at + chunk], lines[v][:, at + half : at + half + chunk]
                    pieces.append(jnp.where(low_col, near, far))
            put(d, 4 + (row ^ k), pieces)


def small_adam_kernel(spec, pos, tiny, *refs):
    heads, groups, chunk, grad_scale = spec
    row = pos[2]
    weights, states, grads, changes, fresh = (refs[3 * i : 3 * i + 3] for i in range(5))
    for part in range(2):
        for h in range(heads):
            at = (part * heads + h) * chunk
            grads[0][part, h : h + 1, :] = tiny[0:1, at : at + chunk] * grad_scale
    side = lax.broadcasted_iota(jnp.int32, (groups, chunk), 0)
    table = jnp.zeros((groups, chunk), WIDE)
    for g in range(groups):
        table = jnp.where(side == g, tiny[1:2, g * chunk : (g + 1) * chunk], table)
    grads[1][...] = table.T * grad_scale
    mine = tiny[pl.ds(4 + row, 1), :] * grad_scale
    for v in range(6):
        for j in range(2):
            at = (v * 2 + j) * chunk
            grads[2][v, j : j + 1, :] = mine[:, at : at + chunk]
    for i in range(3):
        change, low_moment, high_moment = adam_step(weights[i][...].astype(WIDE), grads[i][...], states[i][0], states[i][1], 0.0)
        changes[i][...] = change
        fresh[i][0] = low_moment
        fresh[i][1] = high_moment


def dot_nt(left, right):
    return lax.dot_general(left, right, (((1,), (1,)), ((), ())), preferred_element_type=WIDE)


def dot_nn(left, right):
    return lax.dot_general(left, right, (((1,), (0,)), ((), ())), preferred_element_type=WIDE)


def dot_tn(left, right):
    return lax.dot_general(left, right, (((0,), (0,)), ((), ())), preferred_element_type=WIDE)


def moments_of(stream):
    center = jnp.mean(stream, axis=-1, keepdims=True)
    offset = stream - center
    inv_std = lax.rsqrt(jnp.mean(offset * offset, axis=-1, keepdims=True) + norm_eps)
    return offset * inv_std, inv_std


def norm_backward(grad_norm, scaled, inv_std, gain):
    weighted = grad_norm * gain
    return inv_std * (
        weighted
        - jnp.mean(weighted, axis=-1, keepdims=True)
        - scaled * jnp.mean(weighted * scaled, axis=-1, keepdims=True)
    )


def lay_strips(low_col, near, far, rows):
    pieces = []
    for k in range(rows):
        mine, other = near(k), far(k)
        pieces.append(jnp.where(low_col, mine, other))
        pieces.append(jnp.where(low_col, other, mine))
    return jnp.concatenate(pieces, axis=1)


def soft(scores):
    lane = lax.broadcasted_iota(jnp.int32, scores.shape, 1)
    scores = jnp.where(lane < SEQ, scores * (1.0 / math.sqrt(HD)), -1e30)
    raised = jnp.exp(scores - jnp.max(scores, axis=-1, keepdims=True))
    return raised * (1.0 / jnp.sum(raised, axis=-1, keepdims=True))


class Source:
    def __init__(self, refs, count):
        self.refs, self.count = refs, count

    def block(self, k, first, size):
        at = first + (self.count if k == 2 else 0)
        return self.refs[(k + 1) // 2][at : at + size, :]


def lay_heads(target, sources, me, groups, rows):
    own = HD // len(sources)
    for k in range(rows):
        for d, source in enumerate(sources):
            place = me ^ d if len(sources) > 1 else 0
            for g in range(groups):
                at = g * HD + place * own
                if len(sources) > 1:
                    at = pl.multiple_of(at, own)
                target[k, pl.ds(at, own), :] = source.block(k, g * own, own)


def first_kernel(spec, pos, near, far, *refs):
    n, rows, heads, width = spec
    count = 4 * heads * HD // n
    sources = [Source([refs[d], refs[n + d], refs[2 * n + d]], count) for d in range(n)]
    vec_o, x_o, normed_o, packed_o, att_o, part_o, qkv_s = refs[3 * n :]
    low_col, me = pos[0] == 0, pos[1]
    small = refs[2 * n][count:, :].astype(WIDE)
    for d in range(1, n):
        small = small + refs[2 * n + d][count:, :].astype(WIDE)
    each = small.shape[0] // rows
    vec = jnp.concatenate([small[k * each : k * each + 6] for k in range(rows)], axis=1)
    vec_o[0:6, :] = vec
    lay_heads(qkv_s, sources, me, 4 * heads, rows)
    stream = lay_strips(low_col, lambda k: near[k, 0], lambda k: far[k, 0], rows)
    x_o[...] = stream
    scaled, _ = moments_of(stream.astype(WIDE))
    normed = (scaled * vec[0:1] + vec[1:2]).astype(LOW)
    normed_o[...] = normed
    span = heads * HD
    lines = span // width
    for part in range(3):
        total = dot_nt(normed[:, :width], qkv_s[0, part * span : (part + 1) * span, :])
        for k in range(1, rows):
            total = total + dot_nt(normed[:, k * width : (k + 1) * width], qkv_s[k, part * span : (part + 1) * span, :])
        if part != 1:
            line = 6 + (lines if part == 2 else 0)
            total = total + jnp.concatenate([small[line + i : line + i + 1] for i in range(lines)], axis=1)
        packed_o[:, part * span : (part + 1) * span] = total.astype(LOW)
    two = 2 * HD
    lane = lax.broadcasted_iota(jnp.int32, (1, two), 1)
    for pair in range(heads // 2):
        at = pair * two
        queries = packed_o[:, at : at + two]
        key_rows = packed_o[:, span + at : span + at + two]
        values = packed_o[:, 2 * span + at : 2 * span + at + two]
        halves = []
        for side in range(2):
            mask = (lane < HD) if side == 0 else (lane >= HD)
            probs = soft(dot_nt(jnp.where(mask, queries, jnp.zeros_like(queries)), key_rows))
            halves.append(dot_nn(probs.astype(LOW), values))
        att_o[:, at : at + two] = jnp.where(lane < HD, halves[0], halves[1]).astype(LOW)
    for k in range(rows):
        part_o[:, k * width : (k + 1) * width] = dot_nn(att_o[...], qkv_s[k, 3 * span :, :]).astype(LOW)


def row_blocks(ref, row, parts, rows):
    return [jnp.concatenate([ref[d, row ^ k] for d in range(parts)], axis=0) for k in range(rows)]


def feed_kernel(spec, pos, vec, small, x, part, came, near, far, up, down, *refs):
    parts, rows, width = spec
    mid, normed, dy, dy_sum_o, units_o, hid_o, unit_sum_o, top_o, far_o, back_o, mixed_s, back_s = refs
    low_col, row = pos[0] == 0, pos[2]
    step = pl.program_id(0)

    @pl.when(step == 0)
    def _():
        dy[...] = lay_strips(low_col, lambda k: near[k, 0], lambda k: far[k, 0], rows)
        dy_sum_o[...] = jnp.sum(dy[...].astype(WIDE), axis=0, keepdims=True)
        middle = x[...].astype(WIDE) + (part[...].astype(WIDE) + came[...].astype(WIDE) + vec[2:3, :])
        mid[...] = middle
        scaled, _ = moments_of(middle)
        normed[...] = (scaled * vec[3:4, :] + vec[4:5, :]).astype(LOW)
        mixed_s[...] = jnp.zeros_like(mixed_s)
        back_s[...] = jnp.zeros_like(back_s)

    up_rows, down_rows = row_blocks(up, row, parts, rows), row_blocks(down, row, parts, rows)
    hidden = dot_nt(normed[:, :width], up_rows[0])
    for k in range(1, rows):
        hidden = hidden + dot_nt(normed[:, k * width : (k + 1) * width], up_rows[k])
    active, slope = gelu_both(hidden + small[0])
    active = active.astype(LOW)
    units_o[0] = active
    grad = dot_nt(dy[:, :width], down_rows[0])
    for k in range(1, rows):
        grad = grad + dot_nt(dy[:, k * width : (k + 1) * width], down_rows[k])
    grad = (grad * slope).astype(LOW)
    hid_o[0] = grad
    unit_sum_o[0] = jnp.sum(grad.astype(WIDE), axis=0, keepdims=True)
    for k in range(rows):
        at = slice(k * width, (k + 1) * width)
        mixed_s[:, at] += dot_nn(active, down_rows[k])
        back_s[:, at] += dot_nn(grad, up_rows[k])

    @pl.when(step == pl.num_programs(0) - 1)
    def _():
        back_o[...] = back_s[...].astype(LOW)
        half = width // 2
        for k in range(rows):
            left, right = slice(k * width, k * width + half), slice(k * width + half, (k + 1) * width)
            base = mid[...] + vec[5:6, :]
            top_l, top_r = mixed_s[:, left] + base[:, left], mixed_s[:, right] + base[:, right]
            top_o[k] = jnp.where(low_col, top_l, top_r)
            far_o[k] = jnp.where(low_col, mixed_s[:, right], mixed_s[:, left]).astype(LOW)


def feed_grad_kernel(spec, pos, *refs):
    parts, rows, width, groups = spec
    hids, units, normeds, dys, out = refs[0:2], refs[2:4], refs[4:6], refs[6:8], refs[8]
    row = pos[2]

    def write(left, right):
        wide = [jnp.concatenate([ref[g] for g in range(groups)], axis=1) for ref in left]
        total = dot_tn(jnp.concatenate(wide, axis=0), jnp.concatenate([ref[...] for ref in right], axis=0))
        block = total.shape[0] // (groups * parts)
        for g in range(groups):
            for d in range(parts):
                at = (g * parts + d) * block
                for k in range(rows):
                    value = total[at : at + block, k * width : (k + 1) * width]
                    out[d, row ^ k, g * block : (g + 1) * block, :] = value.astype(LOW)

    half = pl.num_programs(0) // 2

    @pl.when(pl.program_id(0) < half)
    def _():
        write(hids, normeds)

    @pl.when(pl.program_id(0) >= half)
    def _():
        write(units, dys)


def second_kernel(spec, pos, vec, mid, back, came, dy, packed, *refs):
    n, rows, heads, width = spec
    count = 4 * heads * HD // n
    sources = [Source([refs[d], refs[n + d], refs[2 * n + d]], count) for d in range(n)]
    dmid_o, dz_o, dpacked_o, back_o, sums_o, psum_o, qkv_s, datt_s = refs[3 * n :]
    me = pos[1]
    lay_heads(qkv_s, sources, me, 4 * heads, rows)
    span = heads * HD
    grad_norm = back[...].astype(WIDE) + came[...].astype(WIDE)
    scaled, inv_std = moments_of(mid[...])
    dmid = dy[...].astype(WIDE) + norm_backward(grad_norm, scaled, inv_std, vec[3:4, :])
    dmid_o[...] = dmid
    dz = dmid.astype(LOW)
    dz_o[...] = dz
    sums_o[0:1, :] = jnp.sum(dz.astype(WIDE), axis=0, keepdims=True)
    sums_o[1:2, :] = jnp.sum(grad_norm * scaled, axis=0, keepdims=True)
    sums_o[2:3, :] = jnp.sum(grad_norm, axis=0, keepdims=True)
    total = dot_nt(dz[:, :width], qkv_s[0, 3 * span :, :])
    for k in range(1, rows):
        total = total + dot_nt(dz[:, k * width : (k + 1) * width], qkv_s[k, 3 * span :, :])
    datt_s[...] = total.astype(LOW)
    two = 2 * HD
    scale = 1.0 / math.sqrt(HD)
    lane = lax.broadcasted_iota(jnp.int32, (1, two), 1)
    for pair in range(heads // 2):
        at = pair * two
        queries = packed[:, at : at + two]
        key_rows = packed[:, span + at : span + at + two]
        values = packed[:, 2 * span + at : 2 * span + at + two]
        grads = datt_s[:, at : at + two]
        dqs, dks, dvs = [], [], []
        for side in range(2):
            mask = (lane < HD) if side == 0 else (lane >= HD)
            probs = soft(dot_nt(jnp.where(mask, queries, jnp.zeros_like(queries)), key_rows))
            dprobs = dot_nt(jnp.where(mask, grads, jnp.zeros_like(grads)), values)
            dscores = probs * (dprobs - jnp.sum(dprobs * probs, axis=-1, keepdims=True))
            dscores = dscores.astype(LOW)
            dqs.append(dot_nn(dscores, key_rows))
            dks.append(dot_tn(dscores, queries))
            dvs.append(dot_tn(probs.astype(LOW), grads))
        first = lane < HD
        dpacked_o[:, at : at + two] = (jnp.where(first, dqs[0], dqs[1]) * scale).astype(LOW)
        dpacked_o[:, span + at : span + at + two] = (jnp.where(first, dks[0], dks[1]) * scale).astype(LOW)
        dpacked_o[:, 2 * span + at : 2 * span + at + two] = jnp.where(first, dvs[0], dvs[1]).astype(LOW)
    psum_o[...] = jnp.sum(dpacked_o[...].astype(WIDE), axis=0, keepdims=True)
    for k in range(rows):
        back_o[:, k * width : (k + 1) * width] = dot_nn(dpacked_o[...], qkv_s[k, : 3 * span, :]).astype(LOW)


def attn_grad_kernel(spec, pos, *refs):
    n, rows, heads, width = spec
    dpacked, normed, att, dz = refs[0:2], refs[2:4], refs[4:6], refs[6:8]
    outs, total_s = refs[8 : 8 + n], refs[8 + n]
    me = pos[1]
    span = heads * HD
    own = HD // n
    for part in range(4):
        if part < 3:
            at = slice(part * span, (part + 1) * span)
            total = dot_tn(dpacked[0][:, at], normed[0][...]) + dot_tn(dpacked[1][:, at], normed[1][...])
        else:
            total = dot_tn(att[0][...], dz[0][...]) + dot_tn(att[1][...], dz[1][...])
        total_s[...] = total.astype(LOW)
        for d in range(n):
            place = me ^ d if n > 1 else 0
            for g in range(heads):
                line = g * HD + place * own
                if n > 1:
                    line = pl.multiple_of(line, own)
                value = total_s[pl.ds(line, own), :]
                to = (part * heads + g) * own
                for k in range(rows):
                    outs[d][k, to : to + own, :] = value[:, k * width : (k + 1) * width]


def gelu_both(values):
    tail = 0.5 * (1.0 + lax.erf(values * (1.0 / math.sqrt(2.0))))
    bell = jnp.exp(values * values * -0.5) * (1.0 / math.sqrt(2.0 * math.pi))
    return values * tail, tail + values * bell


def last_kernel(spec, pos, vec, *refs):
    rows, width, images = spec
    x, back, came, dmid = (refs[i * images : (i + 1) * images] for i in range(4))
    out_o, sums_o = refs[4 * images :]
    low_col = pos[0] == 0
    half = width // 2
    for i in range(images):
        scaled, inv_std = moments_of(x[i][...].astype(WIDE))
        grad_norm = back[i][...].astype(WIDE) + came[i][...].astype(WIDE)
        value = dmid[i][...] + norm_backward(grad_norm, scaled, inv_std, vec[0:1, :])
        gain_sum = jnp.sum(grad_norm * scaled, axis=0, keepdims=True)
        shift_sum = jnp.sum(grad_norm, axis=0, keepdims=True)
        if i == 0:
            sums_o[0:1, :] = gain_sum
            sums_o[1:2, :] = shift_sum
        else:
            sums_o[0:1, :] += gain_sum
            sums_o[1:2, :] += shift_sum
        for k in range(rows):
            left, right = value[:, k * width : k * width + half], value[:, k * width + half : (k + 1) * width]
            out_o[k, i] = jnp.where(low_col, left, right).astype(LOW)


ROOM = 60 * 1024 * 1024


def whole(array):
    zeros = (0,) * len(array.shape)
    return pl.BlockSpec(tuple(array.shape), lambda *_: zeros)


def run_kernel(body, args, outs, scratch=(), grid=None, in_specs=None, out_specs=None):
    if in_specs is None:
        in_specs = [pl.BlockSpec(memory_space=pltpu.SMEM)] + [whole(a) for a in args[1:]]
    if out_specs is None:
        out_specs = [whole(o) for o in outs]
    return pl.pallas_call(
        body,
        grid=grid or (1,),
        in_specs=in_specs,
        out_specs=out_specs,
        out_shape=outs,
        scratch_shapes=list(scratch),
        compiler_params=pltpu.CompilerParams(vmem_limit_bytes=ROOM),
        cost_estimate=pl.CostEstimate(flops=1024, bytes_accessed=1024, transcendentals=0),
    )(*args)


def shaped(shape, kind):
    return jax.ShapeDtypeStruct(shape, kind)


def on_device(
    tokens, cotangent, w_qkv, b_qkv, w_out, w_up, b_up, w_down, vectors,
    state_qkv, state_qkv_bias, state_out, state_up, state_up_bias, state_down, state_vectors,
):
    parts, rows = lax.axis_size("dp"), lax.axis_size("row")
    col, row_index, me = lax.axis_index("col"), lax.axis_index("row"), lax.axis_index("dp")
    low_col = col == 0
    width = w_qkv.shape[0]
    heads, chunk = w_qkv.shape[2], w_qkv.shape[3]
    groups = w_up.shape[1]
    strip = tokens.shape[1]
    images = tokens.shape[0] // (SEQ * rows)
    model = rows * width
    span = heads * HD
    pos = jnp.stack([col, me, row_index]).astype(jnp.int32)

    qkv_own = w_qkv.transpose(1, 2, 3, 0).reshape(-1, width)
    out_own = w_out.reshape(-1, width)
    up_own = w_up.transpose(1, 2, 0).reshape(-1, width)
    down_own = w_down.reshape(-1, width)
    qkv_count, unit_count = qkv_own.shape[0], up_own.shape[0]
    head_own, feed_own = run_kernel(
        join_kernel,
        (qkv_own, out_own, up_own, down_own),
        [shaped((qkv_count + out_own.shape[0], width), LOW), shaped((2 * unit_count, width), LOW)],
        in_specs=[whole(a) for a in (qkv_own, out_own, up_own, down_own)],
    )
    head_count = head_own.shape[0]

    at_me = (jnp.arange(parts) == me)[:, None]
    vec_own = jnp.where(at_me, vectors[:, :, None, :], 0).reshape(6, -1)
    vec_far = swap(vec_own, "col", 1)
    vec_pair = jnp.stack([jnp.where(low_col, vec_own, vec_far), jnp.where(low_col, vec_far, vec_own)])
    bias_own = jnp.where(at_me, b_qkv[:, :, None, :], 0).reshape(-1, width)
    unit_own = jnp.where(at_me, b_up.reshape(1, -1), 0).reshape(-1, width)
    small_count = 6 + bias_own.shape[0] + unit_own.shape[0]
    small_each = small_count + -small_count % 16

    def to_send(stream, extra):
        blocks = stream.astype(LOW).reshape(rows, images, SEQ, strip)
        blocks = jnp.pad(blocks, ((0, 0), (0, 0), (0, PAD - SEQ), (0, 0)))
        if extra is not None:
            extra = jnp.pad(extra, ((0, 0), (0, 2), (0, 0)))
            blocks = jnp.concatenate([blocks, jnp.broadcast_to(extra, (rows, *extra.shape))], axis=2)
        return [lax.dynamic_index_in_dim(blocks, row_index ^ k, 0, False) for k in range(rows)]

    def send_images(blocks):
        return [blocks[0]] + [swap(block, "row", k) for k, block in enumerate(blocks) if k]

    def near_two(values):
        return [swap(values, "row", 1), swap(values, "row", 2)]

    token = [pos]

    def fence(*values):
        token[0], *values = lax.optimization_barrier((token[0], *values))
        return values

    assert rows == 4 and images == 2 and lax.axis_size("col") == 2
    feed_all = lax.all_gather(feed_own, ("dp", "row"), axis=0).reshape(parts, rows, -1, width)
    head_two = near_two(head_own)
    head_x = across(head_own)
    head_plane = planes(head_own)
    token_blocks, dy_blocks = to_send(tokens, vec_pair), to_send(cotangent, None)
    small_same = jnp.pad(jnp.concatenate([bias_own, unit_own]), ((6, small_each - small_count), (0, 0)))
    head_two, head_x, head_plane, token_blocks = fence(head_two, head_x, head_plane, token_blocks)

    head_three = swap(head_two[1], "row", 1)
    came = send_images(token_blocks)
    head_pair = jnp.concatenate(head_two)
    head_pair_x = across(head_pair)
    head_three, came, head_pair_x, head_pair, head_x = fence(head_three, came, head_pair_x, head_pair, head_x)

    small_rows = jnp.stack([jnp.concatenate([b[0, PAD : PAD + 6], b[1, PAD : PAD + 6]], axis=1) for b in came])
    small_rows = jnp.pad(small_rows, ((0, 0), (0, small_each - 6), (0, 0))) + small_same
    head_third = jnp.concatenate([head_three, small_rows.reshape(-1, width)])
    near = jnp.stack([block[:, :PAD] for block in came])
    far = swap(near, "col", 1)
    head_third_x = across(head_third)
    head_own_planes = [*head_plane, *planes(head_x)]
    head_pair_planes = [*planes(head_pair), *planes(head_pair_x)]
    dy_came = send_images(dy_blocks)
    head_third_x, head_third, head_own_planes, head_pair_planes, far, near, dy_came = fence(
        head_third_x, head_third, head_own_planes, head_pair_planes, far, near, dy_came
    )

    head_third_planes = [*planes(head_third), *planes(head_third_x)]

    split = chunk % 16 == 0
    n = parts if split else 1
    head_weights = [*head_own_planes, *head_pair_planes, *head_third_planes]
    if not split:
        def merge(blocks, lead):
            both = xor_order(jnp.stack(blocks), 0, "dp").reshape(parts, lead, blocks[0].shape[0] // lead, width)
            return both.transpose(1, 0, 2, 3).reshape(-1, width)

        def merge_some(blocks, count, lead, number):
            return [merge([b[k * count : (k + 1) * count] for b in blocks], lead) for k in range(number)]

        small_sum = sum(b[head_count:].astype(WIDE) for b in head_third_planes).astype(LOW)
        head_weights = [
            merge(head_own_planes, 4 * heads),
            jnp.concatenate(merge_some(head_pair_planes, head_count, 4 * heads, 2)),
            jnp.concatenate([*merge_some(head_third_planes, head_count, 4 * heads, 1), small_sum]),
        ]
    head_small = [b[head_count * parts // n :] for b in head_weights[2 * n :]]
    scalars = pl.BlockSpec(memory_space=pltpu.SMEM)
    head_specs = [pl.BlockSpec((head_count * parts // n, width), lambda *_: (0, 0))] * n + [whole(w) for w in head_weights[n:]]
    full, low_full = shaped((PAD, model), WIDE), shaped((PAD, model), LOW)

    def forward_one(i):
        strips = pl.BlockSpec((rows, 1, PAD, strip), lambda *_: (0, i, 0, 0))
        outs = [
            shaped((8, model), WIDE),
            low_full,
            low_full,
            shaped((PAD, 3 * span), LOW),
            shaped((PAD, span), LOW),
            low_full,
        ]
        return run_kernel(
            functools.partial(first_kernel, (n, rows, heads, width)),
            (token[0], near, far, *head_weights),
            outs,
            scratch=[pltpu.VMEM((rows, 4 * span, width), LOW)],
            in_specs=[scalars, strips, strips, *head_specs],
        )

    near_dy = jnp.stack(dy_came)
    far_dy = swap(near_dy, "col", 1)
    done = [forward_one(0)]
    done, far_dy, near_dy = fence(done, far_dy, near_dy)

    came_one = [swap(done[0][5], "col", 1)]
    done.append(forward_one(1))
    vec = done[0][0]
    unit_rows = sum(b[6 + bias_own.shape[0] :][: unit_own.shape[0]].astype(WIDE) for b in head_small)
    steps = 1
    block = unit_count // steps
    unit_rows = unit_rows.reshape(parts, steps, block).transpose(1, 0, 2).reshape(steps, 1, parts * block)
    done, came_one, unit_rows = fence(done, came_one, unit_rows)

    came_one = [*came_one, swap(done[1][5], "col", 1)]

    unit_spec = pl.BlockSpec((1, PAD, parts * block), lambda u: (u, 0, 0))
    unit_sum_spec = pl.BlockSpec((1, 1, parts * block), lambda u: (u, 0, 0))
    unit_shape = (steps, PAD, parts * block)

    def feed_one(i):
        strips = pl.BlockSpec((rows, 1, PAD, strip), lambda *_: (0, i, 0, 0))
        outs = [
            full,
            low_full,
            low_full,
            shaped((1, model), WIDE),
            shaped(unit_shape, LOW),
            shaped(unit_shape, LOW),
            shaped((steps, 1, parts * block), WIDE),
            shaped((rows, PAD, strip), WIDE),
            shaped((rows, PAD, strip), LOW),
            low_full,
        ]
        out_specs = [whole(o) for o in outs]
        out_specs[4], out_specs[5], out_specs[6] = unit_spec, unit_spec, unit_sum_spec
        acts = (done[i][1], done[i][5], came_one[i])
        return run_kernel(
            functools.partial(feed_kernel, (parts, rows, width)),
            (token[0], vec, unit_rows, *acts, near_dy, far_dy, feed_all, feed_all),
            outs,
            scratch=[pltpu.VMEM((PAD, model), WIDE), pltpu.VMEM((PAD, model), WIDE)],
            grid=(steps,),
            in_specs=[
                scalars, whole(vec), unit_sum_spec, *[whole(a) for a in acts], strips, strips,
                pl.BlockSpec((parts, rows, block, width), lambda u: (0, 0, u, 0)),
                pl.BlockSpec((parts, rows, block, width), lambda u: (0, 0, u + steps, 0)),
            ],
            out_specs=out_specs,
        )

    fed = [feed_one(0)]
    fed, came_one = fence(fed, came_one)
    came_two = [swap(fed[0][9], "col", 1)]
    fed.append(feed_one(1))
    fed, came_two = fence(fed, came_two)

    came_two = [*came_two, swap(fed[1][9], "col", 1)]
    turns = 2
    early = pl.BlockSpec((1, PAD, parts * block // 2), lambda u: (0, 0, jnp.minimum(u, 1)))
    late = pl.BlockSpec((1, PAD, parts * block // 2), lambda u: (0, 0, jnp.maximum(u - 2, 0)))
    feed_grad = run_kernel(
        functools.partial(feed_grad_kernel, (parts // 2, rows, width, 1)),
        (token[0], *[f[5] for f in fed], *[f[4] for f in fed], *[f[1] for f in fed], *[f[2] for f in fed]),
        [shaped((parts, rows, 2 * unit_count, width), LOW)],
        grid=(2 * turns,),
        in_specs=[scalars, early, early, late, late, *[whole(low_full)] * 4],
        out_specs=[pl.BlockSpec((parts // 2, rows, block, width), lambda u: (u % 2, 0, u // 2, 0))],
    )[0]
    feed_grad, fed, came_two = fence(feed_grad, fed, came_two)
    feed_total = lax.psum_scatter(feed_grad.reshape(-1, width), ("dp", "row"), scatter_dimension=0, tiled=True)

    def fold(blocks):
        held = dict(enumerate(blocks))
        for bit in bits_of("dp")[:-1]:
            held = join(held, "dp", bit)
        return held[0]

    def ordered(blocks, lead):
        if n == parts:
            return blocks
        both = blocks[0].reshape(rows, lead, parts, -1, width).transpose(2, 0, 1, 3, 4)
        both = xor_order(both.reshape(parts, rows, -1, width), 0, "dp")
        return [both[d] for d in range(parts)]

    half_rows = rows // 2

    def sum_high(near_sum, came_part):
        return [add_low(near_sum[half_rows + k], came_part[k]) for k in range(half_rows)]

    def sum_low(near_sum, came_part):
        return [add_low(near_sum[k], came_part[k]) for k in range(half_rows)]

    def from_images(strips):
        came = [strips[0]] + [swap(strips[k], "row", k) for k in range(1, rows)]
        stacked = xor_order(jnp.stack(came)[:, :, :SEQ], 0, "row")
        return stacked.reshape(-1, strip).astype(WIDE)

    def backward_one(i):
        outs = [full, low_full, shaped((PAD, 3 * span), LOW), low_full, shaped((8, model), WIDE), shaped((1, 3 * span), WIDE)]
        acts = (vec, fed[i][0], fed[i][9], came_two[i], fed[i][2], done[i][3])
        return run_kernel(
            functools.partial(second_kernel, (n, rows, heads, width)),
            (token[0], *acts, *head_weights),
            outs,
            scratch=[pltpu.VMEM((rows, 4 * span, width), LOW), pltpu.VMEM((PAD, span), LOW)],
            in_specs=[scalars, *[whole(a) for a in acts], *head_specs],
        )

    top_far = swap(jnp.stack([f[8] for f in fed]), "col", 1)
    returned = [backward_one(0)]
    returned, top_far = fence(returned, top_far)

    came_three = [swap(returned[0][3], "col", 1)]
    top = jnp.stack([f[7] + t.astype(WIDE) for f, t in zip(fed, top_far)], axis=1).astype(LOW)
    result = from_images(top)
    returned.append(backward_one(1))
    returned, came_three, result = fence(returned, came_three, result)

    came_three = [*came_three, swap(returned[1][3], "col", 1)]
    attn_grad = run_kernel(
        functools.partial(attn_grad_kernel, (n, rows, heads, width)),
        (
            token[0], *[r[2] for r in returned], *[d[2] for d in done], *[d[4] for d in done], *[r[1] for r in returned],
        ),
        [shaped((rows, head_count * parts // n, width), LOW) for _ in range(n)],
        scratch=[pltpu.VMEM((span, model), LOW)],
    )
    attn_grad, came_three = fence(attn_grad, came_three)

    attn_blocks = ordered(attn_grad, 4 * heads)
    attn_far, attn_near = fold(attn_blocks[parts // 2 :]), fold(attn_blocks[: parts // 2])
    grad_strips, sums_one = run_kernel(
        functools.partial(last_kernel, (rows, width, images)),
        (
            token[0], vec, *[d[1] for d in done], *[r[3] for r in returned], *came_three, *[r[0] for r in returned],
        ),
        [shaped((rows, images, PAD, strip), LOW), shaped((8, model), WIDE)],
    )
    attn_far, attn_near, grad_strips, sums_one = fence(attn_far, attn_near, grad_strips, sums_one)

    grad_scale = grad_gain / math.sqrt(tokens.shape[0] * parts)

    lanes = max(unit_count, 2 * heads * chunk, 12 * chunk)
    tiny = run_kernel(
        functools.partial(collect_kernel, (rows, heads, chunk, parts, width, images)),
        (
            token[0], sums_one, *[r[4] for r in returned],
            *[f[3] for f in fed], *[r[5] for r in returned], *[f[6] for f in fed],
        ),
        [shaped((parts, 8, lanes), WIDE)],
    )[0]
    attn_high = across(attn_far[half_rows:])
    tiny = functools.reduce(lambda a, b: a + b, [tiny[0]] + [swap(tiny[d], "dp", d) for d in range(1, parts)])
    def adam(reduced, owns, states, ranges):
        first, pieces = reduced
        outs = []
        for size, _ in ranges:
            outs += [shaped((size, width), WIDE), shaped((size, width), WIDE), shaped((2, size, width), WIDE)]
        args = (first, *pieces, *owns, *states)
        return run_kernel(
            functools.partial(adam_kernel, (len(pieces), [r[0] for r in ranges], grad_scale)),
            args,
            outs,
            in_specs=[whole(a) for a in args],
        )

    state_rows = lambda a, order: a.transpose(order).reshape(2, -1, width)
    out_count = out_own.shape[0]
    attn_high, attn_far, attn_near, grad_strips, tiny = fence(attn_high, attn_far, attn_near, grad_strips, tiny)

    attn_low = across(attn_far[:half_rows])
    attn_two, attn_three = sum_high(attn_near, attn_high)
    attn_three = swap(attn_three, "row", 1)
    grad_tokens = from_images(grad_strips)
    tiny = (tiny + swap(tiny, "row", 1)) + (swap(tiny, "row", 2) + swap(tiny, "row", 3))
    attn_low, attn_two, attn_three, attn_near, grad_tokens, tiny = fence(
        attn_low, attn_two, attn_three, attn_near, grad_tokens, tiny
    )

    attn_zero, attn_one = sum_low(attn_near, attn_low)
    attn_one = swap(attn_one, "row", 1)
    attn_two = swap(add_low(attn_two, attn_three), "row", 2)
    attn_zero, attn_one, attn_two = fence(attn_zero, attn_one, attn_two)
    feed_done = adam(
        (feed_total, []),
        [up_own, down_own],
        [state_rows(state_up, (0, 2, 3, 1)), state_rows(state_down, (0, 1, 2, 3))],
        [(unit_count, 0), (unit_count, 0)],
    )

    flat_up = lambda a: jnp.swapaxes(a, -1, -2)
    small_args = (b_qkv, flat_up(b_up), vectors, state_qkv_bias, flat_up(state_up_bias), state_vectors)
    small_kinds = (b_qkv.shape, flat_up(b_up).shape, vectors.shape)
    small_done = run_kernel(
        functools.partial(small_adam_kernel, (heads, groups, chunk, grad_scale)),
        (token[0], tiny, *small_args),
        [shaped(k, WIDE) for k in (*small_kinds, *small_kinds)] + [shaped((2, *k), WIDE) for k in small_kinds],
    )

    attn_done = adam(
        (attn_zero, [attn_one, attn_two]),
        [qkv_own, out_own],
        [state_rows(state_qkv, (0, 2, 3, 4, 1)), state_rows(state_out, (0, 1, 2, 3))],
        [(qkv_count, 0), (out_count, 0)],
    )

    def shape_all(which):
        lead = (2,) if which == 2 else ()
        more = (0,) if which == 2 else ()
        move = lambda order: (*more, *[o + len(lead) for o in order])
        return (
            attn_done[which].reshape(*lead, 3, heads, chunk, width).transpose(move((3, 0, 1, 2))),
            small_done[3 * which],
            attn_done[3 + which].reshape(*lead, *w_out.shape),
            feed_done[which].reshape(*lead, groups, chunk, width).transpose(move((2, 0, 1))),
            flat_up(small_done[3 * which + 1]),
            feed_done[3 + which].reshape(*lead, *w_down.shape),
            small_done[3 * which + 2],
        )

    return (result, grad_tokens, *shape_all(0), *shape_all(1), *shape_all(2))


def solution(mesh):
    placed = (
        P("dp", ("row", "col")),
        P("dp", ("row", "col")),
        P("row", None, "col", "dp"),
        P(None, "col", "dp"),
        P("col", "dp", "row"),
        P("row", "col", "dp"),
        P("col", "dp"),
        P("col", "dp", "row"),
        P(None, ("row", "col"), "dp"),
        P(None, "row", None, "col", "dp"),
        P(None, None, "col", "dp"),
        P(None, "col", "dp", "row"),
        P(None, "row", "col", "dp"),
        P(None, "col", "dp"),
        P(None, "col", "dp", "row"),
        P(None, None, ("row", "col"), "dp"),
    )
    params = placed[2:9]
    return jax.shard_map(
        on_device,
        mesh=mesh,
        in_specs=placed,
        out_specs=(placed[0], placed[0], *params, *params, *placed[9:]),
        check_vma=False,
    )
```
